32 devices in a mesh: dp: 2 (over x), ctx: 8 (over z, y), tp: 2 (over core).
Axes of the slice: x: 2, y: 2, z: 4, core: 2. Of those that a mesh axis runs over, the one named last changes fastest.
Arguments:
- hidden_in: bfloat16 [2, 2, 1024, 1024], P(None, 'dp', 'ctx'), may hold values from -6 to 6
- lengths: int32 [2, 2], P(None, 'dp'), may hold values from 256 to 1024, as said below
- positions: int32 [2, 2, 1024], P(None, 'dp', 'ctx'), may hold values from 0 to 3069, as said below
- attn_gain: bfloat16 [1024], P(('dp', 'ctx')), may hold values from 0.099609375 to 1.8984375
- w_query: bfloat16 [1024, 1024], P(('dp', 'ctx'), 'tp'), may hold values from -0.1875 to 0.1875
- w_key: bfloat16 [1024, 512], P(('dp', 'ctx'), 'tp'), may hold values from -0.1875 to 0.1875
- w_value: bfloat16 [1024, 512], P(('dp', 'ctx'), 'tp'), may hold values from -0.1875 to 0.1875
- q_gain: bfloat16 [64], replicated, may hold values from 0.099609375 to 1.8984375
- k_gain: bfloat16 [64], replicated, may hold values from 0.099609375 to 1.8984375
- w_output: bfloat16 [1024, 1024], P('tp', ('dp', 'ctx')), may hold values from -1.5 to 1.5
- ffn_gain: bfloat16 [1024], P(('dp', 'ctx')), may hold values from 0.099609375 to 1.8984375
- w_gate: bfloat16 [1024, 4608], P(('dp', 'ctx'), 'tp'), may hold values from -0.1875 to 0.1875
- w_up: bfloat16 [1024, 4608], P(('dp', 'ctx'), 'tp'), may hold values from -0.1875 to 0.1875
- w_down: bfloat16 [4608, 1024], P('tp', ('dp', 'ctx')), may hold values from -0.09375 to 0.09375
- grad_out: bfloat16 [2, 2, 1024, 1024], P(None, 'dp', 'ctx'), may hold values from -6 to 6
Outputs:
- out_hidden: bfloat16 [2, 2, 1024, 1024], P(None, 'dp', 'ctx')
- grad_hidden: bfloat16 [2, 2, 1024, 1024], P(None, 'dp', 'ctx')
- grad_attn_gain: float32 [1024], P(('dp', 'ctx'))
- grad_w_query: float32 [1024, 1024], P(('dp', 'ctx'), 'tp')
- grad_w_key: float32 [1024, 512], P(('dp', 'ctx'), 'tp')
- grad_w_value: float32 [1024, 512], P(('dp', 'ctx'), 'tp')
- grad_q_gain: float32 [64], replicated
- grad_k_gain: float32 [64], replicated
- grad_w_output: float32 [1024, 1024], P('tp', ('dp', 'ctx'))
- grad_ffn_gain: float32 [1024], P(('dp', 'ctx'))
- grad_w_gate: float32 [1024, 4608], P(('dp', 'ctx'), 'tp')
- grad_w_up: float32 [1024, 4608], P(('dp', 'ctx'), 'tp')
- grad_w_down: float32 [4608, 1024], P('tp', ('dp', 'ctx'))
The draws below stay inside these ranges and needn't reach their ends.
Inputs may be any that keep to these rules, and one draw needn't show every extreme that they name: For every slot index s, at least one micro-batch has lengths[m, s] = 1024. positions[m, s, 0] = 0, and from each token to the next the position rises by 1, 2 or 3.
All inputs are finite; a program needn't handle non-finite values.
Results may differ from the reference program's by a relative error of at most 0.025.
Values may be sent and summed in bfloat16 or wider, within the bound.
No kernel may reach another device: no remote copies, remote signals or barrier semaphores. Data moves between devices by JAX's collectives and lax.ppermute only.
A program may use at most 256 MiB of HBM per device.

```python
import math
import jax
import jax.numpy as jnp
from jax import lax

D = 1024
HEADS = 16
KV_HEADS = 8
HEAD_DIM = 64
FF = 4608
MICRO = 2
SLOTS = 2
LENGTH = 1024


def draw_lengths(key, part):
    key = jax.random.fold_in(key, 11)
    first_key, second_key = jax.random.split(key)
    drawn = jax.random.randint(first_key, (MICRO, SLOTS), LENGTH // 4, LENGTH + 1)
    full_micro = jax.random.randint(second_key, (SLOTS,), 0, MICRO)
    micro_rows = jnp.arange(MICRO, dtype=jnp.int32)[:, None]
    return jnp.where(micro_rows == full_micro[None, :], LENGTH, drawn).astype(jnp.int32)


def draw_positions(key, part):
    key = jax.random.fold_in(key, 12)
    first_key, second_key = jax.random.split(key)
    steps = jax.random.randint(first_key, (MICRO, SLOTS, LENGTH), 1, 4)
    chosen = jax.random.randint(second_key, (), 0, MICRO * SLOTS)
    slot_number = jnp.arange(MICRO * SLOTS, dtype=jnp.int32).reshape(MICRO, SLOTS, 1)
    steps = jnp.where(slot_number == chosen, 3, steps)
    token_number = jnp.arange(LENGTH, dtype=jnp.int32)[None, None, :]
    steps = jnp.where(token_number == 0, 0, steps)
    return jnp.cumsum(steps, -1).astype(jnp.int32)


def shard_levels(own_key, extent, pieces, smallest, top_value):
    factor_of, own = 1.0, jax.random.fold_in(own_key, 6)
    for position, blocks in pieces:
        heights = jnp.exp(jax.random.uniform(jax.random.fold_in(own, position), (blocks,), jnp.float32, smallest / len(pieces), top_value / len(pieces)))
        factor_of = factor_of * jnp.repeat(heights, extent[position] // blocks).reshape([-1 if axis == position else 1 for axis in range(len(extent))])
    return factor_of


def gaussian(key, extent, scale, limit, cuts=(), held_as=jnp.bfloat16):
    level = shard_levels(key, extent, cuts, -0.22, 0.18) if cuts else 1.0
    values = jax.random.normal(key, extent, jnp.float32) * scale * level
    return jnp.minimum(jnp.maximum(values, -limit), limit).astype(held_as)


def setup_inputs(seed: int = 0) -> dict:
    arg_keys = jax.random.split(jax.random.key(seed), 16)
    return {
        "hidden_in": gaussian(arg_keys[0], (MICRO, SLOTS, LENGTH, D), 1.0, 6.0, ((1, 2), (2, 8))),
        "lengths": draw_lengths(jax.random.fold_in(arg_keys[15], 71), 0),
        "positions": draw_positions(jax.random.fold_in(arg_keys[15], 71), 0),
        "attn_gain": jnp.clip(1.0 + 0.18 * jax.random.normal(arg_keys[3], (D,), jnp.float32), 0.099609375, 1.8984375).astype(jnp.bfloat16),
        "w_query": gaussian(arg_keys[4], (D, HEADS * HEAD_DIM), D ** -0.5, 0.1875, ((0, 16), (1, 2))),
        "w_key": gaussian(arg_keys[5], (D, KV_HEADS * HEAD_DIM), D ** -0.5, 0.1875, ((0, 16), (1, 2))),
        "w_value": gaussian(arg_keys[6], (D, KV_HEADS * HEAD_DIM), D ** -0.5, 0.1875, ((0, 16), (1, 2))),
        "q_gain": jnp.clip(1.0 + 0.18 * jax.random.normal(arg_keys[7], (HEAD_DIM,), jnp.float32), 0.099609375, 1.8984375).astype(jnp.bfloat16),
        "k_gain": jnp.clip(1.0 + 0.18 * jax.random.normal(arg_keys[8], (HEAD_DIM,), jnp.float32), 0.099609375, 1.8984375).astype(jnp.bfloat16),
        "w_output": gaussian(arg_keys[9], (HEADS * HEAD_DIM, D), (max(1, HEADS * HEAD_DIM * 16 // LENGTH)) ** -0.5, 1.5, ((0, 2), (1, 16))),
        "ffn_gain": jnp.clip(1.0 + 0.18 * jax.random.normal(arg_keys[10], (D,), jnp.float32), 0.099609375, 1.8984375).astype(jnp.bfloat16),
        "w_gate": gaussian(arg_keys[11], (D, FF), D ** -0.5, 0.1875, ((0, 16), (1, 2))),
        "w_up": gaussian(arg_keys[12], (D, FF), D ** -0.5, 0.1875, ((0, 16), (1, 2))),
        "w_down": gaussian(arg_keys[13], (FF, D), FF ** -0.5, 0.09375, ((0, 2), (1, 16))),
        "grad_out": gaussian(arg_keys[14], (MICRO, SLOTS, LENGTH, D), 1.0, 6.0, ((1, 2), (2, 8))),
    }


EPSILON = 1e-05
ROPE_BASE = 1000000.0
MASKED = -1e+30

@jax.custom_vjp
def low(v):
    return lax.optimization_barrier(v.astype(jnp.bfloat16)).astype(jnp.float32)

@jax.custom_vjp
def low_back(v):
    return v

def low_keep(v):
    return (low(v), None)

def low_pass(kept, grad):
    return (grad,)

def back_keep(v):
    return (v, None)

def back_low(kept, grad):
    return (low(grad),)
low.defvjp(low_keep, low_pass)
low_back.defvjp(back_keep, back_low)

def matmul_high(left_side, right_side):
    return jnp.dot(left_side, right_side, precision=lax.Precision.HIGHEST, preferred_element_type=jnp.float32)

def norm_scale(vector):
    return lax.rsqrt(lax.optimization_barrier(jnp.mean(vector * vector, -1, keepdims=True)) + EPSILON)

def rope_tables(offset_row, width):
    inverse = 1.0 / ROPE_BASE ** (jnp.arange(0, width, 2, dtype=jnp.float32) / width)
    angles = offset_row.astype(jnp.float32)[:, None] * inverse[None, :]
    angles = jnp.concatenate([angles, angles], -1)
    return (jnp.cos(angles)[:, None, :], jnp.sin(angles)[:, None, :])

def half_turn(vector):
    middle_index = vector.shape[-1] // 2
    return jnp.concatenate([-vector[..., middle_index:], vector[..., :middle_index]], -1)

def rotate(vector, cosine_table, sine_table):
    return vector * cosine_table + half_turn(vector) * sine_table

def sequence_forward(params, stream, valid_length, offset_row):
    attn_gain, w_query, w_key, w_value, q_gain, k_gain, w_output, ffn_gain, w_gate, w_up, w_down = params
    length = stream.shape[0]
    group = HEADS // KV_HEADS
    score_scale = HEAD_DIM ** (-0.5)
    normed = low(stream * norm_scale(stream) * attn_gain)
    q_raw = low_back(matmul_high(normed, w_query)).reshape(length, HEADS, HEAD_DIM)
    k_raw = low_back(matmul_high(normed, w_key)).reshape(length, KV_HEADS, HEAD_DIM)
    values = low(low_back(matmul_high(normed, w_value))).reshape(length, KV_HEADS, HEAD_DIM)
    cosine_table, sine_table = rope_tables(offset_row, HEAD_DIM)
    queries = low(rotate(q_raw * norm_scale(q_raw) * q_gain, cosine_table, sine_table))
    keys = low(rotate(k_raw * norm_scale(k_raw) * k_gain, cosine_table, sine_table))
    block_rows = math.gcd(length, 512)
    query_blocks = queries.reshape(length // block_rows, block_rows, KV_HEADS, group, HEAD_DIM)
    block_starts = jnp.arange(length // block_rows, dtype=jnp.int32) * block_rows
    key_index = jnp.arange(length, dtype=jnp.int32)

    def attend(bundle):
        query_block, block_start = bundle
        query_index = block_start + jnp.arange(block_rows, dtype=jnp.int32)
        scores = jnp.einsum('tkgd,jkd->kgtj', query_block, keys, precision=lax.Precision.HIGHEST) * score_scale
        visible = (key_index[None, :] <= query_index[:, None]) & (key_index[None, :] < valid_length)
        scores = low_back(jnp.where(visible, scores, MASKED))
        attn_probs = jax.nn.softmax(scores, axis=-1)
        mixed_block = jnp.einsum('kgtj,jkd->tkgd', low(attn_probs), values, precision=lax.Precision.HIGHEST)
        return low(low_back(mixed_block))
    mixed = lax.map(jax.checkpoint(attend), (query_blocks, block_starts)).reshape(length, HEADS * HEAD_DIM)
    middle = stream + low_back(matmul_high(mixed, w_output))
    ffn_in = low(middle * norm_scale(middle) * ffn_gain)
    gate_pre = low_back(matmul_high(ffn_in, w_gate))
    up_pre = low_back(matmul_high(ffn_in, w_up))
    hidden_act = low(jax.nn.silu(gate_pre) * up_pre)
    return middle + low_back(matmul_high(hidden_act, w_down))

def reference(hidden_in, lengths, positions, attn_gain, w_query, w_key, w_value, q_gain, k_gain, w_output, ffn_gain, w_gate, w_up, w_down, grad_out):
    params = tuple((weight.astype(jnp.float32) for weight in (attn_gain, w_query, w_key, w_value, q_gain, k_gain, w_output, ffn_gain, w_gate, w_up, w_down)))
    streams = hidden_in.astype(jnp.float32).reshape(MICRO * SLOTS, LENGTH, D)
    cotangents = grad_out.astype(jnp.float32).reshape(MICRO * SLOTS, LENGTH, D)
    limits = lengths.reshape(MICRO * SLOTS)
    offsets = positions.reshape(MICRO * SLOTS, LENGTH)

    def one_sequence(totals, bundle):
        stream, cotangent, valid_length, offset_row = bundle

        def forward(weights, source):
            return sequence_forward(weights, source, valid_length, offset_row)
        result, pull_back = jax.vjp(forward, params, stream)
        weight_grads, stream_grad = pull_back(cotangent)
        totals = jax.tree.map(jnp.add, totals, weight_grads)
        return (totals, (result.astype(jnp.bfloat16), stream_grad.astype(jnp.bfloat16)))
    initial = jax.tree.map(jnp.zeros_like, params)
    totals, (results, stream_grads) = lax.scan(one_sequence, initial, (streams, cotangents, limits, offsets))
    grad_attn_gain, grad_w_query, grad_w_key, grad_w_value, grad_q_gain, grad_k_gain, grad_w_output, grad_ffn_gain, grad_w_gate, grad_w_up, grad_w_down = totals
    return (results.reshape(MICRO, SLOTS, LENGTH, D), stream_grads.reshape(MICRO, SLOTS, LENGTH, D), grad_attn_gain, grad_w_query, grad_w_key, grad_w_value, grad_q_gain, grad_k_gain, grad_w_output, grad_ffn_gain, grad_w_gate, grad_w_up, grad_w_down)
```

```python
import jax
import jax.numpy as jnp
from jax import lax
from jax.sharding import Mesh, PartitionSpec as P

HEADS = 16
KV_HEADS = 8
HEAD_DIM = 64
EPSILON = 1e-05
ROPE_BASE = 1000000.0
MASKED = -1e30
BF = jnp.bfloat16
F32 = jnp.float32


def dot(a, b, dims):
    return lax.dot_general(a, b, (dims, ((), ())), preferred_element_type=F32)


def mm(a, b):
    return dot(a, b, ((1,), (0,)))


def mm_nt(a, b):
    return dot(a, b, ((1,), (1,)))


def mm_tn(a, b):
    return dot(a, b, ((0,), (0,)))


def swap(v, axis):
    return lax.ppermute(v, axis, [(0, 1), (1, 0)])


def flip(v, axis, size, d):
    return lax.ppermute(v, axis, [(i, i ^ d) for i in range(size)])


def norm_scale(vector):
    return lax.rsqrt(jnp.mean(vector * vector, -1, keepdims=True) + EPSILON)


def norm_back(vector, factor, gain, upstream):
    weighted = upstream * gain
    return factor * weighted - vector * factor * factor * factor * jnp.mean(
        vector * weighted, -1, keepdims=True
    )


def half_turn(vector):
    middle_index = vector.shape[-1] // 2
    return jnp.concatenate([-vector[..., middle_index:], vector[..., :middle_index]], -1)


def half_turn_back(vector):
    middle_index = vector.shape[-1] // 2
    return jnp.concatenate([vector[..., middle_index:], -vector[..., :middle_index]], -1)


def in_order(parts, index):
    bit = 1
    while bit < len(parts):
        flag = (index & bit) != 0
        parts = [jnp.where(flag, parts[i ^ bit], parts[i]) for i in range(len(parts))]
        bit *= 2
    return parts


def body(
    hidden_in,
    lengths,
    positions,
    attn_gain,
    w_query,
    w_key,
    w_value,
    q_gain,
    k_gain,
    w_output,
    ffn_gain,
    w_gate,
    w_up,
    w_down,
    grad_out,
):
    X, H, B, J, T = (lax.axis_size(a) for a in ("dp", "h", "b", "j", "tp"))
    ix, ih, ib, ij, it = (lax.axis_index(a) for a in ("dp", "h", "b", "j", "tp"))
    rows = hidden_in.shape[2]
    d_model = hidden_in.shape[3]
    shard = w_query.shape[0]
    group = HEADS // KV_HEADS
    qw = group * HEAD_DIM
    fw = w_gate.shape[1] // J
    count = T * J * rows
    score_scale = HEAD_DIM ** (-0.5)

    def gather(pack):
        parts = [lax.dynamic_index_in_dim(pack, ij, 0, keepdims=False)]
        for d in range(1, J):
            piece = lax.dynamic_index_in_dim(pack, ij ^ d, 0, keepdims=False)
            parts.append(flip(piece, "j", J, d))
        own = jnp.concatenate(in_order(parts, ij), 0)
        if B > 1:
            own = lax.all_gather(own, "b", axis=0, tiled=True)
        own = jnp.concatenate(in_order([own, swap(own, "h")], ih), 0)
        return jnp.concatenate(in_order([own, swap(own, "dp")], ix), 0)

    def spread(grad):
        for axis, index in (("dp", ix), ("h", ih)):
            half = grad.reshape(2, grad.shape[0] // 2, grad.shape[1])
            give = lax.dynamic_index_in_dim(half, 1 - index, 0, keepdims=False)
            keep = lax.dynamic_index_in_dim(half, index, 0, keepdims=False)
            grad = (keep.astype(F32) + swap(give, axis).astype(F32)).astype(BF)
        if B > 1:
            grad = lax.psum_scatter(grad, "b", scatter_dimension=0, tiled=True)
        pieces = grad.reshape(J, shard, grad.shape[1])
        parts = [lax.dynamic_index_in_dim(pieces, ij, 0, keepdims=False)]
        for d in range(1, J):
            piece = lax.dynamic_index_in_dim(pieces, ij ^ d, 0, keepdims=False)
            parts.append(flip(piece, "j", J, d))
        return jnp.stack(in_order(parts, ij), 1).astype(F32)

    gains = jnp.stack([attn_gain, ffn_gain])
    parts = [gains] + [flip(gains, "j", J, d) for d in range(1, J)]
    gains = jnp.concatenate(in_order(parts, ij), 1)
    if B > 1:
        gains = lax.all_gather(gains, "b", axis=1, tiled=True)
    gains = jnp.concatenate(in_order([gains, swap(gains, "h")], ih), 1)
    gains = jnp.concatenate(in_order([gains, swap(gains, "dp")], ix), 1)
    gain_attn = gains[0].astype(F32)
    gain_ffn = gains[1].astype(F32)

    w_output_t = w_output.T
    w_down_t = w_down.T
    pack_attn = jnp.concatenate(
        [
            w_query.reshape(shard, J, qw),
            w_key.reshape(shard, J, HEAD_DIM),
            w_value.reshape(shard, J, HEAD_DIM),
            w_output_t.reshape(shard, J, qw),
        ],
        2,
    ).transpose(1, 0, 2)
    wa = gather(pack_attn)
    w_qkv = wa[:, : qw + 2 * HEAD_DIM]
    wo = wa[:, qw + 2 * HEAD_DIM :]
    wg = gather(w_gate.reshape(shard, J, fw).transpose(1, 0, 2))
    wu = gather(w_up.reshape(shard, J, fw).transpose(1, 0, 2))
    wd = gather(w_down_t.reshape(shard, J, fw).transpose(1, 0, 2))

    turn = [(0, 0), (1, 2), (2, 1), (3, 3)]

    def fetch(array):
        mine = lax.dynamic_index_in_dim(array, it, 0, keepdims=False)[0]
        return lax.ppermute(mine, ("h", "tp"), turn)

    def give_back(block):
        mine = lax.ppermute(block, ("h", "tp"), turn)
        other = swap(mine, "tp")
        return jnp.stack(in_order([mine, other], it), 0)[:, None]

    def spread_tokens(block):
        parts = [block] + [flip(block, "j", J, d) for d in range(1, J)]
        half = jnp.concatenate(parts, 0)
        return jnp.concatenate([half, swap(half, "tp")], 0)

    def sum_tokens(partial):
        half = partial.reshape(T, J, rows, d_model)
        mine = half[0].astype(F32) + swap(half[1], "tp").astype(F32)
        low = mine.astype(BF)
        total = mine[0]
        for d in range(1, J):
            total = total + flip(low[d], "j", J, d).astype(F32)
        return total

    stream = fetch(hidden_in).astype(F32)
    cot_own = fetch(grad_out)
    pos_own = fetch(positions)[None]
    pos_all = spread_tokens(pos_own).reshape(count)
    valid_length = lax.dynamic_index_in_dim(lengths[:, 0], ih, 0, keepdims=False)

    place = jnp.arange(T * J, dtype=jnp.int32)
    block_of = (it ^ (place // J)) * (B * J) + (ij ^ (place % J))
    row_of = jnp.arange(rows, dtype=jnp.int32)
    query_index = ((block_of + ib * J)[:, None] * rows + row_of[None, :]).reshape(count)
    key_index = (
        (block_of[None, :] + jnp.arange(B, dtype=jnp.int32)[:, None] * J)[..., None] * rows + row_of
    ).reshape(B * count)

    inverse = 1.0 / ROPE_BASE ** (jnp.arange(0, HEAD_DIM, 2, dtype=F32) / HEAD_DIM)
    angles = pos_all.astype(F32)[:, None] * inverse[None, :]
    cosine = jnp.cos(angles)
    sine = jnp.sin(angles)
    cosine = jnp.concatenate([cosine, cosine], -1)[:, None, :]
    sine = jnp.concatenate([sine, sine], -1)[:, None, :]

    attn_factor = norm_scale(stream)
    normed_own = (stream * attn_factor * gain_attn).astype(BF)
    normed = spread_tokens(normed_own)
    raw = mm(normed, w_qkv)
    qk_raw = raw[:, : qw + HEAD_DIM].reshape(count, group + 1, HEAD_DIM)
    qk_gain = jnp.stack([q_gain] * group + [k_gain]).astype(F32)
    qk_factor = norm_scale(qk_raw)
    qk_normed = qk_raw * qk_factor * qk_gain
    qk = (qk_normed * cosine + half_turn(qk_normed) * sine).astype(BF)
    queries = qk[:, :group].transpose(1, 0, 2)
    keys = qk[:, group]
    values = raw[:, qw + HEAD_DIM :].astype(BF)
    if B > 1:
        keys = lax.all_gather(keys, "b", axis=0, tiled=True)
        values = lax.all_gather(values, "b", axis=0, tiled=True)
    visible = (key_index[None, :] <= query_index[:, None]) & (key_index[None, :] < valid_length)

    def scores_of(query_head):
        return jnp.where(visible, mm_nt(query_head, keys) * score_scale, MASKED)

    def attend(query_head):
        scores = scores_of(query_head)
        row_max = jnp.max(scores, -1, keepdims=True)
        exp_scores = jnp.exp(scores - row_max)
        row_total = jnp.sum(exp_scores, -1, keepdims=True)
        probs = (exp_scores / row_total).astype(BF)
        return mm(probs, values).astype(BF), row_max + jnp.log(row_total)

    heads = [attend(queries[g]) for g in range(group)]
    mixed = jnp.concatenate([h[0] for h in heads], -1)
    attn_branch = sum_tokens(mm_nt(mixed, wo).astype(BF))

    middle = stream + attn_branch
    ffn_factor = norm_scale(middle)
    ffn_in = spread_tokens((middle * ffn_factor * gain_ffn).astype(BF))
    cot = spread_tokens(cot_own)
    gate_pre = mm(ffn_in, wg)
    up_pre = mm(ffn_in, wu)
    sigmoid_gate = jax.nn.sigmoid(gate_pre)
    activated = gate_pre * sigmoid_gate
    hidden_act = (activated * up_pre).astype(BF)
    grad_hidden_act = mm(cot, wd)
    grad_gate = (
        grad_hidden_act * up_pre * sigmoid_gate * (1.0 + gate_pre * (1.0 - sigmoid_gate))
    ).astype(BF)
    grad_up = (grad_hidden_act * activated).astype(BF)
    grad_ffn_in = sum_tokens((mm_nt(grad_gate, wg) + mm_nt(grad_up, wu)).astype(BF))
    ffn_branch = sum_tokens(mm_nt(hidden_act, wd).astype(BF))
    out_hidden = give_back((middle + ffn_branch).astype(BF))
    shard_down = spread(mm_tn(cot, hidden_act).astype(BF))
    shard_gate = spread(mm_tn(ffn_in, grad_gate).astype(BF))
    shard_up = spread(mm_tn(ffn_in, grad_up).astype(BF))

    grad_middle = cot_own.astype(F32) + norm_back(middle, ffn_factor, gain_ffn, grad_ffn_in)
    grad_attn = spread_tokens(grad_middle.astype(BF))
    grad_mixed = mm(grad_attn, wo).astype(BF)
    grad_wo = mm_tn(grad_attn, mixed).astype(BF)

    grad_keys = jnp.zeros((B * count, HEAD_DIM), F32)
    grad_values = jnp.zeros((B * count, HEAD_DIM), F32)
    grad_queries = []
    for g in range(group):
        probs = jnp.exp(scores_of(queries[g]) - heads[g][1])
        grad_head = grad_mixed[:, g * HEAD_DIM : (g + 1) * HEAD_DIM]
        grad_probs = mm_nt(grad_head, values)
        row_delta = jnp.sum(grad_probs * probs, -1, keepdims=True)
        grad_scores = (probs * (grad_probs - row_delta)).astype(BF)
        grad_queries.append(mm(grad_scores, keys) * score_scale)
        grad_keys = grad_keys + mm_tn(grad_scores, queries[g]) * score_scale
        grad_values = grad_values + mm_tn(probs.astype(BF), grad_head)
    if B > 1:
        grad_keys = lax.psum_scatter(grad_keys, "b", scatter_dimension=0, tiled=True)
        grad_values = lax.psum_scatter(grad_values, "b", scatter_dimension=0, tiled=True)
    grad_rot = jnp.stack(grad_queries + [grad_keys], 1)
    grad_normed = grad_rot * cosine + half_turn_back(grad_rot * sine)
    grad_qk_raw = norm_back(qk_raw, qk_factor, qk_gain, grad_normed)
    terms = jnp.sum(grad_normed * qk_raw * qk_factor, 0)
    totals = jnp.stack([jnp.sum(terms[:group], 0), terms[group]])
    grad_raw = jnp.concatenate(
        [grad_qk_raw.reshape(count, qw + HEAD_DIM), grad_values], 1
    ).astype(BF)
    grad_wqkv = mm_tn(normed, grad_raw).astype(BF)
    shard_attn = spread(jnp.concatenate([grad_wqkv, grad_wo], 1))
    grad_normed_own = sum_tokens(mm_nt(grad_raw, w_qkv).astype(BF))
    grad_stream = grad_middle + norm_back(stream, attn_factor, gain_attn, grad_normed_own)
    grad_hidden = give_back(grad_stream.astype(BF))

    for axis in ("tp", "dp", "h"):
        totals = totals + swap(totals, axis)
    bit = 1
    while bit < J:
        totals = totals + flip(totals, "j", J, bit)
        bit *= 2
    if B > 1:
        totals = lax.psum(totals, "b")

    shard_query = shard_attn[:, :, :qw].reshape(shard, J * qw)
    shard_key = shard_attn[:, :, qw : qw + HEAD_DIM].reshape(shard, J * HEAD_DIM)
    shard_value = shard_attn[:, :, qw + HEAD_DIM : qw + 2 * HEAD_DIM].reshape(shard, J * HEAD_DIM)
    shard_output = shard_attn[:, :, qw + 2 * HEAD_DIM :].reshape(shard, J * qw)
    shard_gate = shard_gate.reshape(shard, J * fw)
    shard_up = shard_up.reshape(shard, J * fw)
    shard_down = shard_down.reshape(shard, J * fw)

    sum_attn = (
        jnp.sum(shard_query * w_query.astype(F32), 1)
        + jnp.sum(shard_key * w_key.astype(F32), 1)
        + jnp.sum(shard_value * w_value.astype(F32), 1)
    )
    sum_ffn = jnp.sum(shard_gate * w_gate.astype(F32), 1) + jnp.sum(
        shard_up * w_up.astype(F32), 1
    )
    sums = jnp.stack([sum_attn, sum_ffn])
    sums = (sums + swap(sums, "tp")) / jnp.stack([attn_gain, ffn_gain]).astype(F32)

    return (
        out_hidden,
        grad_hidden,
        sums[0],
        shard_query,
        shard_key,
        shard_value,
        totals[0],
        totals[1],
        shard_output.T,
        sums[1],
        shard_gate,
        shard_up,
        shard_down.T,
    )


def solution(mesh):
    places = KV_HEADS // mesh.shape["tp"]

    def run(*args):
        micro = args[0].shape[0]
        shape = (mesh.shape["dp"], micro, mesh.shape["ctx"] // (micro * places), places)
        fine = Mesh(
            mesh.devices.reshape(*shape, mesh.shape["tp"]), ("dp", "h", "b", "j", "tp")
        )
        ctx = ("h", "b", "j")
        rows = ("dp", "h", "b", "j")
        tokens = P(None, "dp", ctx, None)
        return jax.shard_map(
            body,
            mesh=fine,
            in_specs=(
                tokens,
                P(None, "dp"),
                P(None, "dp", ctx),
                P(rows),
                P(rows, "tp"),
                P(rows, "tp"),
                P(rows, "tp"),
                P(),
                P(),
                P("tp", rows),
                P(rows),
                P(rows, "tp"),
                P(rows, "tp"),
                P("tp", rows),
                tokens,
            ),
            out_specs=(
                tokens,
                tokens,
                P(rows),
                P(rows, "tp"),
                P(rows, "tp"),
                P(rows, "tp"),
                P(),
                P(),
                P("tp", rows),
                P(rows),
                P(rows, "tp"),
                P(rows, "tp"),
                P("tp", rows),
            ),
            check_vma=False,
        )(*args)

    return run
```

```python
import functools

import jax
import jax.numpy as jnp
from jax import lax
from jax.experimental import pallas as pl
from jax.experimental.pallas import tpu as pltpu
from jax.sharding import Mesh, PartitionSpec as P

HEADS = 16
KV_HEADS = 8
HEAD_DIM = 64
EPSILON = 1e-05
ROPE_BASE = 1000000.0
MASKED = -1e30
BF = jnp.bfloat16
F32 = jnp.float32
VMEM_BYTES = 60 * 2**20
LANES = 128
SMALL_COST = pl.CostEstimate(flops=1, bytes_accessed=1, transcendentals=0)


def dot(a, b, dims):
    return lax.dot_general(a, b, (dims, ((), ())), preferred_element_type=F32)


def mm(a, b):
    return dot(a, b, ((1,), (0,)))


def mm_nt(a, b):
    return dot(a, b, ((1,), (1,)))


def mm_tn(a, b):
    return dot(a, b, ((0,), (0,)))


def nothing(*refs):
    pass


def after(value, *others):
    anywhere = pl.BlockSpec(memory_space=pl.ANY)
    return pl.pallas_call(
        nothing,
        in_specs=[anywhere] * (1 + len(others)),
        out_specs=anywhere,
        out_shape=jax.ShapeDtypeStruct(value.shape, value.dtype),
        input_output_aliases={0: 0},
        cost_estimate=SMALL_COST,
        name="after",
    )(value, *others)


def swap(v, axis):
    return lax.ppermute(v, axis, [(0, 1), (1, 0)])


def add(a, b):
    return (a.astype(F32) + b.astype(F32)).astype(BF)


def norm_scale(vector):
    return lax.rsqrt(jnp.mean(vector * vector, -1, keepdims=True) + EPSILON)


def norm_back(vector, factor, gain, upstream):
    weighted = upstream * gain
    return factor * weighted - vector * factor * factor * factor * jnp.mean(
        vector * weighted, -1, keepdims=True
    )


def half_turn(vector):
    middle_index = vector.shape[-1] // 2
    return jnp.concatenate([-vector[..., middle_index:], vector[..., :middle_index]], -1)


def half_turn_back(vector):
    middle_index = vector.shape[-1] // 2
    return jnp.concatenate([vector[..., middle_index:], -vector[..., :middle_index]], -1)


def in_order(parts, index):
    bit = 1
    while bit < len(parts):
        flag = (index & bit) != 0
        parts = [jnp.where(flag, parts[i ^ bit], parts[i]) for i in range(len(parts))]
        bit *= 2
    return parts


def row_sums(square, low):
    left = jnp.sum(jnp.where(low, square, 0.0), -1, keepdims=True)
    right = jnp.sum(jnp.where(low, 0.0, square), -1, keepdims=True)
    return jnp.where(low, left, right)


def pair_scale(pair, low):
    return lax.rsqrt(row_sums(pair * pair, low) * (1.0 / HEAD_DIM) + EPSILON)


def lanes(shape):
    return lax.broadcasted_iota(jnp.int32, shape, 1)


def turned(pair, first):
    width = pair.shape[1]
    quarter = HEAD_DIM // 2
    return jnp.where(first, pltpu.roll(pair, width - quarter, 1), pltpu.roll(pair, quarter, 1))


def qkv_kernel(half_tiles, h0_ref, h1_ref, gain_ref, w_ref, qk_gain_ref, cos_ref, sin_ref,
               xa0_ref, xa1_ref, raw_ref, qkv_ref):
    def run(h_ref, xa_ref):
        hidden = h_ref[...].astype(F32)
        factor = lax.rsqrt(jnp.mean(hidden * hidden, -1, keepdims=True) + EPSILON)
        xa = (hidden * factor * gain_ref[...]).astype(BF)
        xa_ref[...] = xa
        raw = mm(xa, w_ref[:, :256])
        raw_ref[...] = raw
        lane = lanes((raw.shape[0], 128))
        low = lane < HEAD_DIM
        first = lane % HEAD_DIM < HEAD_DIM // 2
        cosine, sine = cos_ref[...], sin_ref[...]
        sine = jnp.where(first, -sine, sine)
        for p in range(2):
            pair = raw[:, 128 * p : 128 * (p + 1)]
            normed = pair * pair_scale(pair, low) * qk_gain_ref[p : p + 1, :]
            turned_pair = normed * cosine + turned(normed, first) * sine
            if p == 1:
                turned_pair = jnp.where(low, turned_pair, pair)
            qkv_ref[:, 128 * p : 128 * (p + 1)] = turned_pair.astype(BF)

    @pl.when(pl.program_id(0) < half_tiles)
    def _():
        run(h0_ref, xa0_ref)

    @pl.when(pl.program_id(0) >= half_tiles)
    def _():
        run(h1_ref, xa1_ref)


def qkv_call(h0, h1, gain, w, qk_gain, cosine, sine):
    half, d_model = h0.shape
    tile = min(256, half)
    n = half // tile
    own = pl.BlockSpec((tile, d_model), lambda i: (jnp.minimum(i, n - 1), 0))
    other = pl.BlockSpec((tile, d_model), lambda i: (jnp.maximum(i - n, 0), 0))
    def fixed(a):
        return pl.BlockSpec(a.shape, lambda i: (0, 0))
    def rows(width):
        return pl.BlockSpec((tile, width), lambda i: (i, 0))
    return pl.pallas_call(
        functools.partial(qkv_kernel, n),
        grid=(2 * n,),
        in_specs=[own, other, fixed(gain), fixed(w), fixed(qk_gain), rows(128), rows(128)],
        out_specs=[own, other, rows(256), rows(256)],
        out_shape=[
            jax.ShapeDtypeStruct(h0.shape, BF),
            jax.ShapeDtypeStruct(h0.shape, BF),
            jax.ShapeDtypeStruct((2 * half, 256), F32),
            jax.ShapeDtypeStruct((2 * half, 256), BF),
        ],
        compiler_params=pltpu.CompilerParams(vmem_limit_bytes=VMEM_BYTES),
        cost_estimate=SMALL_COST,
        name="qkv",
    )(h0, h1, gain, w, qk_gain, cosine, sine)


def blocks_of(tiles):
    return [(a, k) for a in range(tiles) for k in range(a + 1)]


def stacked(pair):
    return jnp.concatenate([pair[:, :HEAD_DIM], pair[:, HEAD_DIM:]], 0)


def attend_kernel(tile, tiles, at_ref, qkv_ref, mixed_ref, probs_ref):
    half = tiles // 2
    def place(t):
        return pl.multiple_of((t + half * at_ref[1]) % tiles * tile, tile)
    for a in range(tiles):
        query = stacked(qkv_ref[pl.ds(place(a), tile), :128])
        row = lax.broadcasted_iota(jnp.int32, (2 * tile, 1), 0) % tile + a * tile
        limit = jnp.minimum(row + 1, at_ref[0])
        scores = []
        for k in range(a + 1):
            key = qkv_ref[pl.ds(place(k), tile), 128 : 128 + HEAD_DIM]
            column = lax.broadcasted_iota(jnp.int32, (1, tile), 1) + k * tile
            scores.append(
                jnp.where(column < limit, mm_nt(query, key) * HEAD_DIM ** (-0.5), MASKED)
            )
        peak = functools.reduce(jnp.maximum, [jnp.max(s, -1, keepdims=True) for s in scores])
        exps = [jnp.exp(s - peak) for s in scores]
        total = functools.reduce(jnp.add, [jnp.sum(e, -1, keepdims=True) for e in exps])
        inverse = 1.0 / total
        mixed = 0.0
        for k in range(a + 1):
            probs = (exps[k] * inverse).astype(BF)
            probs_ref[blocks_of(tiles).index((a, k))] = probs
            value = qkv_ref[pl.ds(place(k), tile), 128 + HEAD_DIM :]
            mixed = mixed + mm(probs, value)
        mixed_ref[pl.ds(place(a), tile), :] = jnp.concatenate(
            [mixed[:tile], mixed[tile:]], 1
        ).astype(BF)


def attend_call(at, qkv):
    count = qkv.shape[0]
    tile = min(256, count // 2)
    tiles = count // tile
    pairs = len(blocks_of(tiles))
    return pl.pallas_call(
        functools.partial(attend_kernel, tile, tiles),
        in_specs=[pl.BlockSpec(memory_space=pltpu.SMEM), pl.BlockSpec(memory_space=pltpu.VMEM)],
        out_specs=[pl.BlockSpec(memory_space=pltpu.VMEM)] * 2,
        out_shape=[
            jax.ShapeDtypeStruct((count, 128), BF),
            jax.ShapeDtypeStruct((pairs, 2 * tile, tile), BF),
        ],
        compiler_params=pltpu.CompilerParams(vmem_limit_bytes=VMEM_BYTES),
        cost_estimate=SMALL_COST,
        name="attend",
    )(at, qkv)


def attend_back_kernel(tile, tiles, at_ref, qkv_ref, mixed_ref, probs_ref, raw_ref, g0_ref, g1_ref,
                       wo_ref, qk_gain_ref, cos_ref, sin_ref, out_ref, total_ref, dm_ref, dkv_ref):
    half = tiles // 2
    def place(t):
        return pl.multiple_of((t + half * at_ref[1]) % tiles * tile, tile)
    rows = half * tile
    dm_ref[:rows] = mm(g0_ref[...], wo_ref[...]).astype(BF)
    dm_ref[rows:] = mm(g1_ref[...], wo_ref[...]).astype(BF)
    scale = HEAD_DIM ** (-0.5)
    lane = lanes((tile, 128))
    low = lane < HEAD_DIM
    first = lane % HEAD_DIM < HEAD_DIM // 2

    def finish(t, p, grad):
        at = pl.ds(place(t), tile)
        cosine, sine = cos_ref[at], sin_ref[at]
        pair = raw_ref[at, 128 * p : 128 * (p + 1)]
        factor = pair_scale(pair, low)
        signed = grad * jnp.where(first, -sine, sine)
        upstream = grad * cosine + turned(signed, first)
        gain = qk_gain_ref[p : p + 1, :]
        weighted = upstream * gain
        mean = row_sums(pair * weighted, low) * (1.0 / HEAD_DIM)
        result = factor * weighted - pair * (factor * factor * factor * mean)
        terms = jnp.sum(upstream * pair * factor, 0, keepdims=True)
        if p == 1:
            result = jnp.where(low, result, grad)
        out_ref[at, 128 * p : 128 * (p + 1)] = result.astype(BF)
        total_ref[p : p + 1, :] += terms

    total_ref[...] = jnp.zeros_like(total_ref)
    dkv = [0.0] * tiles
    for a in range(tiles):
        at = pl.ds(place(a), tile)
        query = stacked(qkv_ref[at, :128])
        grad = stacked(dm_ref[at])
        mixed = stacked(mixed_ref[at, :])
        delta = jnp.sum(grad.astype(F32) * mixed.astype(F32), -1, keepdims=True)
        grad_query = 0.0
        for k in range(a + 1):
            keys = pl.ds(place(k), tile)
            key = qkv_ref[keys, 128 : 128 + HEAD_DIM]
            value = qkv_ref[keys, 128 + HEAD_DIM :]
            probs = probs_ref[blocks_of(tiles).index((a, k))]
            grad_scores = (probs.astype(F32) * (mm_nt(grad, value) - delta)).astype(BF)
            grad_query = grad_query + mm(grad_scores, key)
            grad_kv = jnp.concatenate(
                [mm_tn(grad_scores, query) * scale, mm_tn(probs, grad)], 1
            )
            if a == k:
                dkv_ref[k] = grad_kv
            else:
                dkv_ref[k] += grad_kv
        grad_query = grad_query * scale
        finish(a, 0, jnp.concatenate([grad_query[:tile], grad_query[tile:]], 1))
    for k in range(tiles):
        finish(k, 1, dkv_ref[k])


def attend_back_call(at, qkv, mixed, probs, raw, g0, g1, wo, qk_gain, cosine, sine):
    count = qkv.shape[0]
    tile = min(256, count // 2)
    tiles = count // tile
    vmem = pl.BlockSpec(memory_space=pltpu.VMEM)
    return pl.pallas_call(
        functools.partial(attend_back_kernel, tile, tiles),
        in_specs=[pl.BlockSpec(memory_space=pltpu.SMEM)] + [vmem] * 10,
        out_specs=[vmem] * 2,
        out_shape=[
            jax.ShapeDtypeStruct((count, 256), BF),
            jax.ShapeDtypeStruct((8, 128), F32),
        ],
        scratch_shapes=[pltpu.VMEM((count, 128), BF), pltpu.VMEM((tiles, tile, 128), F32)],
        compiler_params=pltpu.CompilerParams(vmem_limit_bytes=VMEM_BYTES),
        cost_estimate=SMALL_COST,
        name="attend_back",
    )(at, qkv, mixed, probs, raw, g0, g1, wo, qk_gain, cosine, sine)


def ffn_kernel(fw, part, x_ref, cot_ref, *refs):
    in_refs, out_refs, (act_ref, grad_ref, grad_in_ref, out_ref) = refs[:4], refs[4:8], refs[8:]
    pre, grad_act = 0.0, 0.0
    for p in range(4):
        cut = slice(p * part, (p + 1) * part)
        pre = pre + mm(x_ref[:, cut], in_refs[p][...])
        grad_act = grad_act + mm(cot_ref[:, cut], out_refs[p][:, :fw])
    gate, up = pre[:, :fw], pre[:, fw:]
    sigmoid = 1.0 / (1.0 + jnp.exp(-gate))
    silu = gate * sigmoid
    act = (silu * up).astype(BF)
    act_ref[...] = act
    grad_gate = grad_act * up * sigmoid * (1.0 + gate * (1.0 - sigmoid))
    grad = jnp.concatenate([grad_gate, grad_act * silu], 1).astype(BF)
    grad_ref[...] = grad
    for p in range(4):
        cut = slice(p * part, (p + 1) * part)
        grad_in_ref[:, cut] = mm_nt(grad, in_refs[p][...]).astype(BF)
        out_ref[:, cut] = mm_nt(act, out_refs[p][:, :fw]).astype(BF)


def ffn_call(fw, x, cot, w_in, w_out):
    count, d_model = x.shape
    part = w_in[0].shape[0]
    tile = min(256, count)
    shapes = [(count, fw), (count, 2 * fw), (count, d_model), (count, d_model)]
    return pl.pallas_call(
        functools.partial(ffn_kernel, fw, part),
        grid=(count // tile,),
        in_specs=[
            pl.BlockSpec((tile, d_model), lambda i: (i, 0)),
            pl.BlockSpec((tile, d_model), lambda i: (i, 0)),
        ]
        + [pl.BlockSpec(p.shape, lambda i: (0, 0)) for p in (*w_in, *w_out)],
        out_specs=[pl.BlockSpec((tile, s[1]), lambda i: (i, 0)) for s in shapes],
        out_shape=[jax.ShapeDtypeStruct(s, BF) for s in shapes],
        compiler_params=pltpu.CompilerParams(vmem_limit_bytes=VMEM_BYTES),
        cost_estimate=SMALL_COST,
        name="ffn",
    )(x, cot, *w_in, *w_out)


def ffn_grad_kernel(fw, *refs):
    ins, outs = refs[:8], refs[8:]
    x0, x1, cot0, cot1, grad0, grad1, act0, act1 = (r[...] for r in ins)
    grad_in = (mm_tn(x0, grad0) + mm_tn(x1, grad1)).astype(BF)
    grad_out = (mm_tn(cot0, act0) + mm_tn(cot1, act1)).astype(BF)
    for p in range(2):

        @pl.when(pl.program_id(0) == p)
        def _():
            outs[2 * p][...] = grad_in
            outs[2 * p + 1][:, :fw] = grad_out
            rest = outs[2 * p + 1].shape[1] - fw
            if rest:
                outs[2 * p + 1][:, fw:] = jnp.zeros((grad_out.shape[0], rest), BF)


def ffn_grad_call(p, x, cot, grad, act):
    count, d_model = x[0].shape
    fw = act[0].shape[1]
    part = d_model // 4
    width = -(-fw // LANES) * LANES
    columns = pl.BlockSpec((count, part), lambda i: (0, p + i))
    whole = [pl.BlockSpec(a.shape, lambda i: (0, 0)) for a in (*grad, *act)]
    shapes = [(part, 2 * fw), (part, width)] * 2
    return pl.pallas_call(
        functools.partial(ffn_grad_kernel, fw),
        grid=(2,),
        in_specs=[columns] * 4 + whole,
        out_specs=[pl.BlockSpec(s, lambda i: (0, 0)) for s in shapes],
        out_shape=[jax.ShapeDtypeStruct(s, BF) for s in shapes],
        compiler_params=pltpu.CompilerParams(vmem_limit_bytes=VMEM_BYTES),
        cost_estimate=SMALL_COST,
        name="ffn_grad",
    )(*x, *cot, *grad, *act)


def body(
    hidden_in,
    lengths,
    positions,
    attn_gain,
    w_query,
    w_key,
    w_value,
    q_gain,
    k_gain,
    w_output,
    ffn_gain,
    w_gate,
    w_up,
    w_down,
    grad_out,
):
    H, B, J, T = (lax.axis_size(a) for a in ("h", "b", "j", "tp"))
    ix, ih, ib, ij, it = (lax.axis_index(a) for a in ("dp", "h", "b", "j", "tp"))
    rows = hidden_in.shape[2]
    d_model = hidden_in.shape[3]
    shard = w_query.shape[0]
    group = HEADS // KV_HEADS
    qw = group * HEAD_DIM
    fw = w_gate.shape[1] // J
    count = T * J * rows
    side = J * rows
    down_width = -(-fw // LANES) * LANES
    ffn_width = 2 * fw + down_width
    score_scale = HEAD_DIM ** (-0.5)
    quarter = 2 * ix + ih
    part = d_model // 4

    def cut(array, p, width):
        return array[:, p * width : (p + 1) * width]

    def exchange(name, pieces):
        with jax.named_scope(name):
            return lax.all_to_all(pieces, "j", 0, 0)

    def exchange_beside(name, pieces):
        with jax.named_scope(name):
            pieces = in_order(pieces, ij)
            parts = [pieces[0]]
            for d in range(1, J):
                parts.append(lax.ppermute(pieces[d], "j", [(i, i ^ d) for i in range(J)]))
            return jnp.concatenate(in_order(parts, ij), 0)

    def two_numbers(values):
        high = values.astype(BF)
        low = (values - high.astype(F32)).astype(BF)
        return jnp.pad(jnp.concatenate([high, low], 0), ((0, 6), (0, 0)))

    def one_number(block):
        return block[..., 0:1, :].astype(F32) + block[..., 1:2, :].astype(F32)

    def relative(array):
        pieces = [array[..., p * part : (p + 1) * part] for p in range(4)]
        return jnp.concatenate(in_order(pieces, quarter), -1)

    turn = [(0, 0), (1, 2), (2, 1), (3, 3)]

    def fetch(name, array):
        with jax.named_scope(name):
            mine = lax.dynamic_index_in_dim(array, it, 0, keepdims=False)[0]
            return lax.ppermute(mine, ("h", "tp"), turn)

    def give_back_turned(name, mine):
        with jax.named_scope(name):
            return jnp.stack(in_order([mine, swap(mine, "tp")], it), 0)[:, None]

    def give_back(name, block):
        with jax.named_scope(name):
            return give_back_turned(name, lax.ppermute(block, ("h", "tp"), turn))

    def gather_half(name, block, *others):
        with jax.named_scope(name):
            sent = jnp.broadcast_to(block[None], (J, *block.shape))
            if others:
                sent = after(sent, *others)
            return lax.all_to_all(sent, "j", 0, 0).reshape(side, d_model)

    def sum_tokens(name, half, *others):
        with jax.named_scope(name):
            got = lax.all_to_all(half.reshape(J, rows, d_model), "j", 0, 0)
            if others:
                got = after(got, *others)
            return jnp.sum(got.astype(F32), 0)

    w_output_t = w_output.T
    w_down_t = w_down.T
    wide = 2 * qw + 2 * HEAD_DIM
    pos = positions[:, 0].reshape(1, H * rows)
    high = pos // 256
    extra = [jnp.concatenate([attn_gain, ffn_gain])[None], high.astype(BF), (pos - high * 256).astype(BF)]
    extra = [jnp.pad(e, ((0, 0), (0, wide - e.shape[1]))) for e in extra]
    extra = jnp.pad(jnp.concatenate(extra, 0), ((0, 5), (0, 0)))
    pack = [
        jnp.concatenate(
            [
                jnp.concatenate(
                    [
                        cut(w_query, p, qw),
                        cut(w_key, p, HEAD_DIM),
                        cut(w_value, p, HEAD_DIM),
                        cut(w_output_t, p, qw),
                    ],
                    1,
                ),
                extra,
            ],
            0,
        )
        for p in range(J)
    ]
    own = exchange_beside("weights_attn", pack).reshape(J, shard + 8, wide)
    pack = [
        jnp.pad(
            jnp.concatenate([cut(w_gate, p, fw), cut(w_up, p, fw), cut(w_down_t, p, fw)], 1),
            ((0, 0), (0, ffn_width - 3 * fw)),
        )
        for p in range(J)
    ]
    ffn_own = exchange_beside("weights_ffn", pack)
    hidden_own = relative(fetch("fetch_hidden", hidden_in))
    cot_own = relative(fetch("fetch_cot", grad_out))
    own = after(own, ffn_own)
    with jax.named_scope("weights_attn"):
        if B > 1:
            own = lax.all_gather(own, "b", axis=0, tiled=True)
        across = lax.ppermute(own, ("dp", "h"), [(i, i ^ 3) for i in range(4)])
        beside = swap(own, "h")
        opposite = swap(own, "dp")
    half = gather_half("tokens_hidden", hidden_own)
    half = after(half, beside, opposite, across, cot_own)
    with jax.named_scope("weights_ffn"):
        if B > 1:
            ffn_own = lax.all_gather(ffn_own, "b", axis=0, tiled=True)
        ffn_own = after(ffn_own, half)
        w_in = [ffn_own[:, : 2 * fw]]
        w_out = [ffn_own[:, 2 * fw :]]
        w_in += [swap(w_in[0], "h"), swap(w_in[0], "dp")]
        w_out += [swap(after(w_out[0], w_in[1]), "h"), swap(w_out[0], "dp")]
    with jax.named_scope("tokens_hidden"):
        hidden = [half, swap(half, "tp")]

    with jax.named_scope("weights_attn"):
        parts = [own, beside, opposite, across]
        wa = jnp.stack([p[:, :shard] for p in parts]).reshape(d_model, wide)
        extra = jnp.stack([p[:, shard : shard + 3] for p in parts])
    gains = extra[:, :, 0, : 2 * shard].reshape(4, B * J, 2, shard)
    gains = gains.transpose(2, 0, 1, 3).reshape(2, d_model).astype(F32)
    gain_attn = gains[0]
    gain_ffn = gains[1]
    pos = extra[:2, :, 1:, : H * rows].astype(F32)
    pos = pos[:, :, 0] * 256.0 + pos[:, :, 1]
    pos = lax.dynamic_index_in_dim(pos.reshape(H, B, J, H, rows), ib, 1, keepdims=False)
    pos = jnp.where(ih == 0, pos[:, :, 0], pos[:, :, 1])
    pos = jnp.stack(in_order([pos[0], pos[1]], ih ^ it), 0)
    pos_all = pos.reshape(count)

    stream = hidden_own.astype(F32)
    valid_length = lax.dynamic_index_in_dim(lengths[:, 0], ih, 0, keepdims=False)

    place = jnp.arange(T * J, dtype=jnp.int32)
    block_of = (it ^ (place // J)) * (B * J) + place % J
    row_of = jnp.arange(rows, dtype=jnp.int32)
    query_index = ((block_of + ib * J)[:, None] * rows + row_of[None, :]).reshape(count)
    key_index = (
        (block_of[None, :] + jnp.arange(B, dtype=jnp.int32)[:, None] * J)[..., None] * rows + row_of
    ).reshape(B * count)

    inverse = 1.0 / ROPE_BASE ** (jnp.arange(0, HEAD_DIM, 2, dtype=F32) / HEAD_DIM)
    if B == 1:
        inverse = jnp.tile(inverse, 2 * LANES // HEAD_DIM)
    angles = pos_all[:, None] * inverse[None, :]
    cosine = jnp.cos(angles)
    sine = jnp.sin(angles)

    attn_factor = norm_scale(stream)
    if B == 1:
        at = jnp.stack([valid_length, it])
        ones = jnp.ones((HEAD_DIM,), F32)
        qk_gain = jnp.stack(
            [jnp.concatenate([q_gain, q_gain]).astype(F32), jnp.concatenate([k_gain.astype(F32), ones])]
        )
        *normed, raw, qkv = qkv_call(*hidden, gain_attn[None], wa, qk_gain, cosine, sine)
        mixed, probs = attend_call(at, qkv)
    else:
        hidden = jnp.concatenate(hidden, 0).astype(F32)
        normed = (hidden * norm_scale(hidden) * gain_attn).astype(BF)
        cosine = jnp.concatenate([cosine, cosine], -1)[:, None, :]
        sine = jnp.concatenate([sine, sine], -1)[:, None, :]
        raw = mm(normed, wa[:, : qw + 2 * HEAD_DIM])
        normed = [normed[:side], normed[side:]]
        qk_raw = raw[:, : qw + HEAD_DIM].reshape(count, group + 1, HEAD_DIM)
        qk_gain = jnp.stack([q_gain] * group + [k_gain]).astype(F32)
        qk_factor = norm_scale(qk_raw)
        qk_normed = qk_raw * qk_factor * qk_gain
        qk = (qk_normed * cosine + half_turn(qk_normed) * sine).astype(BF)
        queries = qk[:, :group].transpose(1, 0, 2)
        keys = qk[:, group]
        values = raw[:, qw + HEAD_DIM :].astype(BF)
        if B > 1:
            keys = lax.all_gather(keys, "b", axis=0, tiled=True)
            values = lax.all_gather(values, "b", axis=0, tiled=True)
        visible = (key_index[None, :] <= query_index[:, None]) & (key_index[None, :] < valid_length)

        def scores_of(query_head):
            return jnp.where(visible, mm_nt(query_head, keys) * score_scale, MASKED)

        def attend(query_head):
            scores = scores_of(query_head)
            row_max = jnp.max(scores, -1, keepdims=True)
            exp_scores = jnp.exp(scores - row_max)
            row_total = jnp.sum(exp_scores, -1, keepdims=True)
            probs = (exp_scores / row_total).astype(BF)
            return mm(probs, values).astype(BF), row_max + jnp.log(row_total)

        heads = [attend(queries[g]) for g in range(group)]
        mixed = jnp.concatenate([h[0] for h in heads], -1)
    cot_half = gather_half("tokens_cot", cot_own, half)
    mixed = after(mixed, cot_half, w_in[1], w_in[2])
    with jax.named_scope("sum_attn"):
        wo = wa[:, qw + 2 * HEAD_DIM :]
        low = swap(mm_nt(mixed[side:], wo).astype(BF), "tp")
        low = add(mm_nt(mixed[:side], wo), low)
        attn_branch = sum_tokens("sum_attn", low, w_out[1], w_out[2])

    middle = stream + attn_branch
    with jax.named_scope("weights_ffn"):
        w_in.append(swap(w_in[1], "dp"))
        w_out.append(swap(w_out[1], "dp"))
    ffn_factor = norm_scale(middle)
    xf_own = (middle * ffn_factor * gain_ffn).astype(BF)
    ffn_half = gather_half("tokens_xf", xf_own)
    ffn_half = after(ffn_half, w_out[3], w_in[3])
    ffn_in = [ffn_half, swap(ffn_half, "tp")]
    cot = [cot_half, swap(cot_half, "tp")]
    hidden_act, grad_pre, grad_in, branch = zip(
        *[ffn_call(fw, ffn_in[i], cot[i], w_in, w_out) for i in range(2)]
    )
    low = add(grad_in[0], swap(grad_in[1], "tp"))
    opposite_in, opposite_out, across_in, across_out = ffn_grad_call(
        2, ffn_in, cot, grad_pre, hidden_act
    )
    with jax.named_scope("grads_ffn"):
        got_out, got_in = swap(across_out, "dp"), swap(across_in, "dp")
    grad_ffn_in = sum_tokens("sum_dxf", low, got_in)
    late = [after(a, grad_ffn_in) for a in hidden_act]
    near_in, near_out, beside_in, beside_out = ffn_grad_call(0, ffn_in, cot, grad_pre, late)

    grad_middle = cot_own.astype(F32) + norm_back(middle, ffn_factor, gain_ffn, grad_ffn_in)
    with jax.named_scope("grads_ffn"):
        beside_in = add(beside_in, got_in)
    half = gather_half("tokens_dattn", grad_middle.astype(BF))
    with jax.named_scope("sum_out"):
        low = add(branch[0], swap(after(branch[1], grad_ffn_in), "tp"))
    with jax.named_scope("grads_ffn"):
        got_in = swap(beside_in, "h")
        half = after(half, low, got_out, beside_in)
        beside_out = add(beside_out, got_out)
        opposite = after(opposite_out, half), after(opposite_in, half)
        opposite = swap(opposite[0], "dp"), swap(opposite[1], "dp")
    grad_attn = [half, swap(half, "tp")]
    low = after(low, half)
    total = sum_tokens("sum_out", low)
    if B == 1:
        grad_raw, totals = attend_back_call(
            at, qkv, mixed, probs, raw, *grad_attn, wo, qk_gain, cosine, sine
        )
        totals = jnp.concatenate([totals[0, :HEAD_DIM] + totals[0, HEAD_DIM:], totals[1, :HEAD_DIM]])
    else:
        grad_mixed = mm(jnp.concatenate(grad_attn, 0), wo).astype(BF)
        grad_keys = jnp.zeros((B * count, HEAD_DIM), F32)
        grad_values = jnp.zeros((B * count, HEAD_DIM), F32)
        grad_queries = []
        for g in range(group):
            probs = jnp.exp(scores_of(queries[g]) - heads[g][1])
            grad_head = grad_mixed[:, g * HEAD_DIM : (g + 1) * HEAD_DIM]
            grad_probs = mm_nt(grad_head, values)
            row_delta = jnp.sum(grad_probs * probs, -1, keepdims=True)
            grad_scores = (probs * (grad_probs - row_delta)).astype(BF)
            grad_queries.append(mm(grad_scores, keys) * score_scale)
            grad_keys = grad_keys + mm_tn(grad_scores, queries[g]) * score_scale
            grad_values = grad_values + mm_tn(probs.astype(BF), grad_head)
        if B > 1:
            grad_keys = lax.psum_scatter(grad_keys, "b", scatter_dimension=0, tiled=True)
            grad_values = lax.psum_scatter(grad_values, "b", scatter_dimension=0, tiled=True)
        grad_rot = jnp.stack(grad_queries + [grad_keys], 1)
        grad_normed = grad_rot * cosine + half_turn_back(grad_rot * sine)
        grad_qk_raw = norm_back(qk_raw, qk_factor, qk_gain, grad_normed)
        terms = jnp.sum(grad_normed * qk_raw * qk_factor, 0)
        totals = jnp.concatenate([jnp.sum(terms[:group], 0), terms[group]])
        grad_raw = jnp.concatenate(
            [grad_qk_raw.reshape(count, qw + HEAD_DIM), grad_values], 1
        ).astype(BF)
    w_qkv = wa[:, : qw + 2 * HEAD_DIM]
    low = swap(mm_nt(grad_raw[side:], w_qkv).astype(BF), "tp")
    low = add(mm_nt(grad_raw[:side], w_qkv), low)
    with jax.named_scope("grads_ffn"):
        got_h = swap(after(beside_out, grad_raw), "h")
        opposite = after(opposite[0], low), after(opposite[1], low)
    total = after(total, low)
    out_own = relative((middle + total).astype(BF))
    late, mixed = after(grad_raw, low), after(mixed, low)
    grad_wqkv = mm_tn(normed[0], late[:side]) + mm_tn(normed[1], late[side:])
    grad_wo = mm_tn(grad_attn[0], mixed[:side]) + mm_tn(grad_attn[1], mixed[side:])
    grad_wa = jnp.concatenate([grad_wqkv, grad_wo], 1).astype(BF)
    grad_normed_own = sum_tokens("sum_dxa", low, out_own, grad_wa)
    grad_stream = grad_middle + norm_back(stream, attn_factor, gain_attn, grad_normed_own)
    with jax.named_scope("return_out"):
        out_turned = lax.ppermute(out_own, ("h", "tp"), turn)
    sent = after(relative(grad_stream.astype(BF)), out_turned)
    grad_hidden = give_back("return_grad", sent)
    out_hidden = give_back_turned("return_out", out_turned)
    with jax.named_scope("grads_attn"):
        totals = jnp.pad(totals[None], ((0, 0), (0, wide - 2 * HEAD_DIM)))
        near, beside, opposed, across = (grad_wa[p * part : (p + 1) * part] for p in range(4))
        got = swap(jnp.concatenate([across, two_numbers(totals)], 0), "dp")
        got_near = swap(opposed, "dp")
        totals = totals + one_number(got[part:])
        beside = jnp.concatenate([add(beside, got[:part]), two_numbers(totals)], 0)
        got = swap(beside, "h")
        got = after(got, sent)
        near = add(near.astype(F32) + got_near.astype(F32), got[:part])
        totals = totals + one_number(got[part:])
    with jax.named_scope("grads"):
        near_in = add(near_in.astype(F32) + opposite[1].astype(F32), after(got_in, low))
        near_out = add(near_out.astype(F32) + opposite[0].astype(F32), after(got_h, low))
        near = jnp.concatenate([near, near_in, near_out], 1)
        if B > 1:
            near = lax.psum_scatter(near, "b", scatter_dimension=0, tiled=True)
            totals = lax.psum(totals, "b")
        extra = two_numbers(totals[:, :LANES])
        extra = jnp.pad(extra, ((0, shard - extra.shape[0]), (0, 0)))
        extra = jnp.broadcast_to(extra[None], (J, shard, LANES))
        near = jnp.concatenate([near.reshape(J, shard, near.shape[1]), extra], 2)
        shards = lax.all_to_all(near, "j", 0, 0)
    totals = jnp.sum(one_number(shards[:, :, -LANES:]), (0, 1))

    def join(arrays, start, width):
        return jnp.concatenate([a[:, start : start + width] for a in arrays], 1).astype(F32)

    shard_query = join(shards, 0, qw)
    shard_key = join(shards, qw, HEAD_DIM)
    shard_value = join(shards, qw + HEAD_DIM, HEAD_DIM)
    shard_output = join(shards, qw + 2 * HEAD_DIM, qw)
    shard_gate = join(shards, wide, fw)
    shard_up = join(shards, wide + fw, fw)
    shard_down = join(shards, wide + 2 * fw, fw)

    sum_attn = (
        jnp.sum(shard_query * w_query.astype(F32), 1)
        + jnp.sum(shard_key * w_key.astype(F32), 1)
        + jnp.sum(shard_value * w_value.astype(F32), 1)
    )
    sum_ffn = jnp.sum(shard_gate * w_gate.astype(F32), 1) + jnp.sum(
        shard_up * w_up.astype(F32), 1
    )
    sums = jnp.concatenate([totals[: 2 * HEAD_DIM], sum_attn, sum_ffn])
    sums = sums + swap(sums, "tp")
    totals = sums[: 2 * HEAD_DIM].reshape(2, HEAD_DIM)
    sums = sums[2 * HEAD_DIM :].reshape(2, shard) / jnp.stack([attn_gain, ffn_gain]).astype(F32)

    return (
        out_hidden,
        grad_hidden,
        sums[0],
        shard_query,
        shard_key,
        shard_value,
        totals[0],
        totals[1],
        shard_output.T,
        sums[1],
        shard_gate,
        shard_up,
        shard_down.T,
    )


def solution(mesh):
    places = KV_HEADS // mesh.shape["tp"]

    def run(*args):
        micro = args[0].shape[0]
        shape = (mesh.shape["dp"], micro, mesh.shape["ctx"] // (micro * places), places)
        fine = Mesh(
            mesh.devices.reshape(*shape, mesh.shape["tp"]), ("dp", "h", "b", "j", "tp")
        )
        ctx = ("h", "b", "j")
        rows = ("dp", "h", "b", "j")
        tokens = P(None, "dp", ctx, None)
        return jax.shard_map(
            body,
            mesh=fine,
            in_specs=(
                tokens,
                P(None, "dp"),
                P(None, "dp", ctx),
                P(rows),
                P(rows, "tp"),
                P(rows, "tp"),
                P(rows, "tp"),
                P(),
                P(),
                P("tp", rows),
                P(rows),
                P(rows, "tp"),
                P(rows, "tp"),
                P("tp", rows),
                tokens,
            ),
            out_specs=(
                tokens,
                tokens,
                P(rows),
                P(rows, "tp"),
                P(rows, "tp"),
                P(rows, "tp"),
                P(),
                P(),
                P("tp", rows),
                P(rows),
                P(rows, "tp"),
                P(rows, "tp"),
                P("tp", rows),
            ),
            check_vma=False,
        )(*args)

    return run
```

```python
import functools

import jax
import jax.numpy as jnp
from jax import lax
from jax.experimental import pallas as pl
from jax.experimental.pallas import tpu as pltpu
from jax.sharding import Mesh, PartitionSpec as P

HEADS = 16
KV_HEADS = 8
HEAD_DIM = 64
EPSILON = 1e-05
ROPE_BASE = 1000000.0
MASKED = -1e30
BF = jnp.bfloat16
F32 = jnp.float32
VMEM_BYTES = 60 * 2**20
LANES = 128
SMALL_COST = pl.CostEstimate(flops=1, bytes_accessed=1, transcendentals=0)


def dot(a, b, dims):
    return lax.dot_general(a, b, (dims, ((), ())), preferred_element_type=F32)


def mm(a, b):
    return dot(a, b, ((1,), (0,)))


def mm_nt(a, b):
    return dot(a, b, ((1,), (1,)))


def mm_tn(a, b):
    return dot(a, b, ((0,), (0,)))


def nothing(*refs):
    pass


def after(value, *others):
    anywhere = pl.BlockSpec(memory_space=pl.ANY)
    return pl.pallas_call(
        nothing,
        in_specs=[anywhere] * (1 + len(others)),
        out_specs=anywhere,
        out_shape=jax.ShapeDtypeStruct(value.shape, value.dtype),
        input_output_aliases={0: 0},
        cost_estimate=SMALL_COST,
        name="after",
    )(value, *others)


def swap(v, axis):
    return lax.ppermute(v, axis, [(0, 1), (1, 0)])


def add(a, b):
    return (a.astype(F32) + b.astype(F32)).astype(BF)


def norm_scale(vector):
    return lax.rsqrt(jnp.mean(vector * vector, -1, keepdims=True) + EPSILON)


def norm_back(vector, factor, gain, upstream):
    weighted = upstream * gain
    return factor * weighted - vector * factor * factor * factor * jnp.mean(
        vector * weighted, -1, keepdims=True
    )


def half_turn(vector):
    middle_index = vector.shape[-1] // 2
    return jnp.concatenate([-vector[..., middle_index:], vector[..., :middle_index]], -1)


def half_turn_back(vector):
    middle_index = vector.shape[-1] // 2
    return jnp.concatenate([vector[..., middle_index:], -vector[..., :middle_index]], -1)


def in_order(parts, index):
    bit = 1
    while bit < len(parts):
        flag = (index & bit) != 0
        parts = [jnp.where(flag, parts[i ^ bit], parts[i]) for i in range(len(parts))]
        bit *= 2
    return parts


def row_sums(square, low):
    left = jnp.sum(jnp.where(low, square, 0.0), -1, keepdims=True)
    right = jnp.sum(jnp.where(low, 0.0, square), -1, keepdims=True)
    return jnp.where(low, left, right)


def pair_scale(pair, low):
    return lax.rsqrt(row_sums(pair * pair, low) * (1.0 / HEAD_DIM) + EPSILON)


def lanes(shape):
    return lax.broadcasted_iota(jnp.int32, shape, 1)


def turned(pair, first):
    width = pair.shape[1]
    quarter = HEAD_DIM // 2
    return jnp.where(first, pltpu.roll(pair, width - quarter, 1), pltpu.roll(pair, quarter, 1))


def qkv_kernel(half_tiles, h0_ref, h1_ref, gain_ref, w_ref, qk_gain_ref, cos_ref, sin_ref,
               xa0_ref, xa1_ref, raw_ref, qkv_ref):
    def run(h_ref, xa_ref):
        hidden = h_ref[...].astype(F32)
        factor = lax.rsqrt(jnp.mean(hidden * hidden, -1, keepdims=True) + EPSILON)
        xa = (hidden * factor * gain_ref[...]).astype(BF)
        xa_ref[...] = xa
        raw = mm(xa, w_ref[:, :256])
        raw_ref[...] = raw
        lane = lanes((raw.shape[0], 128))
        low = lane < HEAD_DIM
        first = lane % HEAD_DIM < HEAD_DIM // 2
        cosine, sine = cos_ref[...], sin_ref[...]
        sine = jnp.where(first, -sine, sine)
        for p in range(2):
            pair = raw[:, 128 * p : 128 * (p + 1)]
            normed = pair * pair_scale(pair, low) * qk_gain_ref[p : p + 1, :]
            turned_pair = normed * cosine + turned(normed, first) * sine
            if p == 1:
                turned_pair = jnp.where(low, turned_pair, pair)
            qkv_ref[:, 128 * p : 128 * (p + 1)] = turned_pair.astype(BF)

    @pl.when(pl.program_id(0) < half_tiles)
    def _():
        run(h0_ref, xa0_ref)

    @pl.when(pl.program_id(0) >= half_tiles)
    def _():
        run(h1_ref, xa1_ref)


def qkv_call(h0, h1, gain, w, qk_gain, cosine, sine):
    half, d_model = h0.shape
    tile = min(256, half)
    n = half // tile
    own = pl.BlockSpec((tile, d_model), lambda i: (jnp.minimum(i, n - 1), 0))
    other = pl.BlockSpec((tile, d_model), lambda i: (jnp.maximum(i - n, 0), 0))
    def fixed(a):
        return pl.BlockSpec(a.shape, lambda i: (0, 0))
    def rows(width):
        return pl.BlockSpec((tile, width), lambda i: (i, 0))
    return pl.pallas_call(
        functools.partial(qkv_kernel, n),
        grid=(2 * n,),
        in_specs=[own, other, fixed(gain), fixed(w), fixed(qk_gain), rows(128), rows(128)],
        out_specs=[own, other, rows(256), rows(256)],
        out_shape=[
            jax.ShapeDtypeStruct(h0.shape, BF),
            jax.ShapeDtypeStruct(h0.shape, BF),
            jax.ShapeDtypeStruct((2 * half, 256), F32),
            jax.ShapeDtypeStruct((2 * half, 256), BF),
        ],
        compiler_params=pltpu.CompilerParams(vmem_limit_bytes=VMEM_BYTES),
        cost_estimate=SMALL_COST,
        name="qkv",
    )(h0, h1, gain, w, qk_gain, cosine, sine)


def blocks_of(tiles):
    return [(a, k) for a in range(tiles) for k in range(a + 1)]


def stacked(pair):
    return jnp.concatenate([pair[:, :HEAD_DIM], pair[:, HEAD_DIM:]], 0)


def attend_kernel(tile, tiles, at_ref, qkv_ref, mixed_ref, probs_ref):
    half = tiles // 2
    def place(t):
        return pl.multiple_of((t + half * at_ref[1]) % tiles * tile, tile)
    for a in range(tiles):
        query = stacked(qkv_ref[pl.ds(place(a), tile), :128])
        row = lax.broadcasted_iota(jnp.int32, (2 * tile, 1), 0) % tile + a * tile
        limit = jnp.minimum(row + 1, at_ref[0])
        scores = []
        for k in range(a + 1):
            key = qkv_ref[pl.ds(place(k), tile), 128 : 128 + HEAD_DIM]
            column = lax.broadcasted_iota(jnp.int32, (1, tile), 1) + k * tile
            scores.append(
                jnp.where(column < limit, mm_nt(query, key) * HEAD_DIM ** (-0.5), MASKED)
            )
        peak = functools.reduce(jnp.maximum, [jnp.max(s, -1, keepdims=True) for s in scores])
        exps = [jnp.exp(s - peak) for s in scores]
        total = functools.reduce(jnp.add, [jnp.sum(e, -1, keepdims=True) for e in exps])
        inverse = 1.0 / total
        mixed = 0.0
        for k in range(a + 1):
            probs = (exps[k] * inverse).astype(BF)
            probs_ref[blocks_of(tiles).index((a, k))] = probs
            value = qkv_ref[pl.ds(place(k), tile), 128 + HEAD_DIM :]
            mixed = mixed + mm(probs, value)
        mixed_ref[pl.ds(place(a), tile), :] = jnp.concatenate(
            [mixed[:tile], mixed[tile:]], 1
        ).astype(BF)


def attend_call(at, qkv):
    count = qkv.shape[0]
    tile = min(256, count // 2)
    tiles = count // tile
    pairs = len(blocks_of(tiles))
    return pl.pallas_call(
        functools.partial(attend_kernel, tile, tiles),
        in_specs=[pl.BlockSpec(memory_space=pltpu.SMEM), pl.BlockSpec(memory_space=pltpu.VMEM)],
        out_specs=[pl.BlockSpec(memory_space=pltpu.VMEM)] * 2,
        out_shape=[
            jax.ShapeDtypeStruct((count, 128), BF),
            jax.ShapeDtypeStruct((pairs, 2 * tile, tile), BF),
        ],
        compiler_params=pltpu.CompilerParams(vmem_limit_bytes=VMEM_BYTES),
        cost_estimate=SMALL_COST,
        name="attend",
    )(at, qkv)


def attend_back_kernel(tile, tiles, at_ref, qkv_ref, mixed_ref, probs_ref, raw_ref, g0_ref, g1_ref,
                       wo_ref, qk_gain_ref, cos_ref, sin_ref, out_ref, total_ref, dm_ref, dkv_ref):
    half = tiles // 2
    def place(t):
        return pl.multiple_of((t + half * at_ref[1]) % tiles * tile, tile)
    rows = half * tile
    dm_ref[:rows] = mm(g0_ref[...], wo_ref[...]).astype(BF)
    dm_ref[rows:] = mm(g1_ref[...], wo_ref[...]).astype(BF)
    scale = HEAD_DIM ** (-0.5)
    lane = lanes((tile, 128))
    low = lane < HEAD_DIM
    first = lane % HEAD_DIM < HEAD_DIM // 2

    def finish(t, p, grad):
        at = pl.ds(place(t), tile)
        cosine, sine = cos_ref[at], sin_ref[at]
        pair = raw_ref[at, 128 * p : 128 * (p + 1)]
        factor = pair_scale(pair, low)
        signed = grad * jnp.where(first, -sine, sine)
        upstream = grad * cosine + turned(signed, first)
        gain = qk_gain_ref[p : p + 1, :]
        weighted = upstream * gain
        mean = row_sums(pair * weighted, low) * (1.0 / HEAD_DIM)
        result = factor * weighted - pair * (factor * factor * factor * mean)
        terms = jnp.sum(upstream * pair * factor, 0, keepdims=True)
        if p == 1:
            result = jnp.where(low, result, grad)
        out_ref[at, 128 * p : 128 * (p + 1)] = result.astype(BF)
        total_ref[p : p + 1, :] += terms

    total_ref[...] = jnp.zeros_like(total_ref)
    dkv = [0.0] * tiles
    for a in range(tiles):
        at = pl.ds(place(a), tile)
        query = stacked(qkv_ref[at, :128])
        grad = stacked(dm_ref[at])
        mixed = stacked(mixed_ref[at, :])
        delta = jnp.sum(grad.astype(F32) * mixed.astype(F32), -1, keepdims=True)
        grad_query = 0.0
        for k in range(a + 1):
            keys = pl.ds(place(k), tile)
            key = qkv_ref[keys, 128 : 128 + HEAD_DIM]
            value = qkv_ref[keys, 128 + HEAD_DIM :]
            probs = probs_ref[blocks_of(tiles).index((a, k))]
            grad_scores = (probs.astype(F32) * (mm_nt(grad, value) - delta)).astype(BF)
            grad_query = grad_query + mm(grad_scores, key)
            grad_kv = jnp.concatenate(
                [mm_tn(grad_scores, query) * scale, mm_tn(probs, grad)], 1
            )
            if a == k:
                dkv_ref[k] = grad_kv
            else:
                dkv_ref[k] += grad_kv
        grad_query = grad_query * scale
        finish(a, 0, jnp.concatenate([grad_query[:tile], grad_query[tile:]], 1))
    for k in range(tiles):
        finish(k, 1, dkv_ref[k])


def attend_back_call(at, qkv, mixed, probs, raw, g0, g1, wo, qk_gain, cosine, sine):
    count = qkv.shape[0]
    tile = min(256, count // 2)
    tiles = count // tile
    vmem = pl.BlockSpec(memory_space=pltpu.VMEM)
    return pl.pallas_call(
        functools.partial(attend_back_kernel, tile, tiles),
        in_specs=[pl.BlockSpec(memory_space=pltpu.SMEM)] + [vmem] * 10,
        out_specs=[vmem] * 2,
        out_shape=[
            jax.ShapeDtypeStruct((count, 256), BF),
            jax.ShapeDtypeStruct((8, 128), F32),
        ],
        scratch_shapes=[pltpu.VMEM((count, 128), BF), pltpu.VMEM((tiles, tile, 128), F32)],
        compiler_params=pltpu.CompilerParams(vmem_limit_bytes=VMEM_BYTES),
        cost_estimate=SMALL_COST,
        name="attend_back",
    )(at, qkv, mixed, probs, raw, g0, g1, wo, qk_gain, cosine, sine)


def ffn_kernel(fw, part, x_ref, cot_ref, *refs):
    a_refs, b_refs, (w_ref, act_ref, grad_ref, grad_in_ref, out_ref) = refs[:3], refs[3:6], refs[6:]
    width = a_refs[0].shape[1]
    a_refs = [*a_refs[:2], w_ref.at[:, :width], a_refs[2]]
    b_refs = [*b_refs[:2], w_ref.at[:, width:], b_refs[2]]
    rest = 2 * fw - width
    pre_a, pre_b, grad_act = 0.0, 0.0, 0.0
    for p in range(4):
        cut = slice(p * part, (p + 1) * part)
        pre_a = pre_a + mm(x_ref[:, cut], a_refs[p][...])
        pre_b = pre_b + mm(x_ref[:, cut], b_refs[p][:, :rest])
        grad_act = grad_act + mm(cot_ref[:, cut], b_refs[p][:, rest : rest + fw])
    pre = jnp.concatenate([pre_a, pre_b], 1)
    gate, up = pre[:, :fw], pre[:, fw:]
    sigmoid = 1.0 / (1.0 + jnp.exp(-gate))
    silu = gate * sigmoid
    act = (silu * up).astype(BF)
    act_ref[...] = act
    grad_gate = grad_act * up * sigmoid * (1.0 + gate * (1.0 - sigmoid))
    grad = jnp.concatenate([grad_gate, grad_act * silu], 1).astype(BF)
    grad_ref[...] = grad
    for p in range(4):
        cut = slice(p * part, (p + 1) * part)
        grad_in = mm_nt(grad[:, :width], a_refs[p][...])
        grad_in = grad_in + mm_nt(grad[:, width:], b_refs[p][:, :rest])
        grad_in_ref[:, cut] = grad_in.astype(BF)
        out_ref[:, cut] = mm_nt(act, b_refs[p][:, rest : rest + fw]).astype(BF)


def ffn_call(fw, x, cot, w_a, w_b, w_own):
    count, d_model = x.shape
    part = w_a[0].shape[0]
    tile = min(256, count)
    shapes = [(count, fw), (count, 2 * fw), (count, d_model), (count, d_model)]
    return pl.pallas_call(
        functools.partial(ffn_kernel, fw, part),
        grid=(count // tile,),
        in_specs=[
            pl.BlockSpec((tile, d_model), lambda i: (i, 0)),
            pl.BlockSpec((tile, d_model), lambda i: (i, 0)),
        ]
        + [pl.BlockSpec(p.shape, lambda i: (0, 0)) for p in (*w_a, *w_b, w_own)],
        out_specs=[pl.BlockSpec((tile, s[1]), lambda i: (i, 0)) for s in shapes],
        out_shape=[jax.ShapeDtypeStruct(s, BF) for s in shapes],
        compiler_params=pltpu.CompilerParams(vmem_limit_bytes=VMEM_BYTES),
        cost_estimate=SMALL_COST,
        name="ffn",
    )(x, cot, *w_a, *w_b, w_own)


def ffn_grad_kernel(fw, width, whole, *refs):
    ins, outs = refs[:8], refs[8:]
    x0, x1, cot0, cot1, grad0, grad1, act0, act1 = (r[...] for r in ins)
    grad_in = (mm_tn(x0, grad0) + mm_tn(x1, grad1)).astype(BF)
    grad_out = (mm_tn(cot0, act0) + mm_tn(cot1, act1)).astype(BF)
    rest = 2 * fw - width

    def write(a_ref, b_ref):
        a_ref[...] = grad_in[:, :width]
        b_ref[:, :rest] = grad_in[:, width:]
        b_ref[:, rest : rest + fw] = grad_out
        left = width - rest - fw
        if left:
            b_ref[:, rest + fw :] = jnp.zeros((grad_out.shape[0], left), BF)

    @pl.when(pl.program_id(0) == 0)
    def _():
        if whole:
            write(outs[0].at[:, :width], outs[0].at[:, width:])
        else:
            write(*outs[:2])

    @pl.when(pl.program_id(0) == 1)
    def _():
        write(*outs[-2:])


def ffn_grad_call(p, width, whole, x, cot, grad, act):
    count, d_model = x[0].shape
    fw = act[0].shape[1]
    part = d_model // 4
    columns = pl.BlockSpec((count, part), lambda i: (0, p + i))
    operands = [pl.BlockSpec(a.shape, lambda i: (0, 0)) for a in (*grad, *act)]
    shapes = ([(part, 2 * width)] if whole else [(part, width)] * 2) + [(part, width)] * 2
    return pl.pallas_call(
        functools.partial(ffn_grad_kernel, fw, width, whole),
        grid=(2,),
        in_specs=[columns] * 4 + operands,
        out_specs=[pl.BlockSpec(s, lambda i: (0, 0)) for s in shapes],
        out_shape=[jax.ShapeDtypeStruct(s, BF) for s in shapes],
        compiler_params=pltpu.CompilerParams(vmem_limit_bytes=VMEM_BYTES),
        cost_estimate=SMALL_COST,
        name="ffn_grad",
    )(*x, *cot, *grad, *act)


def attn_grad_kernel(x0_ref, x1_ref, g0_ref, g1_ref, raw_ref, mixed_ref, *outs):
    side = x0_ref.shape[0]
    wide = raw_ref.shape[1]
    grad_qkv = mm_tn(x0_ref[...], raw_ref[:side]) + mm_tn(x1_ref[...], raw_ref[side:])
    grad_o = mm_tn(g0_ref[...], mixed_ref[:side]) + mm_tn(g1_ref[...], mixed_ref[side:])
    for p in range(4):

        @pl.when(pl.program_id(0) == p)
        def _():
            outs[p][:, :wide] = grad_qkv.astype(BF)
            outs[p][:, wide:] = grad_o.astype(BF)


def attn_grad_call(x, g, raw, mixed):
    count, d_model = x[0].shape
    part = d_model // 4
    shape = (part, raw.shape[1] + mixed.shape[1])
    columns = pl.BlockSpec((count, part), lambda i: (0, i))
    return pl.pallas_call(
        attn_grad_kernel,
        grid=(4,),
        in_specs=[columns] * 4 + [pl.BlockSpec(a.shape, lambda i: (0, 0)) for a in (raw, mixed)],
        out_specs=[pl.BlockSpec(shape, lambda i: (0, 0))] * 4,
        out_shape=[jax.ShapeDtypeStruct(shape, BF)] * 4,
        compiler_params=pltpu.CompilerParams(vmem_limit_bytes=VMEM_BYTES),
        cost_estimate=SMALL_COST,
        name="attn_grad",
    )(*x, *g, raw, mixed)


def merge_kernel(place_ref, near_a, near_b, got_a, got_b, opposite, *outs):
    height, width = outs[0].shape[0], near_a.shape[1]
    for d, out_ref in enumerate(outs):
        at = pl.ds(pl.multiple_of((place_ref[0] ^ d) * height, height), height)
        for near, got, start in ((near_a, got_a, 0), (near_b, got_b, width)):
            total = near[at, :].astype(F32) + got[at, :].astype(F32)
            total = total + opposite[at, start : start + width].astype(F32)
            out_ref[:, start : start + width] = total.astype(BF)


def merge_call(place, places, *arrays):
    rows, width = arrays[0].shape
    shape = jax.ShapeDtypeStruct((rows // places, 2 * width), BF)
    vmem = pl.BlockSpec(memory_space=pltpu.VMEM)
    return pl.pallas_call(
        merge_kernel,
        in_specs=[pl.BlockSpec(memory_space=pltpu.SMEM)] + [vmem] * 5,
        out_specs=[vmem] * places,
        out_shape=[shape] * places,
        compiler_params=pltpu.CompilerParams(vmem_limit_bytes=VMEM_BYTES),
        cost_estimate=SMALL_COST,
        name="merge",
    )(place, *arrays)


def final_kernel(
    qw, fw, place_ref, got_ref, p0_ref, p1_ref, p2_ref, p3_ref, wq_ref, wk_ref, wv_ref, wg_ref, wu_ref,
    q_ref, k_ref, v_ref, o_ref, gate_ref, up_ref, down_ref, sum_ref,
):
    places = got_ref.shape[0]

    def side_by_side(start, width):
        return jnp.concatenate(
            [got_ref[p, :, start : start + width] for p in range(places)], 1
        ).astype(F32)

    def rows(weight_ref, grad):
        return jnp.sum(weight_ref[...].astype(F32) * grad, 1, keepdims=True)

    query, key, value = side_by_side(0, qw), side_by_side(qw, HEAD_DIM), side_by_side(qw + HEAD_DIM, HEAD_DIM)
    q_ref[...], k_ref[...], v_ref[...] = query, key, value
    sum_attn = rows(wq_ref, query) + rows(wk_ref, key) + rows(wv_ref, value)
    start = qw + 2 * HEAD_DIM
    o_ref[...] = side_by_side(start, qw)
    pieces = in_order([r[...].astype(F32) for r in (p0_ref, p1_ref, p2_ref, p3_ref)], place_ref[0])
    gate, up, down = (
        jnp.concatenate([p[:, n * fw : (n + 1) * fw] for p in pieces], 1) for n in range(3)
    )
    gate_ref[...], up_ref[...] = gate, up
    sum_ffn = rows(wg_ref, gate) + rows(wu_ref, up)
    down_ref[...] = down
    lane = lanes(sum_ref.shape)
    sum_ref[...] = jnp.where(lane == 0, sum_attn, sum_ffn)


def final_call(qw, fw, place, got, pieces, wq, wk, wv, wg, wu):
    shard = got.shape[1]
    vmem = pl.BlockSpec(memory_space=pltpu.VMEM)
    shapes = [wq.shape, wk.shape, wv.shape, wq.shape, wg.shape, wu.shape, wg.shape]
    shapes.append((shard, LANES))
    return pl.pallas_call(
        functools.partial(final_kernel, qw, fw),
        in_specs=[pl.BlockSpec(memory_space=pltpu.SMEM)] + [vmem] * 10,
        out_specs=[vmem] * 8,
        out_shape=[jax.ShapeDtypeStruct(s, F32) for s in shapes],
        compiler_params=pltpu.CompilerParams(vmem_limit_bytes=VMEM_BYTES),
        cost_estimate=SMALL_COST,
        name="final",
    )(place, got, *pieces, wq, wk, wv, wg, wu)


def body(
    hidden_in,
    lengths,
    positions,
    attn_gain,
    w_query,
    w_key,
    w_value,
    q_gain,
    k_gain,
    w_output,
    ffn_gain,
    w_gate,
    w_up,
    w_down,
    grad_out,
):
    H, B, J, T = (lax.axis_size(a) for a in ("h", "b", "j", "tp"))
    ix, ih, ib, ij, it = (lax.axis_index(a) for a in ("dp", "h", "b", "j", "tp"))
    rows = hidden_in.shape[2]
    d_model = hidden_in.shape[3]
    shard = w_query.shape[0]
    group = HEADS // KV_HEADS
    qw = group * HEAD_DIM
    fw = w_gate.shape[1] // J
    count = T * J * rows
    side = J * rows
    ffn_width = -(-3 * fw // (2 * LANES)) * LANES
    score_scale = HEAD_DIM ** (-0.5)
    quarter = 2 * ix + ih
    part = d_model // 4

    def cut(array, p, width):
        return array[:, p * width : (p + 1) * width]

    def exchange(name, pieces):
        with jax.named_scope(name):
            return lax.all_to_all(pieces, "j", 0, 0)

    def exchange_beside(name, pieces):
        with jax.named_scope(name):
            pieces = in_order(pieces, ij)
            parts = [pieces[0]]
            for d in range(1, J):
                parts.append(lax.ppermute(pieces[d], "j", [(i, i ^ d) for i in range(J)]))
            return parts

    def two_numbers(values):
        high = values.astype(BF)
        low = (values - high.astype(F32)).astype(BF)
        return jnp.pad(jnp.concatenate([high, low], 0), ((0, 6), (0, 0)))

    def one_number(block):
        return block[..., 0:1, :].astype(F32) + block[..., 1:2, :].astype(F32)

    def relative(array):
        pieces = [array[..., p * part : (p + 1) * part] for p in range(4)]
        return jnp.concatenate(in_order(pieces, quarter), -1)

    turn = [(0, 0), (1, 2), (2, 1), (3, 3)]

    def fetch(name, array, *others):
        with jax.named_scope(name):
            mine = lax.dynamic_index_in_dim(array, it, 0, keepdims=False)[0]
            if others:
                mine = after(mine, *others)
            return lax.ppermute(mine, ("h", "tp"), turn)

    def give_back(name, block):
        with jax.named_scope(name):
            mine = lax.ppermute(block, ("h", "tp"), turn)
            both = in_order([mine, swap(mine, "tp")], it)
            return [jnp.stack([b[n] for b in both])[:, None] for n in range(block.shape[0])]

    def gather_half(name, block, *others):
        with jax.named_scope(name):
            sent = jnp.broadcast_to(block[None], (J, *block.shape))
            if others:
                sent = after(sent, *others)
            return lax.all_to_all(sent, "j", 0, 0).reshape(side, d_model)

    def sum_tokens(name, half, *others):
        with jax.named_scope(name):
            got = lax.all_to_all(half.reshape(J, rows, d_model), "j", 0, 0)
            if others:
                got = after(got, *others)
            return jnp.sum(got.astype(F32), 0)

    w_output_t = w_output.T
    w_down_t = w_down.T
    wide = 2 * qw + 2 * HEAD_DIM
    pos = positions[:, 0].reshape(1, H * rows)
    high = pos // 256
    extra = [jnp.concatenate([attn_gain, ffn_gain])[None], high.astype(BF), (pos - high * 256).astype(BF)]
    extra = [jnp.pad(e, ((0, 0), (0, wide - e.shape[1]))) for e in extra]
    extra = jnp.pad(jnp.concatenate(extra, 0), ((0, 5), (0, 0)))
    pack = [
        jnp.concatenate(
            [
                jnp.concatenate(
                    [
                        cut(w_query, p, qw),
                        cut(w_key, p, HEAD_DIM),
                        cut(w_value, p, HEAD_DIM),
                        cut(w_output_t, p, qw),
                    ],
                    1,
                ),
                extra,
            ],
            0,
        )
        for p in range(J)
    ]
    own = exchange("weights_attn", jnp.stack(pack))
    pack = [
        jnp.pad(
            jnp.concatenate([cut(w_gate, p, fw), cut(w_up, p, fw), cut(w_down_t, p, fw)], 1),
            ((0, 0), (0, 2 * ffn_width - 3 * fw)),
        )
        for p in range(J)
    ]
    ffn_own = exchange("weights_ffn", jnp.stack(pack))
    hidden_own = relative(fetch("fetch_hidden", hidden_in))

    def share(name, block):
        with jax.named_scope(name):
            return [block] + [
                lax.ppermute(block, "j", [(i, i ^ d) for i in range(J)]) for d in range(1, J)
            ]

    with jax.named_scope("weights_attn"):
        if B > 1:
            own = lax.all_gather(own, "b", axis=0, tiled=True)
        beside = swap(own, "h")
        opposite = swap(own, "dp")
    half = gather_half("tokens_hidden", hidden_own, ffn_own, beside)
    with jax.named_scope("weights_attn"):
        across = swap(beside, "dp")
    cot_own = relative(fetch("fetch_cot", grad_out, beside))
    with jax.named_scope("weights_attn"):
        parts = [own, beside, opposite, across]
        wa = jnp.stack([p[:, :shard] for p in parts]).reshape(d_model, wide)
        extra = jnp.stack([p[:, shard : shard + 3] for p in parts])
    gains = extra[:, :, 0, : 2 * shard].reshape(4, B * J, 2, shard)
    gains = gains.transpose(2, 0, 1, 3).reshape(2, d_model).astype(F32)
    gain_attn = gains[0]
    gain_ffn = gains[1]
    pos = extra[:2, :, 1:, : H * rows].astype(F32)
    pos = pos[:, :, 0] * 256.0 + pos[:, :, 1]
    pos = lax.dynamic_index_in_dim(pos.reshape(H, B, J, H, rows), ib, 1, keepdims=False)
    pos = jnp.where(ih == 0, pos[:, :, 0], pos[:, :, 1])
    pos = jnp.stack(in_order([pos[0], pos[1]], ih ^ it), 0)
    pos_all = pos.reshape(count)

    place = jnp.arange(T * J, dtype=jnp.int32)
    block_of = (it ^ (place // J)) * (B * J) + place % J
    row_of = jnp.arange(rows, dtype=jnp.int32)
    query_index = ((block_of + ib * J)[:, None] * rows + row_of[None, :]).reshape(count)
    key_index = (
        (block_of[None, :] + jnp.arange(B, dtype=jnp.int32)[:, None] * J)[..., None] * rows + row_of
    ).reshape(B * count)

    inverse = 1.0 / ROPE_BASE ** (jnp.arange(0, HEAD_DIM, 2, dtype=F32) / HEAD_DIM)
    if B == 1:
        inverse = jnp.tile(inverse, 2 * LANES // HEAD_DIM)
    angles = pos_all[:, None] * inverse[None, :]
    cosine = jnp.cos(angles)
    sine = jnp.sin(angles)

    half = after(half, wa, gains, cosine, sine, cot_own)
    with jax.named_scope("weights_ffn"):
        ffn_own = ffn_own.reshape(J * shard, 2 * ffn_width)
        if B > 1:
            ffn_own = lax.all_gather(ffn_own, "b", axis=0, tiled=True)
        w_a = [ffn_own[:, :ffn_width]]
        w_b = [ffn_own[:, ffn_width:]]
        w_a.append(swap(after(w_a[0], half), "h"))
        w_b.append(swap(after(w_b[0], w_a[1]), "h"))
        w_own = swap(after(ffn_own, half), "dp")
    with jax.named_scope("tokens_hidden"):
        hidden = [half, swap(half, "tp")]
    stream = hidden_own.astype(F32)
    valid_length = lax.dynamic_index_in_dim(lengths[:, 0], ih, 0, keepdims=False)

    attn_factor = norm_scale(stream)
    if B == 1:
        at = jnp.stack([valid_length, it])
        ones = jnp.ones((HEAD_DIM,), F32)
        qk_gain = jnp.stack(
            [jnp.concatenate([q_gain, q_gain]).astype(F32), jnp.concatenate([k_gain.astype(F32), ones])]
        )
        *normed, raw, qkv = qkv_call(*hidden, gain_attn[None], wa, qk_gain, cosine, sine)
        mixed, probs = attend_call(at, qkv)
    else:
        hidden = jnp.concatenate(hidden, 0).astype(F32)
        normed = (hidden * norm_scale(hidden) * gain_attn).astype(BF)
        cosine = jnp.concatenate([cosine, cosine], -1)[:, None, :]
        sine = jnp.concatenate([sine, sine], -1)[:, None, :]
        raw = mm(normed, wa[:, : qw + 2 * HEAD_DIM])
        normed = [normed[:side], normed[side:]]
        qk_raw = raw[:, : qw + HEAD_DIM].reshape(count, group + 1, HEAD_DIM)
        qk_gain = jnp.stack([q_gain] * group + [k_gain]).astype(F32)
        qk_factor = norm_scale(qk_raw)
        qk_normed = qk_raw * qk_factor * qk_gain
        qk = (qk_normed * cosine + half_turn(qk_normed) * sine).astype(BF)
        queries = qk[:, :group].transpose(1, 0, 2)
        keys = qk[:, group]
        values = raw[:, qw + HEAD_DIM :].astype(BF)
        if B > 1:
            keys = lax.all_gather(keys, "b", axis=0, tiled=True)
            values = lax.all_gather(values, "b", axis=0, tiled=True)
        visible = (key_index[None, :] <= query_index[:, None]) & (key_index[None, :] < valid_length)

        def scores_of(query_head):
            return jnp.where(visible, mm_nt(query_head, keys) * score_scale, MASKED)

        def attend(query_head):
            scores = scores_of(query_head)
            row_max = jnp.max(scores, -1, keepdims=True)
            exp_scores = jnp.exp(scores - row_max)
            row_total = jnp.sum(exp_scores, -1, keepdims=True)
            probs = (exp_scores / row_total).astype(BF)
            return mm(probs, values).astype(BF), row_max + jnp.log(row_total)

        heads = [attend(queries[g]) for g in range(group)]
        mixed = jnp.concatenate([h[0] for h in heads], -1)
    parts = share("tokens_cot", after(cot_own, half))
    mixed = after(mixed, w_a[1], w_own, *parts[1:])
    with jax.named_scope("tokens_cot"):
        cot_half = jnp.concatenate(in_order(parts, ij), 0)
    with jax.named_scope("sum_attn"):
        wo = wa[:, qw + 2 * HEAD_DIM :]
        low = swap(mm_nt(mixed[side:], wo).astype(BF), "tp")
        low = add(mm_nt(mixed[:side], wo), low)
        w_a.append(swap(w_a[1], "dp"))
        attn_branch = sum_tokens("sum_attn", low, w_b[1], w_a[2])

    middle = stream + attn_branch
    ffn_factor = norm_scale(middle)
    xf_own = (middle * ffn_factor * gain_ffn).astype(BF)
    ffn_half = gather_half("tokens_xf", xf_own)
    with jax.named_scope("weights_ffn"):
        w_b.append(swap(w_b[1], "dp"))
    ffn_half = after(ffn_half, w_b[2])
    ffn_in = [ffn_half, swap(ffn_half, "tp")]
    cot = [cot_half, swap(cot_half, "tp")]
    hidden_act, grad_pre, grad_in, branch = zip(
        *[ffn_call(fw, ffn_in[i], cot[i], w_a, w_b, w_own) for i in range(2)]
    )
    low = swap(grad_in[1], "tp")
    opposite, across_a, across_b = ffn_grad_call(
        2, ffn_width, True, ffn_in, cot, grad_pre, hidden_act
    )
    low = add(grad_in[0], after(low, across_b))
    with jax.named_scope("grads_ffn"):
        got_b, got_a = swap(across_b, "dp"), swap(across_a, "dp")
    near_a, near_b, beside_a, beside_b = ffn_grad_call(
        0, ffn_width, False, ffn_in, cot, grad_pre, hidden_act
    )
    grad_ffn_in = sum_tokens("sum_dxf", low, got_b, near_a)

    grad_middle = cot_own.astype(F32) + norm_back(middle, ffn_factor, gain_ffn, grad_ffn_in)
    with jax.named_scope("grads_ffn"):
        beside_b = add(beside_b, got_b)
    half = gather_half("tokens_dattn", grad_middle.astype(BF), beside_b)
    with jax.named_scope("sum_out"):
        low = add(branch[0], swap(after(branch[1], grad_ffn_in), "tp"))
    with jax.named_scope("grads_ffn"):
        got_b = swap(beside_b, "h")
        beside_a = add(beside_a, got_a)
        half = after(half, low, got_b, beside_a)
        got_a = swap(beside_a, "h")
        opposite = swap(after(opposite, beside_a), "dp")
    grad_attn = [half, swap(half, "tp")]
    with jax.named_scope("sum_out"):
        low = after(low, half).reshape(J, rows, d_model)
        parts = lax.all_to_all(low, "j", 0, 0)
    if B == 1:
        grad_raw, totals = attend_back_call(
            at, qkv, mixed, probs, raw, *grad_attn, wo, qk_gain, cosine, sine
        )
        totals = jnp.concatenate([totals[0, :HEAD_DIM] + totals[0, HEAD_DIM:], totals[1, :HEAD_DIM]])
    else:
        grad_mixed = mm(jnp.concatenate(grad_attn, 0), wo).astype(BF)
        grad_keys = jnp.zeros((B * count, HEAD_DIM), F32)
        grad_values = jnp.zeros((B * count, HEAD_DIM), F32)
        grad_queries = []
        for g in range(group):
            probs = jnp.exp(scores_of(queries[g]) - heads[g][1])
            grad_head = grad_mixed[:, g * HEAD_DIM : (g + 1) * HEAD_DIM]
            grad_probs = mm_nt(grad_head, values)
            row_delta = jnp.sum(grad_probs * probs, -1, keepdims=True)
            grad_scores = (probs * (grad_probs - row_delta)).astype(BF)
            grad_queries.append(mm(grad_scores, keys) * score_scale)
            grad_keys = grad_keys + mm_tn(grad_scores, queries[g]) * score_scale
            grad_values = grad_values + mm_tn(probs.astype(BF), grad_head)
        if B > 1:
            grad_keys = lax.psum_scatter(grad_keys, "b", scatter_dimension=0, tiled=True)
            grad_values = lax.psum_scatter(grad_values, "b", scatter_dimension=0, tiled=True)
        grad_rot = jnp.stack(grad_queries + [grad_keys], 1)
        grad_normed = grad_rot * cosine + half_turn_back(grad_rot * sine)
        grad_qk_raw = norm_back(qk_raw, qk_factor, qk_gain, grad_normed)
        terms = jnp.sum(grad_normed * qk_raw * qk_factor, 0)
        totals = jnp.concatenate([jnp.sum(terms[:group], 0), terms[group]])
        grad_raw = jnp.concatenate(
            [grad_qk_raw.reshape(count, qw + HEAD_DIM), grad_values], 1
        ).astype(BF)
    w_qkv = wa[:, : qw + 2 * HEAD_DIM]
    grad_raw = after(grad_raw, parts, got_a, opposite)
    low = swap(mm_nt(grad_raw[side:], w_qkv).astype(BF), "tp")
    grads_attn = attn_grad_call(normed, grad_attn, grad_raw, mixed)
    low = add(mm_nt(grad_raw[:side], w_qkv), after(low, *grads_attn[2:]))
    grad_normed_own = sum_tokens("sum_dxa", low)
    total = jnp.sum(after(parts, low).astype(F32), 0)
    out_own = relative((middle + total).astype(BF))
    with jax.named_scope("grads_ffn"):
        pieces = [near_a, near_b, got_a, got_b, opposite]
        if B == 1:
            pieces = list(merge_call(ij[None], J, after(near_a, low), *pieces[1:]))
        else:
            near = jnp.concatenate([add(near_a, got_a), add(near_b, got_b)], 1)
            near = lax.psum_scatter(add(near, opposite), "b", scatter_dimension=0, tiled=True)
            near = near.reshape(J, shard, 2 * ffn_width)
            pieces = [lax.dynamic_index_in_dim(near, ij ^ d, 0, keepdims=False) for d in range(J)]
        for d in range(1, J):
            pieces[d] = lax.ppermute(pieces[d], "j", [(i, i ^ d) for i in range(J)])
    grad_stream = grad_middle + norm_back(stream, attn_factor, gain_attn, grad_normed_own)
    sent = jnp.stack([out_own, relative(grad_stream.astype(BF))])
    out_hidden, grad_hidden = give_back("return", sent)
    with jax.named_scope("grads_attn"):
        totals = jnp.pad(totals[None], ((0, 0), (0, wide - 2 * HEAD_DIM)))
        near, beside, opposed, across = grads_attn
        got = swap(jnp.concatenate([across, two_numbers(totals)], 0), "dp")
        got_near = swap(opposed, "dp")
        got = after(got, low)
        totals = totals + one_number(got[part:])
        beside = jnp.concatenate([add(beside, got[:part]), two_numbers(totals)], 0)
        got = swap(beside, "h")
        totals = totals + one_number(got[part:])
    with jax.named_scope("grads"):
        got = after(got, grad_normed_own)
        near = add(near.astype(F32) + got_near.astype(F32), got[:part])
        extra = two_numbers(totals[:, :LANES])
        extra = jnp.pad(extra, ((0, shard - extra.shape[0]), (0, 0)))
        extra = jnp.broadcast_to(extra[None], (B * J, shard, LANES))
        near = jnp.concatenate([near.reshape(B * J, shard, near.shape[1]), extra], 2)
        if B > 1:
            near = lax.psum_scatter(near, "b", scatter_dimension=0, tiled=True)
        shards = lax.all_to_all(near, "j", 0, 0)
    totals = jnp.sum(one_number(shards[:, :, -LANES:]), (0, 1))
    *shard_grads, sums = final_call(qw, fw, ij[None], shards, pieces, w_query, w_key, w_value, w_gate, w_up)

    sums = jnp.concatenate([totals, sums[:, 0], sums[:, 1]])
    sums = sums + swap(sums, "tp")
    totals = sums[: 2 * HEAD_DIM].reshape(2, HEAD_DIM)
    sums = sums[2 * HEAD_DIM :].reshape(2, shard) / jnp.stack([attn_gain, ffn_gain]).astype(F32)

    shard_query, shard_key, shard_value, shard_output, shard_gate, shard_up, shard_down = shard_grads
    return (
        out_hidden,
        grad_hidden,
        sums[0],
        shard_query,
        shard_key,
        shard_value,
        totals[0],
        totals[1],
        shard_output.T,
        sums[1],
        shard_gate,
        shard_up,
        shard_down.T,
    )


def solution(mesh):
    places = KV_HEADS // mesh.shape["tp"]

    def run(*args):
        micro = args[0].shape[0]
        shape = (mesh.shape["dp"], micro, mesh.shape["ctx"] // (micro * places), places)
        fine = Mesh(
            mesh.devices.reshape(*shape, mesh.shape["tp"]), ("dp", "h", "b", "j", "tp")
        )
        ctx = ("h", "b", "j")
        rows = ("dp", "h", "b", "j")
        tokens = P(None, "dp", ctx, None)
        return jax.shard_map(
            body,
            mesh=fine,
            in_specs=(
                tokens,
                P(None, "dp"),
                P(None, "dp", ctx),
                P(rows),
                P(rows, "tp"),
                P(rows, "tp"),
                P(rows, "tp"),
                P(),
                P(),
                P("tp", rows),
                P(rows),
                P(rows, "tp"),
                P(rows, "tp"),
                P("tp", rows),
                tokens,
            ),
            out_specs=(
                tokens,
                tokens,
                P(rows),
                P(rows, "tp"),
                P(rows, "tp"),
                P(rows, "tp"),
                P(),
                P(),
                P("tp", rows),
                P(rows),
                P(rows, "tp"),
                P(rows, "tp"),
                P("tp", rows),
            ),
            check_vma=False,
        )(*args)

    return run
```

```python
import functools

import jax
import jax.numpy as jnp
from jax import lax
from jax.experimental import pallas as pl
from jax.experimental.pallas import tpu as pltpu
from jax.sharding import Mesh, PartitionSpec as P

HEADS = 16
KV_HEADS = 8
HEAD_DIM = 64
EPSILON = 1e-05
ROPE_BASE = 1000000.0
MASKED = -1e30
BF = jnp.bfloat16
F32 = jnp.float32
VMEM_BYTES = 60 * 2**20
LANES = 128
SMALL_COST = pl.CostEstimate(flops=1, bytes_accessed=1, transcendentals=0)


def dot(a, b, dims):
    return lax.dot_general(a, b, (dims, ((), ())), preferred_element_type=F32)


def mm(a, b):
    return dot(a, b, ((1,), (0,)))


def mm_nt(a, b):
    return dot(a, b, ((1,), (1,)))


def mm_tn(a, b):
    return dot(a, b, ((0,), (0,)))


def nothing(*refs):
    pass


def after(value, *others):
    anywhere = pl.BlockSpec(memory_space=pl.ANY)
    return pl.pallas_call(
        nothing,
        in_specs=[anywhere] * (1 + len(others)),
        out_specs=anywhere,
        out_shape=jax.ShapeDtypeStruct(value.shape, value.dtype),
        input_output_aliases={0: 0},
        cost_estimate=SMALL_COST,
        name="after",
    )(value, *others)


def swap(v, axis):
    return lax.ppermute(v, axis, [(0, 1), (1, 0)])


def add(a, b):
    return (a.astype(F32) + b.astype(F32)).astype(BF)


def norm_scale(vector):
    return lax.rsqrt(jnp.mean(vector * vector, -1, keepdims=True) + EPSILON)


def norm_back(vector, factor, gain, upstream):
    weighted = upstream * gain
    return factor * weighted - vector * factor * factor * factor * jnp.mean(
        vector * weighted, -1, keepdims=True
    )


def half_turn(vector):
    middle_index = vector.shape[-1] // 2
    return jnp.concatenate([-vector[..., middle_index:], vector[..., :middle_index]], -1)


def half_turn_back(vector):
    middle_index = vector.shape[-1] // 2
    return jnp.concatenate([vector[..., middle_index:], -vector[..., :middle_index]], -1)


def in_order(parts, index):
    bit = 1
    while bit < len(parts):
        flag = (index & bit) != 0
        parts = [jnp.where(flag, parts[i ^ bit], parts[i]) for i in range(len(parts))]
        bit *= 2
    return parts


def row_sums(square, low):
    left = jnp.sum(jnp.where(low, square, 0.0), -1, keepdims=True)
    right = jnp.sum(jnp.where(low, 0.0, square), -1, keepdims=True)
    return jnp.where(low, left, right)


def pair_scale(pair, low):
    return lax.rsqrt(row_sums(pair * pair, low) * (1.0 / HEAD_DIM) + EPSILON)


def lanes(shape):
    return lax.broadcasted_iota(jnp.int32, shape, 1)


def turned(pair, first):
    width = pair.shape[1]
    quarter = HEAD_DIM // 2
    return jnp.where(first, pltpu.roll(pair, width - quarter, 1), pltpu.roll(pair, quarter, 1))


def qkv_kernel(half_tiles, h0_ref, h1_ref, gain_ref, w_ref, qk_gain_ref, cos_ref, sin_ref,
               xa0_ref, xa1_ref, raw_ref, qkv_ref):
    def run(h_ref, xa_ref):
        hidden = h_ref[...].astype(F32)
        factor = lax.rsqrt(jnp.mean(hidden * hidden, -1, keepdims=True) + EPSILON)
        xa = (hidden * factor * gain_ref[...]).astype(BF)
        xa_ref[...] = xa
        raw = mm(xa, w_ref[:, :256])
        raw_ref[...] = raw
        lane = lanes((raw.shape[0], 128))
        low = lane < HEAD_DIM
        first = lane % HEAD_DIM < HEAD_DIM // 2
        cosine, sine = cos_ref[...], sin_ref[...]
        sine = jnp.where(first, -sine, sine)
        for p in range(2):
            pair = raw[:, 128 * p : 128 * (p + 1)]
            normed = pair * pair_scale(pair, low) * qk_gain_ref[p : p + 1, :]
            turned_pair = normed * cosine + turned(normed, first) * sine
            if p == 1:
                turned_pair = jnp.where(low, turned_pair, pair)
            qkv_ref[:, 128 * p : 128 * (p + 1)] = turned_pair.astype(BF)

    @pl.when(pl.program_id(0) < half_tiles)
    def _():
        run(h0_ref, xa0_ref)

    @pl.when(pl.program_id(0) >= half_tiles)
    def _():
        run(h1_ref, xa1_ref)


def qkv_call(h0, h1, gain, w, qk_gain, cosine, sine):
    half, d_model = h0.shape
    tile = min(256, half)
    n = half // tile
    own = pl.BlockSpec((tile, d_model), lambda i: (jnp.minimum(i, n - 1), 0))
    other = pl.BlockSpec((tile, d_model), lambda i: (jnp.maximum(i - n, 0), 0))
    def fixed(a):
        return pl.BlockSpec(a.shape, lambda i: (0, 0))
    def rows(width):
        return pl.BlockSpec((tile, width), lambda i: (i, 0))
    return pl.pallas_call(
        functools.partial(qkv_kernel, n),
        grid=(2 * n,),
        in_specs=[own, other, fixed(gain), fixed(w), fixed(qk_gain), rows(128), rows(128)],
        out_specs=[own, other, rows(256), rows(256)],
        out_shape=[
            jax.ShapeDtypeStruct(h0.shape, BF),
            jax.ShapeDtypeStruct(h0.shape, BF),
            jax.ShapeDtypeStruct((2 * half, 256), F32),
            jax.ShapeDtypeStruct((2 * half, 256), BF),
        ],
        compiler_params=pltpu.CompilerParams(vmem_limit_bytes=VMEM_BYTES),
        cost_estimate=SMALL_COST,
        name="qkv",
    )(h0, h1, gain, w, qk_gain, cosine, sine)


def blocks_of(tiles):
    return [(a, k) for a in range(tiles) for k in range(a + 1)]


def stacked(pair):
    return jnp.concatenate([pair[:, :HEAD_DIM], pair[:, HEAD_DIM:]], 0)


def attend_kernel(tile, tiles, at_ref, qkv_ref, mixed_ref, probs_ref):
    half = tiles // 2
    def place(t):
        return pl.multiple_of((t + half * at_ref[1]) % tiles * tile, tile)
    for a in range(tiles):
        query = stacked(qkv_ref[pl.ds(place(a), tile), :128])
        row = lax.broadcasted_iota(jnp.int32, (2 * tile, 1), 0) % tile + a * tile
        limit = jnp.minimum(row + 1, at_ref[0])
        scores = []
        for k in range(a + 1):
            key = qkv_ref[pl.ds(place(k), tile), 128 : 128 + HEAD_DIM]
            column = lax.broadcasted_iota(jnp.int32, (1, tile), 1) + k * tile
            scores.append(
                jnp.where(column < limit, mm_nt(query, key) * HEAD_DIM ** (-0.5), MASKED)
            )
        peak = functools.reduce(jnp.maximum, [jnp.max(s, -1, keepdims=True) for s in scores])
        exps = [jnp.exp(s - peak) for s in scores]
        total = functools.reduce(jnp.add, [jnp.sum(e, -1, keepdims=True) for e in exps])
        inverse = 1.0 / total
        mixed = 0.0
        for k in range(a + 1):
            probs = (exps[k] * inverse).astype(BF)
            probs_ref[blocks_of(tiles).index((a, k))] = probs
            value = qkv_ref[pl.ds(place(k), tile), 128 + HEAD_DIM :]
            mixed = mixed + mm(probs, value)
        mixed_ref[pl.ds(place(a), tile), :] = jnp.concatenate(
            [mixed[:tile], mixed[tile:]], 1
        ).astype(BF)


def attend_call(at, qkv):
    count = qkv.shape[0]
    tile = min(256, count // 2)
    tiles = count // tile
    pairs = len(blocks_of(tiles))
    return pl.pallas_call(
        functools.partial(attend_kernel, tile, tiles),
        in_specs=[pl.BlockSpec(memory_space=pltpu.SMEM), pl.BlockSpec(memory_space=pltpu.VMEM)],
        out_specs=[pl.BlockSpec(memory_space=pltpu.VMEM)] * 2,
        out_shape=[
            jax.ShapeDtypeStruct((count, 128), BF),
            jax.ShapeDtypeStruct((pairs, 2 * tile, tile), BF),
        ],
        compiler_params=pltpu.CompilerParams(vmem_limit_bytes=VMEM_BYTES),
        cost_estimate=SMALL_COST,
        name="attend",
    )(at, qkv)


def attend_back_kernel(tile, tiles, at_ref, qkv_ref, mixed_ref, probs_ref, raw_ref, g0_ref, g1_ref,
                       wa_ref, qk_gain_ref, cos_ref, sin_ref, out_ref, total_ref, give0_ref,
                       give1_ref, keep_ref, dm_ref, dkv_ref):
    half = tiles // 2
    def place(t):
        return pl.multiple_of((t + half * at_ref[1]) % tiles * tile, tile)
    rows = half * tile
    wide = out_ref.shape[1]
    dm_ref[:rows] = mm(g0_ref[...], wa_ref[:, wide:]).astype(BF)
    dm_ref[rows:] = mm(g1_ref[...], wa_ref[:, wide:]).astype(BF)
    scale = HEAD_DIM ** (-0.5)
    lane = lanes((tile, 128))
    low = lane < HEAD_DIM
    first = lane % HEAD_DIM < HEAD_DIM // 2

    def finish(t, p, grad):
        at = pl.ds(place(t), tile)
        cosine, sine = cos_ref[at], sin_ref[at]
        pair = raw_ref[at, 128 * p : 128 * (p + 1)]
        factor = pair_scale(pair, low)
        signed = grad * jnp.where(first, -sine, sine)
        upstream = grad * cosine + turned(signed, first)
        gain = qk_gain_ref[p : p + 1, :]
        weighted = upstream * gain
        mean = row_sums(pair * weighted, low) * (1.0 / HEAD_DIM)
        result = factor * weighted - pair * (factor * factor * factor * mean)
        terms = jnp.sum(upstream * pair * factor, 0, keepdims=True)
        if p == 1:
            result = jnp.where(low, result, grad)
        out_ref[at, 128 * p : 128 * (p + 1)] = result.astype(BF)
        total_ref[p : p + 1, :] += terms

    total_ref[...] = jnp.zeros_like(total_ref)
    dkv = [0.0] * tiles
    for a in range(tiles):
        at = pl.ds(place(a), tile)
        query = stacked(qkv_ref[at, :128])
        grad = stacked(dm_ref[at])
        mixed = stacked(mixed_ref[at, :])
        delta = jnp.sum(grad.astype(F32) * mixed.astype(F32), -1, keepdims=True)
        grad_query = 0.0
        for k in range(a + 1):
            keys = pl.ds(place(k), tile)
            key = qkv_ref[keys, 128 : 128 + HEAD_DIM]
            value = qkv_ref[keys, 128 + HEAD_DIM :]
            probs = probs_ref[blocks_of(tiles).index((a, k))]
            grad_scores = (probs.astype(F32) * (mm_nt(grad, value) - delta)).astype(BF)
            grad_query = grad_query + mm(grad_scores, key)
            grad_kv = jnp.concatenate(
                [mm_tn(grad_scores, query) * scale, mm_tn(probs, grad)], 1
            )
            if a == k:
                dkv_ref[k] = grad_kv
            else:
                dkv_ref[k] += grad_kv
        grad_query = grad_query * scale
        finish(a, 0, jnp.concatenate([grad_query[:tile], grad_query[tile:]], 1))
    for k in range(tiles):
        finish(k, 1, dkv_ref[k])
    w = wa_ref[:, :wide]
    middle = rows + rows // 2
    give0_ref[...] = mm_nt(out_ref[rows:middle], w).astype(BF)
    give1_ref[...] = mm_nt(out_ref[middle:], w).astype(BF)
    keep_ref[...] = mm_nt(out_ref[:rows], w).astype(BF)


def attend_back_call(at, qkv, mixed, probs, raw, g0, g1, wa, qk_gain, cosine, sine):
    count, d_model = qkv.shape[0], g0.shape[1]
    tile = min(256, count // 2)
    tiles = count // tile
    vmem = pl.BlockSpec(memory_space=pltpu.VMEM)
    return pl.pallas_call(
        functools.partial(attend_back_kernel, tile, tiles),
        in_specs=[pl.BlockSpec(memory_space=pltpu.SMEM)] + [vmem] * 10,
        out_specs=[vmem] * 5,
        out_shape=[
            jax.ShapeDtypeStruct((count, 256), BF),
            jax.ShapeDtypeStruct((8, 128), F32),
            jax.ShapeDtypeStruct((count // 4, d_model), BF),
            jax.ShapeDtypeStruct((count // 4, d_model), BF),
            jax.ShapeDtypeStruct((count // 2, d_model), BF),
        ],
        scratch_shapes=[pltpu.VMEM((count, 128), BF), pltpu.VMEM((tiles, tile, 128), F32)],
        compiler_params=pltpu.CompilerParams(vmem_limit_bytes=VMEM_BYTES),
        cost_estimate=SMALL_COST,
        name="attend_back",
    )(at, qkv, mixed, probs, raw, g0, g1, wa, qk_gain, cosine, sine)


def ffn_kernel(fw, part, x_ref, cot_ref, *refs):
    a_refs, b_refs, (w_ref, act_ref, grad_ref, grad_in_ref, out_ref) = refs[:3], refs[3:6], refs[6:]
    width = a_refs[0].shape[1]
    a_refs = [*a_refs[:2], w_ref.at[:, :width], a_refs[2]]
    b_refs = [*b_refs[:2], w_ref.at[:, width:], b_refs[2]]
    rest = 2 * fw - width
    pre_a, pre_b, grad_act = 0.0, 0.0, 0.0
    for p in range(4):
        cut = slice(p * part, (p + 1) * part)
        pre_a = pre_a + mm(x_ref[:, cut], a_refs[p][...])
        pre_b = pre_b + mm(x_ref[:, cut], b_refs[p][:, :rest])
        grad_act = grad_act + mm(cot_ref[:, cut], b_refs[p][:, rest : rest + fw])
    pre = jnp.concatenate([pre_a, pre_b], 1)
    gate, up = pre[:, :fw], pre[:, fw:]
    sigmoid = 1.0 / (1.0 + jnp.exp(-gate))
    silu = gate * sigmoid
    act = (silu * up).astype(BF)
    act_ref[...] = act
    grad_gate = grad_act * up * sigmoid * (1.0 + gate * (1.0 - sigmoid))
    grad = jnp.concatenate([grad_gate, grad_act * silu], 1).astype(BF)
    grad_ref[...] = grad
    for p in range(4):
        cut = slice(p * part, (p + 1) * part)
        grad_in = mm_nt(grad[:, :width], a_refs[p][...])
        grad_in = grad_in + mm_nt(grad[:, width:], b_refs[p][:, :rest])
        grad_in_ref[:, cut] = grad_in.astype(BF)
        out_ref[:, cut] = mm_nt(act, b_refs[p][:, rest : rest + fw]).astype(BF)


def ffn_call(fw, x, cot, w_a, w_b, w_own):
    count, d_model = x.shape
    part = w_a[0].shape[0]
    tile = min(256, count)
    shapes = [(count, fw), (count, 2 * fw), (count, d_model), (count, d_model)]
    return pl.pallas_call(
        functools.partial(ffn_kernel, fw, part),
        grid=(count // tile,),
        in_specs=[
            pl.BlockSpec((tile, d_model), lambda i: (i, 0)),
            pl.BlockSpec((tile, d_model), lambda i: (i, 0)),
        ]
        + [pl.BlockSpec(p.shape, lambda i: (0, 0)) for p in (*w_a, *w_b, w_own)],
        out_specs=[pl.BlockSpec((tile, s[1]), lambda i: (i, 0)) for s in shapes],
        out_shape=[jax.ShapeDtypeStruct(s, BF) for s in shapes],
        compiler_params=pltpu.CompilerParams(vmem_limit_bytes=VMEM_BYTES),
        cost_estimate=SMALL_COST,
        name="ffn",
    )(x, cot, *w_a, *w_b, w_own)


def ffn_grad_kernel(fw, width, whole, *refs):
    ins, outs = refs[:8], refs[8:]
    x0, x1, cot0, cot1, grad0, grad1, act0, act1 = (r[...] for r in ins)
    grad_in = (mm_tn(x0, grad0) + mm_tn(x1, grad1)).astype(BF)
    grad_out = (mm_tn(cot0, act0) + mm_tn(cot1, act1)).astype(BF)
    rest = 2 * fw - width

    def write(a_ref, b_ref):
        a_ref[...] = grad_in[:, :width]
        b_ref[:, :rest] = grad_in[:, width:]
        b_ref[:, rest : rest + fw] = grad_out
        left = width - rest - fw
        if left:
            b_ref[:, rest + fw :] = jnp.zeros((grad_out.shape[0], left), BF)

    @pl.when(pl.program_id(0) == 0)
    def _():
        if whole:
            write(outs[0].at[:, :width], outs[0].at[:, width:])
        else:
            write(*outs[:2])

    @pl.when(pl.program_id(0) == 1)
    def _():
        write(*outs[-2:])


def ffn_grad_call(p, width, whole, x, cot, grad, act):
    count, d_model = x[0].shape
    fw = act[0].shape[1]
    part = d_model // 4
    columns = pl.BlockSpec((count, part), lambda i: (0, p + i))
    operands = [pl.BlockSpec(a.shape, lambda i: (0, 0)) for a in (*grad, *act)]
    shapes = ([(part, 2 * width)] if whole else [(part, width)] * 2) + [(part, width)] * 2
    return pl.pallas_call(
        functools.partial(ffn_grad_kernel, fw, width, whole),
        grid=(2,),
        in_specs=[columns] * 4 + operands,
        out_specs=[pl.BlockSpec(s, lambda i: (0, 0)) for s in shapes],
        out_shape=[jax.ShapeDtypeStruct(s, BF) for s in shapes],
        compiler_params=pltpu.CompilerParams(vmem_limit_bytes=VMEM_BYTES),
        cost_estimate=SMALL_COST,
        name="ffn_grad",
    )(*x, *cot, *grad, *act)


def add_kernel(keep_ref, got0_ref, got1_ref, out_ref):
    rows = got0_ref.shape[0]
    out_ref[:rows] = (keep_ref[:rows].astype(F32) + got0_ref[...].astype(F32)).astype(BF)
    out_ref[rows:] = (keep_ref[rows:].astype(F32) + got1_ref[...].astype(F32)).astype(BF)


def add_call(keep, got0, got1):
    vmem = pl.BlockSpec(memory_space=pltpu.VMEM)
    return pl.pallas_call(
        add_kernel,
        in_specs=[vmem] * 3,
        out_specs=vmem,
        out_shape=jax.ShapeDtypeStruct(keep.shape, BF),
        compiler_params=pltpu.CompilerParams(vmem_limit_bytes=VMEM_BYTES),
        cost_estimate=SMALL_COST,
        name="add",
    )(keep, got0, got1)


def attn_grad_kernel(x0_ref, x1_ref, g0_ref, g1_ref, raw_ref, mixed_ref, *outs):
    side = x0_ref.shape[0]
    wide = raw_ref.shape[1]
    grad_qkv = mm_tn(x0_ref[...], raw_ref[:side]) + mm_tn(x1_ref[...], raw_ref[side:])
    grad_o = mm_tn(g0_ref[...], mixed_ref[:side]) + mm_tn(g1_ref[...], mixed_ref[side:])
    for p in range(4):

        @pl.when(pl.program_id(0) == p)
        def _():
            outs[p][:, :wide] = grad_qkv.astype(BF)
            outs[p][:, wide:] = grad_o.astype(BF)


def attn_grad_call(x, g, raw, mixed):
    count, d_model = x[0].shape
    part = d_model // 4
    shape = (part, raw.shape[1] + mixed.shape[1])
    columns = pl.BlockSpec((count, part), lambda i: (0, i))
    return pl.pallas_call(
        attn_grad_kernel,
        grid=(4,),
        in_specs=[columns] * 4 + [pl.BlockSpec(a.shape, lambda i: (0, 0)) for a in (raw, mixed)],
        out_specs=[pl.BlockSpec(shape, lambda i: (0, 0))] * 4,
        out_shape=[jax.ShapeDtypeStruct(shape, BF)] * 4,
        compiler_params=pltpu.CompilerParams(vmem_limit_bytes=VMEM_BYTES),
        cost_estimate=SMALL_COST,
        name="attn_grad",
    )(*x, *g, raw, mixed)


def merge_kernel(place_ref, near_a, near_b, got_a, got_b, opposite, *outs):
    height, width = outs[0].shape[0], near_a.shape[1]
    for d, out_ref in enumerate(outs):
        at = pl.ds(pl.multiple_of((place_ref[0] ^ d) * height, height), height)
        for near, got, start in ((near_a, got_a, 0), (near_b, got_b, width)):
            total = near[at, :].astype(F32) + got[at, :].astype(F32)
            total = total + opposite[at, start : start + width].astype(F32)
            out_ref[:, start : start + width] = total.astype(BF)


def merge_call(place, places, *arrays):
    rows, width = arrays[0].shape
    shape = jax.ShapeDtypeStruct((rows // places, 2 * width), BF)
    vmem = pl.BlockSpec(memory_space=pltpu.VMEM)
    return pl.pallas_call(
        merge_kernel,
        in_specs=[pl.BlockSpec(memory_space=pltpu.SMEM)] + [vmem] * 5,
        out_specs=[vmem] * places,
        out_shape=[shape] * places,
        compiler_params=pltpu.CompilerParams(vmem_limit_bytes=VMEM_BYTES),
        cost_estimate=SMALL_COST,
        name="merge",
    )(place, *arrays)


def final_kernel(
    qw, fw, place_ref, got_ref, p0_ref, p1_ref, p2_ref, p3_ref, wq_ref, wk_ref, wv_ref, wg_ref, wu_ref,
    q_ref, k_ref, v_ref, o_ref, gate_ref, up_ref, down_ref, sum_ref,
):
    places = got_ref.shape[0]

    def side_by_side(start, width):
        return jnp.concatenate(
            [got_ref[p, :, start : start + width] for p in range(places)], 1
        ).astype(F32)

    def rows(weight_ref, grad):
        return jnp.sum(weight_ref[...].astype(F32) * grad, 1, keepdims=True)

    query, key, value = side_by_side(0, qw), side_by_side(qw, HEAD_DIM), side_by_side(qw + HEAD_DIM, HEAD_DIM)
    q_ref[...], k_ref[...], v_ref[...] = query, key, value
    sum_attn = rows(wq_ref, query) + rows(wk_ref, key) + rows(wv_ref, value)
    start = qw + 2 * HEAD_DIM
    o_ref[...] = side_by_side(start, qw)
    pieces = in_order([r[...].astype(F32) for r in (p0_ref, p1_ref, p2_ref, p3_ref)], place_ref[0])
    gate, up, down = (
        jnp.concatenate([p[:, n * fw : (n + 1) * fw] for p in pieces], 1) for n in range(3)
    )
    gate_ref[...], up_ref[...] = gate, up
    sum_ffn = rows(wg_ref, gate) + rows(wu_ref, up)
    down_ref[...] = down
    lane = lanes(sum_ref.shape)
    sum_ref[...] = jnp.where(lane == 0, sum_attn, sum_ffn)


def final_call(qw, fw, place, got, pieces, wq, wk, wv, wg, wu):
    shard = got.shape[1]
    vmem = pl.BlockSpec(memory_space=pltpu.VMEM)
    shapes = [wq.shape, wk.shape, wv.shape, wq.shape, wg.shape, wu.shape, wg.shape]
    shapes.append((shard, LANES))
    return pl.pallas_call(
        functools.partial(final_kernel, qw, fw),
        in_specs=[pl.BlockSpec(memory_space=pltpu.SMEM)] + [vmem] * 10,
        out_specs=[vmem] * 8,
        out_shape=[jax.ShapeDtypeStruct(s, F32) for s in shapes],
        compiler_params=pltpu.CompilerParams(vmem_limit_bytes=VMEM_BYTES),
        cost_estimate=SMALL_COST,
        name="final",
    )(place, got, *pieces, wq, wk, wv, wg, wu)


def body(
    hidden_in,
    lengths,
    positions,
    attn_gain,
    w_query,
    w_key,
    w_value,
    q_gain,
    k_gain,
    w_output,
    ffn_gain,
    w_gate,
    w_up,
    w_down,
    grad_out,
):
    H, B, J, T = (lax.axis_size(a) for a in ("h", "b", "j", "tp"))
    ix, ih, ib, ij, it = (lax.axis_index(a) for a in ("dp", "h", "b", "j", "tp"))
    rows = hidden_in.shape[2]
    d_model = hidden_in.shape[3]
    shard = w_query.shape[0]
    group = HEADS // KV_HEADS
    qw = group * HEAD_DIM
    fw = w_gate.shape[1] // J
    count = T * J * rows
    side = J * rows
    ffn_width = -(-3 * fw // (2 * LANES)) * LANES
    score_scale = HEAD_DIM ** (-0.5)
    quarter = 2 * ix + ih
    part = d_model // 4

    def cut(array, p, width):
        return array[:, p * width : (p + 1) * width]

    def exchange(name, pieces):
        with jax.named_scope(name):
            return lax.all_to_all(pieces, "j", 0, 0)

    def exchange_beside(name, pieces):
        with jax.named_scope(name):
            pieces = in_order(pieces, ij)
            parts = [pieces[0]]
            for d in range(1, J):
                parts.append(lax.ppermute(pieces[d], "j", [(i, i ^ d) for i in range(J)]))
            return parts

    def two_numbers(values):
        high = values.astype(BF)
        low = (values - high.astype(F32)).astype(BF)
        return jnp.pad(jnp.concatenate([high, low], 0), ((0, 6), (0, 0)))

    def one_number(block):
        return block[..., 0:1, :].astype(F32) + block[..., 1:2, :].astype(F32)

    def relative(array):
        pieces = [array[..., p * part : (p + 1) * part] for p in range(4)]
        return jnp.concatenate(in_order(pieces, quarter), -1)

    turn = [(0, 0), (1, 2), (2, 1), (3, 3)]

    def fetch(name, array, *others):
        with jax.named_scope(name):
            mine = lax.dynamic_index_in_dim(array, it, 0, keepdims=False)[0]
            if others:
                mine = after(mine, *others)
            return lax.ppermute(mine, ("h", "tp"), turn)

    def give_back(name, block):
        with jax.named_scope(name):
            mine = lax.ppermute(block, ("h", "tp"), turn)
            both = in_order([mine, swap(mine, "tp")], it)
            return [jnp.stack([b[n] for b in both])[:, None] for n in range(block.shape[0])]

    def gather_half(name, block, *others):
        with jax.named_scope(name):
            sent = jnp.broadcast_to(block[None], (J, *block.shape))
            if others:
                sent = after(sent, *others)
            return lax.all_to_all(sent, "j", 0, 0).reshape(side, d_model)

    def sum_tokens(name, half, *others):
        with jax.named_scope(name):
            got = lax.all_to_all(half.reshape(J, rows, d_model), "j", 0, 0)
            if others:
                got = after(got, *others)
            return jnp.sum(got.astype(F32), 0)

    w_output_t = w_output.T
    w_down_t = w_down.T
    wide = 2 * qw + 2 * HEAD_DIM
    pos = positions[:, 0].reshape(1, H * rows)
    high = pos // 256
    extra = [jnp.concatenate([attn_gain, ffn_gain])[None], high.astype(BF), (pos - high * 256).astype(BF)]
    extra = [jnp.pad(e, ((0, 0), (0, wide - e.shape[1]))) for e in extra]
    extra = jnp.pad(jnp.concatenate(extra, 0), ((0, 5), (0, 0)))
    pack = [
        jnp.concatenate(
            [
                jnp.concatenate(
                    [
                        cut(w_query, p, qw),
                        cut(w_key, p, HEAD_DIM),
                        cut(w_value, p, HEAD_DIM),
                        cut(w_output_t, p, qw),
                    ],
                    1,
                ),
                extra,
            ],
            0,
        )
        for p in range(J)
    ]
    own = exchange("weights_attn", jnp.stack(pack))
    pack = [
        jnp.pad(
            jnp.concatenate([cut(w_gate, p, fw), cut(w_up, p, fw), cut(w_down_t, p, fw)], 1),
            ((0, 0), (0, 2 * ffn_width - 3 * fw)),
        )
        for p in range(J)
    ]
    ffn_own = exchange("weights_ffn", jnp.stack(pack))
    hidden_own = relative(fetch("fetch_hidden", hidden_in))

    def share(name, block):
        with jax.named_scope(name):
            return [block] + [
                lax.ppermute(block, "j", [(i, i ^ d) for i in range(J)]) for d in range(1, J)
            ]

    with jax.named_scope("weights_attn"):
        if B > 1:
            own = lax.all_gather(own, "b", axis=0, tiled=True)
        beside = swap(own, "h")
        opposite = swap(own, "dp")
    half = gather_half("tokens_hidden", hidden_own, ffn_own)
    with jax.named_scope("weights_attn"):
        across = swap(beside, "dp")
    cot_own = relative(fetch("fetch_cot", grad_out, beside))
    with jax.named_scope("weights_attn"):
        parts = [own, beside, opposite, across]
        wa = jnp.stack([p[:, :shard] for p in parts]).reshape(d_model, wide)
        extra = jnp.stack([p[:, shard : shard + 3] for p in parts])
    gains = extra[:, :, 0, : 2 * shard].reshape(4, B * J, 2, shard)
    gains = gains.transpose(2, 0, 1, 3).reshape(2, d_model).astype(F32)
    gain_attn = gains[0]
    gain_ffn = gains[1]
    pos = extra[:2, :, 1:, : H * rows].astype(F32)
    pos = pos[:, :, 0] * 256.0 + pos[:, :, 1]
    pos = lax.dynamic_index_in_dim(pos.reshape(H, B, J, H, rows), ib, 1, keepdims=False)
    pos = jnp.where(ih == 0, pos[:, :, 0], pos[:, :, 1])
    pos = jnp.stack(in_order([pos[0], pos[1]], ih ^ it), 0)
    pos_all = pos.reshape(count)

    place = jnp.arange(T * J, dtype=jnp.int32)
    block_of = (it ^ (place // J)) * (B * J) + place % J
    row_of = jnp.arange(rows, dtype=jnp.int32)
    query_index = ((block_of + ib * J)[:, None] * rows + row_of[None, :]).reshape(count)
    key_index = (
        (block_of[None, :] + jnp.arange(B, dtype=jnp.int32)[:, None] * J)[..., None] * rows + row_of
    ).reshape(B * count)

    inverse = 1.0 / ROPE_BASE ** (jnp.arange(0, HEAD_DIM, 2, dtype=F32) / HEAD_DIM)
    if B == 1:
        inverse = jnp.tile(inverse, 2 * LANES // HEAD_DIM)
    angles = pos_all[:, None] * inverse[None, :]
    cosine = jnp.cos(angles)
    sine = jnp.sin(angles)

    valid_length = lax.dynamic_index_in_dim(lengths[:, 0], ih, 0, keepdims=False)
    at = jnp.stack([valid_length, it])
    ones = jnp.ones((HEAD_DIM,), F32)
    qk_gain = jnp.stack(
        [jnp.concatenate([q_gain, q_gain]).astype(F32), jnp.concatenate([k_gain.astype(F32), ones])]
    )
    half = after(half, wa, gains, cosine, sine, cot_own, at, qk_gain)
    with jax.named_scope("weights_ffn"):
        ffn_own = ffn_own.reshape(J * shard, 2 * ffn_width)
        if B > 1:
            ffn_own = lax.all_gather(ffn_own, "b", axis=0, tiled=True)
        w_a = [ffn_own[:, :ffn_width]]
        w_b = [ffn_own[:, ffn_width:]]
        w_a.append(swap(after(w_a[0], half), "h"))
        w_b.append(swap(after(w_b[0], w_a[1]), "h"))
        w_own = swap(after(ffn_own, half), "dp")
    with jax.named_scope("tokens_hidden"):
        hidden = [half, swap(half, "tp")]
    stream = hidden_own.astype(F32)

    attn_factor = norm_scale(stream)
    if B == 1:
        *normed, raw, qkv = qkv_call(*hidden, gain_attn[None], wa, qk_gain, cosine, sine)
        mixed, probs = attend_call(at, qkv)
    else:
        hidden = jnp.concatenate(hidden, 0).astype(F32)
        normed = (hidden * norm_scale(hidden) * gain_attn).astype(BF)
        cosine = jnp.concatenate([cosine, cosine], -1)[:, None, :]
        sine = jnp.concatenate([sine, sine], -1)[:, None, :]
        raw = mm(normed, wa[:, : qw + 2 * HEAD_DIM])
        normed = [normed[:side], normed[side:]]
        qk_raw = raw[:, : qw + HEAD_DIM].reshape(count, group + 1, HEAD_DIM)
        qk_gain = jnp.stack([q_gain] * group + [k_gain]).astype(F32)
        qk_factor = norm_scale(qk_raw)
        qk_normed = qk_raw * qk_factor * qk_gain
        qk = (qk_normed * cosine + half_turn(qk_normed) * sine).astype(BF)
        queries = qk[:, :group].transpose(1, 0, 2)
        keys = qk[:, group]
        values = raw[:, qw + HEAD_DIM :].astype(BF)
        if B > 1:
            keys = lax.all_gather(keys, "b", axis=0, tiled=True)
            values = lax.all_gather(values, "b", axis=0, tiled=True)
        visible = (key_index[None, :] <= query_index[:, None]) & (key_index[None, :] < valid_length)

        def scores_of(query_head):
            return jnp.where(visible, mm_nt(query_head, keys) * score_scale, MASKED)

        def attend(query_head):
            scores = scores_of(query_head)
            row_max = jnp.max(scores, -1, keepdims=True)
            exp_scores = jnp.exp(scores - row_max)
            row_total = jnp.sum(exp_scores, -1, keepdims=True)
            probs = (exp_scores / row_total).astype(BF)
            return mm(probs, values).astype(BF), row_max + jnp.log(row_total)

        heads = [attend(queries[g]) for g in range(group)]
        mixed = jnp.concatenate([h[0] for h in heads], -1)
    parts = share("tokens_cot", after(cot_own, half))
    mixed = after(mixed, w_a[1], w_own, *parts[1:])
    with jax.named_scope("tokens_cot"):
        cot_half = jnp.concatenate(in_order(parts, ij), 0)
    with jax.named_scope("sum_attn"):
        wo = wa[:, qw + 2 * HEAD_DIM :]
        low = swap(mm_nt(mixed[side:], wo).astype(BF), "tp")
        low = add(mm_nt(mixed[:side], wo), low)
        w_a.append(swap(w_a[1], "dp"))
        attn_branch = sum_tokens("sum_attn", low)

    middle = stream + attn_branch
    gain_ffn = after(gain_ffn, w_b[1], w_a[2])
    ffn_factor = norm_scale(middle)
    xf_own = (middle * ffn_factor * gain_ffn).astype(BF)
    ffn_half = gather_half("tokens_xf", xf_own)
    with jax.named_scope("weights_ffn"):
        w_b.append(swap(w_b[1], "dp"))
    ffn_half = after(ffn_half, w_b[2])
    ffn_in = [ffn_half, swap(ffn_half, "tp")]
    cot = [cot_half, swap(cot_half, "tp")]
    first = ffn_call(fw, ffn_in[0], cot[0], w_a, w_b, w_own)
    second = ffn_call(fw, after(ffn_in[1], first[0]), cot[1], w_a, w_b, w_own)
    hidden_act, grad_pre, grad_in, branch = zip(first, second)
    low = swap(grad_in[1], "tp")
    opposite, across_a, across_b = ffn_grad_call(
        2, ffn_width, True, ffn_in, cot, grad_pre, hidden_act
    )
    low = add(grad_in[0], after(low, across_b))
    with jax.named_scope("grads_ffn"):
        got_b, got_a = swap(across_b, "dp"), swap(across_a, "dp")
    near_a, near_b, beside_a, beside_b = ffn_grad_call(
        0, ffn_width, False, ffn_in, cot, grad_pre, hidden_act
    )
    grad_ffn_in = sum_tokens("sum_dxf", low)
    gain_ffn = after(gain_ffn, got_b, near_a)

    grad_middle = cot_own.astype(F32) + norm_back(middle, ffn_factor, gain_ffn, grad_ffn_in)
    with jax.named_scope("grads_ffn"):
        beside_b = add(beside_b, got_b)
    half = gather_half("tokens_dattn", grad_middle.astype(BF), beside_b)
    with jax.named_scope("sum_out"):
        low = swap(after(branch[1], grad_ffn_in), "tp")
        low = add(branch[0], low)
    with jax.named_scope("grads_ffn"):
        got_b = swap(beside_b, "h")
        beside_a = add(beside_a, got_a)
        half = after(half, low, got_b, beside_a)
        got_a = swap(beside_a, "h")
        opposite = swap(after(opposite, half), "dp")
    grad_attn = [half, swap(half, "tp")]
    with jax.named_scope("sum_out"):
        parts = lax.all_to_all(after(low, half).reshape(J, rows, d_model), "j", 0, 0)
    if B == 1:
        grad_raw, totals, *gives, keep = attend_back_call(
            at, qkv, mixed, probs, raw, *grad_attn, wa, qk_gain, cosine, sine
        )
        totals = jnp.concatenate([totals[0, :HEAD_DIM] + totals[0, HEAD_DIM:], totals[1, :HEAD_DIM]])
    else:
        grad_mixed = mm(jnp.concatenate(grad_attn, 0), wo).astype(BF)
        grad_keys = jnp.zeros((B * count, HEAD_DIM), F32)
        grad_values = jnp.zeros((B * count, HEAD_DIM), F32)
        grad_queries = []
        for g in range(group):
            probs = jnp.exp(scores_of(queries[g]) - heads[g][1])
            grad_head = grad_mixed[:, g * HEAD_DIM : (g + 1) * HEAD_DIM]
            grad_probs = mm_nt(grad_head, values)
            row_delta = jnp.sum(grad_probs * probs, -1, keepdims=True)
            grad_scores = (probs * (grad_probs - row_delta)).astype(BF)
            grad_queries.append(mm(grad_scores, keys) * score_scale)
            grad_keys = grad_keys + mm_tn(grad_scores, queries[g]) * score_scale
            grad_values = grad_values + mm_tn(probs.astype(BF), grad_head)
        if B > 1:
            grad_keys = lax.psum_scatter(grad_keys, "b", scatter_dimension=0, tiled=True)
            grad_values = lax.psum_scatter(grad_values, "b", scatter_dimension=0, tiled=True)
        grad_rot = jnp.stack(grad_queries + [grad_keys], 1)
        grad_normed = grad_rot * cosine + half_turn_back(grad_rot * sine)
        grad_qk_raw = norm_back(qk_raw, qk_factor, qk_gain, grad_normed)
        terms = jnp.sum(grad_normed * qk_raw * qk_factor, 0)
        totals = jnp.concatenate([jnp.sum(terms[:group], 0), terms[group]])
        grad_raw = jnp.concatenate(
            [grad_qk_raw.reshape(count, qw + HEAD_DIM), grad_values], 1
        ).astype(BF)
    if B > 1:
        w_qkv = wa[:, : qw + 2 * HEAD_DIM]
        gives = [mm_nt(g, w_qkv).astype(BF) for g in jnp.split(grad_raw[side:], 2)]
        keep = mm_nt(grad_raw[:side], w_qkv).astype(BF)
    grad_raw = after(grad_raw, got_a)
    gives = [swap(after(g, grad_raw), "tp") for g in gives]
    grads_attn = attn_grad_call(normed, grad_attn, grad_raw, mixed)
    gives[0] = after(gives[0], parts, *grads_attn[2:])
    gives[1] = after(gives[1], opposite)
    low = add_call(keep, *gives)
    grad_normed_own = sum_tokens("sum_dxa", low)
    total = jnp.sum(after(parts, low).astype(F32), 0)
    out_own = relative((middle + total).astype(BF))
    with jax.named_scope("grads_ffn"):
        pieces = [near_a, near_b, got_a, got_b, opposite]
        if B == 1:
            pieces = list(merge_call(ij[None], J, after(near_a, low), *pieces[1:]))
        else:
            near = jnp.concatenate([add(near_a, got_a), add(near_b, got_b)], 1)
            near = lax.psum_scatter(add(near, opposite), "b", scatter_dimension=0, tiled=True)
            near = near.reshape(J, shard, 2 * ffn_width)
            pieces = [lax.dynamic_index_in_dim(near, ij ^ d, 0, keepdims=False) for d in range(J)]
        for d in range(1, J):
            pieces[d] = lax.ppermute(pieces[d], "j", [(i, i ^ d) for i in range(J)])
    grad_stream = grad_middle + norm_back(stream, attn_factor, gain_attn, grad_normed_own)
    sent = jnp.stack([out_own, relative(grad_stream.astype(BF))])
    out_hidden, grad_hidden = give_back("return", sent)
    with jax.named_scope("grads_attn"):
        totals = jnp.pad(totals[None], ((0, 0), (0, wide - 2 * HEAD_DIM)))
        near, beside, opposed, across = grads_attn
        got = swap(jnp.concatenate([across, two_numbers(totals)], 0), "dp")
        got_near = swap(opposed, "dp")
        got = after(got, low)
        totals = totals + one_number(got[part:])
        beside = jnp.concatenate([add(beside, got[:part]), two_numbers(totals)], 0)
        got = swap(beside, "h")
        totals = totals + one_number(got[part:])
    with jax.named_scope("grads"):
        got = after(got, grad_normed_own)
        near = add(near.astype(F32) + got_near.astype(F32), got[:part])
        extra = two_numbers(totals[:, :LANES])
        extra = jnp.pad(extra, ((0, shard - extra.shape[0]), (0, 0)))
        extra = jnp.broadcast_to(extra[None], (B * J, shard, LANES))
        near = jnp.concatenate([near.reshape(B * J, shard, near.shape[1]), extra], 2)
        if B > 1:
            near = lax.psum_scatter(near, "b", scatter_dimension=0, tiled=True)
        shards = lax.all_to_all(near, "j", 0, 0)
    totals = jnp.sum(one_number(shards[:, :, -LANES:]), (0, 1))
    *shard_grads, sums = final_call(qw, fw, ij[None], shards, pieces, w_query, w_key, w_value, w_gate, w_up)

    sums = jnp.concatenate([totals, sums[:, 0], sums[:, 1]])
    sums = sums + swap(sums, "tp")
    totals = sums[: 2 * HEAD_DIM].reshape(2, HEAD_DIM)
    sums = sums[2 * HEAD_DIM :].reshape(2, shard) / jnp.stack([attn_gain, ffn_gain]).astype(F32)

    shard_query, shard_key, shard_value, shard_output, shard_gate, shard_up, shard_down = shard_grads
    return (
        out_hidden,
        grad_hidden,
        sums[0],
        shard_query,
        shard_key,
        shard_value,
        totals[0],
        totals[1],
        shard_output.T,
        sums[1],
        shard_gate,
        shard_up,
        shard_down.T,
    )


def solution(mesh):
    places = KV_HEADS // mesh.shape["tp"]

    def run(*args):
        micro = args[0].shape[0]
        shape = (mesh.shape["dp"], micro, mesh.shape["ctx"] // (micro * places), places)
        fine = Mesh(
            mesh.devices.reshape(*shape, mesh.shape["tp"]), ("dp", "h", "b", "j", "tp")
        )
        ctx = ("h", "b", "j")
        rows = ("dp", "h", "b", "j")
        tokens = P(None, "dp", ctx, None)
        return jax.shard_map(
            body,
            mesh=fine,
            in_specs=(
                tokens,
                P(None, "dp"),
                P(None, "dp", ctx),
                P(rows),
                P(rows, "tp"),
                P(rows, "tp"),
                P(rows, "tp"),
                P(),
                P(),
                P("tp", rows),
                P(rows),
                P(rows, "tp"),
                P(rows, "tp"),
                P("tp", rows),
                tokens,
            ),
            out_specs=(
                tokens,
                tokens,
                P(rows),
                P(rows, "tp"),
                P(rows, "tp"),
                P(rows, "tp"),
                P(),
                P(),
                P("tp", rows),
                P(rows),
                P(rows, "tp"),
                P(rows, "tp"),
                P("tp", rows),
            ),
            check_vma=False,
        )(*args)

    return run
```

```python
import functools

import jax
import jax.numpy as jnp
from jax import lax
from jax.experimental import pallas as pl
from jax.experimental.pallas import tpu as pltpu
from jax.sharding import Mesh, PartitionSpec as P

HEADS = 16
KV_HEADS = 8
HEAD_DIM = 64
EPSILON = 1e-05
ROPE_BASE = 1000000.0
MASKED = -1e30
BF = jnp.bfloat16
F32 = jnp.float32
VMEM_BYTES = 60 * 2**20
LANES = 128
SMALL_COST = pl.CostEstimate(flops=1, bytes_accessed=1, transcendentals=0)


def dot(a, b, dims):
    return lax.dot_general(a, b, (dims, ((), ())), preferred_element_type=F32)


def mm(a, b):
    return dot(a, b, ((1,), (0,)))


def mm_nt(a, b):
    return dot(a, b, ((1,), (1,)))


def mm_tn(a, b):
    return dot(a, b, ((0,), (0,)))


def nothing(*refs):
    pass


def after(value, *others):
    anywhere = pl.BlockSpec(memory_space=pl.ANY)
    return pl.pallas_call(
        nothing,
        in_specs=[anywhere] * (1 + len(others)),
        out_specs=anywhere,
        out_shape=jax.ShapeDtypeStruct(value.shape, value.dtype),
        input_output_aliases={0: 0},
        cost_estimate=SMALL_COST,
        name="after",
    )(value, *others)


def swap(v, axis):
    return lax.ppermute(v, axis, [(0, 1), (1, 0)])


def add(a, b):
    return (a.astype(F32) + b.astype(F32)).astype(BF)


def norm_scale(vector):
    return lax.rsqrt(jnp.mean(vector * vector, -1, keepdims=True) + EPSILON)


def norm_back(vector, factor, gain, upstream):
    weighted = upstream * gain
    return factor * weighted - vector * factor * factor * factor * jnp.mean(
        vector * weighted, -1, keepdims=True
    )


def half_turn(vector):
    middle_index = vector.shape[-1] // 2
    return jnp.concatenate([-vector[..., middle_index:], vector[..., :middle_index]], -1)


def half_turn_back(vector):
    middle_index = vector.shape[-1] // 2
    return jnp.concatenate([vector[..., middle_index:], -vector[..., :middle_index]], -1)


def in_order(parts, index):
    bit = 1
    while bit < len(parts):
        flag = (index & bit) != 0
        parts = [jnp.where(flag, parts[i ^ bit], parts[i]) for i in range(len(parts))]
        bit *= 2
    return parts


def row_sums(square, low):
    left = jnp.sum(jnp.where(low, square, 0.0), -1, keepdims=True)
    right = jnp.sum(jnp.where(low, 0.0, square), -1, keepdims=True)
    return jnp.where(low, left, right)


def pair_scale(pair, low):
    return lax.rsqrt(row_sums(pair * pair, low) * (1.0 / HEAD_DIM) + EPSILON)


def lanes(shape):
    return lax.broadcasted_iota(jnp.int32, shape, 1)


def turned(pair, first):
    width = pair.shape[1]
    quarter = HEAD_DIM // 2
    return jnp.where(first, pltpu.roll(pair, width - quarter, 1), pltpu.roll(pair, quarter, 1))


def qkv_kernel(half_tiles, h0_ref, h1_ref, gain_ref, w_ref, qk_gain_ref, cos_ref, sin_ref,
               xa0_ref, xa1_ref, raw_ref, qkv_ref):
    def run(h_ref, xa_ref):
        hidden = h_ref[...].astype(F32)
        factor = lax.rsqrt(jnp.mean(hidden * hidden, -1, keepdims=True) + EPSILON)
        xa = (hidden * factor * gain_ref[...]).astype(BF)
        xa_ref[...] = xa
        raw = mm(xa, w_ref[:, :256])
        raw_ref[...] = raw
        lane = lanes((raw.shape[0], 128))
        low = lane < HEAD_DIM
        first = lane % HEAD_DIM < HEAD_DIM // 2
        cosine, sine = cos_ref[...], sin_ref[...]
        sine = jnp.where(first, -sine, sine)
        for p in range(2):
            pair = raw[:, 128 * p : 128 * (p + 1)]
            normed = pair * pair_scale(pair, low) * qk_gain_ref[p : p + 1, :]
            turned_pair = normed * cosine + turned(normed, first) * sine
            if p == 1:
                turned_pair = jnp.where(low, turned_pair, pair)
            qkv_ref[:, 128 * p : 128 * (p + 1)] = turned_pair.astype(BF)

    @pl.when(pl.program_id(0) < half_tiles)
    def _():
        run(h0_ref, xa0_ref)

    @pl.when(pl.program_id(0) >= half_tiles)
    def _():
        run(h1_ref, xa1_ref)


def qkv_call(h0, h1, gain, w, qk_gain, cosine, sine):
    half, d_model = h0.shape
    tile = min(256, half)
    n = half // tile
    own = pl.BlockSpec((tile, d_model), lambda i: (jnp.minimum(i, n - 1), 0))
    other = pl.BlockSpec((tile, d_model), lambda i: (jnp.maximum(i - n, 0), 0))
    def fixed(a):
        return pl.BlockSpec(a.shape, lambda i: (0, 0))
    def rows(width):
        return pl.BlockSpec((tile, width), lambda i: (i, 0))
    return pl.pallas_call(
        functools.partial(qkv_kernel, n),
        grid=(2 * n,),
        in_specs=[own, other, fixed(gain), fixed(w), fixed(qk_gain), rows(128), rows(128)],
        out_specs=[own, other, rows(256), rows(256)],
        out_shape=[
            jax.ShapeDtypeStruct(h0.shape, BF),
            jax.ShapeDtypeStruct(h0.shape, BF),
            jax.ShapeDtypeStruct((2 * half, 256), F32),
            jax.ShapeDtypeStruct((2 * half, 256), BF),
        ],
        compiler_params=pltpu.CompilerParams(vmem_limit_bytes=VMEM_BYTES),
        cost_estimate=SMALL_COST,
        name="qkv",
    )(h0, h1, gain, w, qk_gain, cosine, sine)


def blocks_of(tiles):
    return [(a, k) for a in range(tiles) for k in range(a + 1)]


def stacked(pair):
    return jnp.concatenate([pair[:, :HEAD_DIM], pair[:, HEAD_DIM:]], 0)


def attend_kernel(tile, tiles, at_ref, qkv_ref, mixed_ref, probs_ref):
    half = tiles // 2
    def place(t):
        return pl.multiple_of((t + half * at_ref[1]) % tiles * tile, tile)
    for a in range(tiles):
        query = stacked(qkv_ref[pl.ds(place(a), tile), :128])
        row = lax.broadcasted_iota(jnp.int32, (2 * tile, 1), 0) % tile + a * tile
        limit = jnp.minimum(row + 1, at_ref[0])
        scores = []
        for k in range(a + 1):
            key = qkv_ref[pl.ds(place(k), tile), 128 : 128 + HEAD_DIM]
            column = lax.broadcasted_iota(jnp.int32, (1, tile), 1) + k * tile
            scores.append(
                jnp.where(column < limit, mm_nt(query, key) * HEAD_DIM ** (-0.5), MASKED)
            )
        peak = functools.reduce(jnp.maximum, [jnp.max(s, -1, keepdims=True) for s in scores])
        exps = [jnp.exp(s - peak) for s in scores]
        total = functools.reduce(jnp.add, [jnp.sum(e, -1, keepdims=True) for e in exps])
        inverse = 1.0 / total
        mixed = 0.0
        for k in range(a + 1):
            probs = (exps[k] * inverse).astype(BF)
            probs_ref[blocks_of(tiles).index((a, k))] = probs
            value = qkv_ref[pl.ds(place(k), tile), 128 + HEAD_DIM :]
            mixed = mixed + mm(probs, value)
        mixed_ref[pl.ds(place(a), tile), :] = jnp.concatenate(
            [mixed[:tile], mixed[tile:]], 1
        ).astype(BF)


def attend_call(at, qkv):
    count = qkv.shape[0]
    tile = min(256, count // 2)
    tiles = count // tile
    pairs = len(blocks_of(tiles))
    return pl.pallas_call(
        functools.partial(attend_kernel, tile, tiles),
        in_specs=[pl.BlockSpec(memory_space=pltpu.SMEM), pl.BlockSpec(memory_space=pltpu.VMEM)],
        out_specs=[pl.BlockSpec(memory_space=pltpu.VMEM)] * 2,
        out_shape=[
            jax.ShapeDtypeStruct((count, 128), BF),
            jax.ShapeDtypeStruct((pairs, 2 * tile, tile), BF),
        ],
        compiler_params=pltpu.CompilerParams(vmem_limit_bytes=VMEM_BYTES),
        cost_estimate=SMALL_COST,
        name="attend",
    )(at, qkv)


def attend_back_kernel(tile, tiles, at_ref, qkv_ref, mixed_ref, probs_ref, raw_ref, g0_ref, g1_ref,
                       wa_ref, qk_gain_ref, cos_ref, sin_ref, out_ref, total_ref, give0_ref,
                       give1_ref, keep_ref, dm_ref, dkv_ref):
    half = tiles // 2
    def place(t):
        return pl.multiple_of((t + half * at_ref[1]) % tiles * tile, tile)
    rows = half * tile
    wide = out_ref.shape[1]
    dm_ref[:rows] = mm(g0_ref[...], wa_ref[:, wide:]).astype(BF)
    dm_ref[rows:] = mm(g1_ref[...], wa_ref[:, wide:]).astype(BF)
    scale = HEAD_DIM ** (-0.5)
    lane = lanes((tile, 128))
    low = lane < HEAD_DIM
    first = lane % HEAD_DIM < HEAD_DIM // 2

    def finish(t, p, grad):
        at = pl.ds(place(t), tile)
        cosine, sine = cos_ref[at], sin_ref[at]
        pair = raw_ref[at, 128 * p : 128 * (p + 1)]
        factor = pair_scale(pair, low)
        signed = grad * jnp.where(first, -sine, sine)
        upstream = grad * cosine + turned(signed, first)
        gain = qk_gain_ref[p : p + 1, :]
        weighted = upstream * gain
        mean = row_sums(pair * weighted, low) * (1.0 / HEAD_DIM)
        result = factor * weighted - pair * (factor * factor * factor * mean)
        terms = jnp.sum(upstream * pair * factor, 0, keepdims=True)
        if p == 1:
            result = jnp.where(low, result, grad)
        out_ref[at, 128 * p : 128 * (p + 1)] = result.astype(BF)
        total_ref[p : p + 1, :] += terms

    total_ref[...] = jnp.zeros_like(total_ref)
    dkv = [0.0] * tiles
    for a in range(tiles):
        at = pl.ds(place(a), tile)
        query = stacked(qkv_ref[at, :128])
        grad = stacked(dm_ref[at])
        mixed = stacked(mixed_ref[at, :])
        delta = jnp.sum(grad.astype(F32) * mixed.astype(F32), -1, keepdims=True)
        grad_query = 0.0
        for k in range(a + 1):
            keys = pl.ds(place(k), tile)
            key = qkv_ref[keys, 128 : 128 + HEAD_DIM]
            value = qkv_ref[keys, 128 + HEAD_DIM :]
            probs = probs_ref[blocks_of(tiles).index((a, k))]
            grad_scores = (probs.astype(F32) * (mm_nt(grad, value) - delta)).astype(BF)
            grad_query = grad_query + mm(grad_scores, key)
            grad_kv = jnp.concatenate(
                [mm_tn(grad_scores, query) * scale, mm_tn(probs, grad)], 1
            )
            if a == k:
                dkv_ref[k] = grad_kv
            else:
                dkv_ref[k] += grad_kv
        grad_query = grad_query * scale
        finish(a, 0, jnp.concatenate([grad_query[:tile], grad_query[tile:]], 1))
    for k in range(tiles):
        finish(k, 1, dkv_ref[k])
    w = wa_ref[:, :wide]
    middle = rows + rows // 2
    give0_ref[...] = mm_nt(out_ref[rows:middle], w).astype(BF)
    give1_ref[...] = mm_nt(out_ref[middle:], w).astype(BF)
    keep_ref[...] = mm_nt(out_ref[:rows], w).astype(BF)


def attend_back_call(at, qkv, mixed, probs, raw, g0, g1, wa, qk_gain, cosine, sine):
    count, d_model = qkv.shape[0], g0.shape[1]
    tile = min(256, count // 2)
    tiles = count // tile
    vmem = pl.BlockSpec(memory_space=pltpu.VMEM)
    return pl.pallas_call(
        functools.partial(attend_back_kernel, tile, tiles),
        in_specs=[pl.BlockSpec(memory_space=pltpu.SMEM)] + [vmem] * 10,
        out_specs=[vmem] * 5,
        out_shape=[
            jax.ShapeDtypeStruct((count, 256), BF),
            jax.ShapeDtypeStruct((8, 128), F32),
            jax.ShapeDtypeStruct((count // 4, d_model), BF),
            jax.ShapeDtypeStruct((count // 4, d_model), BF),
            jax.ShapeDtypeStruct((count // 2, d_model), BF),
        ],
        scratch_shapes=[pltpu.VMEM((count, 128), BF), pltpu.VMEM((tiles, tile, 128), F32)],
        compiler_params=pltpu.CompilerParams(vmem_limit_bytes=VMEM_BYTES),
        cost_estimate=SMALL_COST,
        name="attend_back",
    )(at, qkv, mixed, probs, raw, g0, g1, wa, qk_gain, cosine, sine)


def ffn_kernel(fw, part, x_ref, cot_ref, *refs):
    a_refs, b_refs, (w_ref, act_ref, grad_ref, grad_in_ref, out_ref) = refs[:3], refs[3:6], refs[6:]
    width = a_refs[0].shape[1]
    a_refs = [*a_refs[:2], w_ref.at[:, :width], a_refs[2]]
    b_refs = [*b_refs[:2], w_ref.at[:, width:], b_refs[2]]
    rest = 2 * fw - width
    pre_a, pre_b, grad_act = 0.0, 0.0, 0.0
    for p in range(4):
        cut = slice(p * part, (p + 1) * part)
        pre_a = pre_a + mm(x_ref[:, cut], a_refs[p][...])
        pre_b = pre_b + mm(x_ref[:, cut], b_refs[p][:, :rest])
        grad_act = grad_act + mm(cot_ref[:, cut], b_refs[p][:, rest : rest + fw])
    pre = jnp.concatenate([pre_a, pre_b], 1)
    gate, up = pre[:, :fw], pre[:, fw:]
    sigmoid = 1.0 / (1.0 + jnp.exp(-gate))
    silu = gate * sigmoid
    act = (silu * up).astype(BF)
    act_ref[...] = act
    grad_gate = grad_act * up * sigmoid * (1.0 + gate * (1.0 - sigmoid))
    grad = jnp.concatenate([grad_gate, grad_act * silu], 1).astype(BF)
    grad_ref[...] = grad
    for p in range(4):
        cut = slice(p * part, (p + 1) * part)
        grad_in = mm_nt(grad[:, :width], a_refs[p][...])
        grad_in = grad_in + mm_nt(grad[:, width:], b_refs[p][:, :rest])
        grad_in_ref[:, cut] = grad_in.astype(BF)
        out_ref[:, cut] = mm_nt(act, b_refs[p][:, rest : rest + fw]).astype(BF)


def ffn_call(fw, x, cot, w_a, w_b, w_own):
    count, d_model = x.shape
    part = w_a[0].shape[0]
    tile = min(256, count)
    shapes = [(count, fw), (count, 2 * fw), (count, d_model), (count, d_model)]
    return pl.pallas_call(
        functools.partial(ffn_kernel, fw, part),
        grid=(count // tile,),
        in_specs=[
            pl.BlockSpec((tile, d_model), lambda i: (i, 0)),
            pl.BlockSpec((tile, d_model), lambda i: (i, 0)),
        ]
        + [pl.BlockSpec(p.shape, lambda i: (0, 0)) for p in (*w_a, *w_b, w_own)],
        out_specs=[pl.BlockSpec((tile, s[1]), lambda i: (i, 0)) for s in shapes],
        out_shape=[jax.ShapeDtypeStruct(s, BF) for s in shapes],
        compiler_params=pltpu.CompilerParams(vmem_limit_bytes=VMEM_BYTES),
        cost_estimate=SMALL_COST,
        name="ffn",
    )(x, cot, *w_a, *w_b, w_own)


def ffn_grad_kernel(fw, width, whole, *refs):
    ins, outs = refs[:8], refs[8:]
    x0, x1, cot0, cot1, grad0, grad1, act0, act1 = (r[...] for r in ins)
    grad_in = (mm_tn(x0, grad0) + mm_tn(x1, grad1)).astype(BF)
    grad_out = (mm_tn(cot0, act0) + mm_tn(cot1, act1)).astype(BF)
    rest = 2 * fw - width

    def write(a_ref, b_ref):
        a_ref[...] = grad_in[:, :width]
        b_ref[:, :rest] = grad_in[:, width:]
        b_ref[:, rest : rest + fw] = grad_out
        left = width - rest - fw
        if left:
            b_ref[:, rest + fw :] = jnp.zeros((grad_out.shape[0], left), BF)

    @pl.when(pl.program_id(0) == 0)
    def _():
        if whole:
            write(outs[0].at[:, :width], outs[0].at[:, width:])
        else:
            write(*outs[:2])

    @pl.when(pl.program_id(0) == 1)
    def _():
        write(*outs[-2:])


def ffn_grad_call(p, width, whole, x, cot, grad, act):
    count, d_model = x[0].shape
    fw = act[0].shape[1]
    part = d_model // 4
    columns = pl.BlockSpec((count, part), lambda i: (0, p + i))
    operands = [pl.BlockSpec(a.shape, lambda i: (0, 0)) for a in (*grad, *act)]
    shapes = ([(part, 2 * width)] if whole else [(part, width)] * 2) + [(part, width)] * 2
    return pl.pallas_call(
        functools.partial(ffn_grad_kernel, fw, width, whole),
        grid=(2,),
        in_specs=[columns] * 4 + operands,
        out_specs=[pl.BlockSpec(s, lambda i: (0, 0)) for s in shapes],
        out_shape=[jax.ShapeDtypeStruct(s, BF) for s in shapes],
        compiler_params=pltpu.CompilerParams(vmem_limit_bytes=VMEM_BYTES),
        cost_estimate=SMALL_COST,
        name="ffn_grad",
    )(*x, *cot, *grad, *act)


def add_kernel(keep_ref, got0_ref, got1_ref, out_ref):
    rows = got0_ref.shape[0]
    out_ref[:rows] = (keep_ref[:rows].astype(F32) + got0_ref[...].astype(F32)).astype(BF)
    out_ref[rows:] = (keep_ref[rows:].astype(F32) + got1_ref[...].astype(F32)).astype(BF)


def add_call(keep, got0, got1):
    vmem = pl.BlockSpec(memory_space=pltpu.VMEM)
    return pl.pallas_call(
        add_kernel,
        in_specs=[vmem] * 3,
        out_specs=vmem,
        out_shape=jax.ShapeDtypeStruct(keep.shape, BF),
        compiler_params=pltpu.CompilerParams(vmem_limit_bytes=VMEM_BYTES),
        cost_estimate=SMALL_COST,
        name="add",
    )(keep, got0, got1)


def add_cut_kernel(place_ref, a_ref, b_ref, *outs):
    height = outs[0].shape[0]
    for d, out_ref in enumerate(outs):
        at = pl.ds(pl.multiple_of((place_ref[0] ^ d) * height, height), height)
        out_ref[...] = (a_ref[at, :].astype(F32) + b_ref[at, :].astype(F32)).astype(BF)


def add_cut_call(place, places, a, b):
    vmem = pl.BlockSpec(memory_space=pltpu.VMEM)
    shape = jax.ShapeDtypeStruct((a.shape[0] // places, a.shape[1]), BF)
    return pl.pallas_call(
        add_cut_kernel,
        in_specs=[pl.BlockSpec(memory_space=pltpu.SMEM)] + [vmem] * 2,
        out_specs=[vmem] * places,
        out_shape=[shape] * places,
        compiler_params=pltpu.CompilerParams(vmem_limit_bytes=VMEM_BYTES),
        cost_estimate=SMALL_COST,
        name="add_cut",
    )(place, a, b)


def attn_grad_kernel(x0_ref, x1_ref, g0_ref, g1_ref, raw_ref, mixed_ref, *outs):
    side = x0_ref.shape[0]
    wide = raw_ref.shape[1]
    grad_qkv = mm_tn(x0_ref[...], raw_ref[:side]) + mm_tn(x1_ref[...], raw_ref[side:])
    grad_o = mm_tn(g0_ref[...], mixed_ref[:side]) + mm_tn(g1_ref[...], mixed_ref[side:])
    for p in range(4):

        @pl.when(pl.program_id(0) == p)
        def _():
            outs[p][:, :wide] = grad_qkv.astype(BF)
            outs[p][:, wide:] = grad_o.astype(BF)


def attn_grad_call(x, g, raw, mixed):
    count, d_model = x[0].shape
    part = d_model // 4
    shape = (part, raw.shape[1] + mixed.shape[1])
    columns = pl.BlockSpec((count, part), lambda i: (0, i))
    return pl.pallas_call(
        attn_grad_kernel,
        grid=(4,),
        in_specs=[columns] * 4 + [pl.BlockSpec(a.shape, lambda i: (0, 0)) for a in (raw, mixed)],
        out_specs=[pl.BlockSpec(shape, lambda i: (0, 0))] * 4,
        out_shape=[jax.ShapeDtypeStruct(shape, BF)] * 4,
        compiler_params=pltpu.CompilerParams(vmem_limit_bytes=VMEM_BYTES),
        cost_estimate=SMALL_COST,
        name="attn_grad",
    )(*x, *g, raw, mixed)


def merge_kernel(place_ref, near_a, near_b, got_a, got_b, opposite, *outs):
    height, width = outs[0].shape[0], near_a.shape[1]
    for d, out_ref in enumerate(outs):
        at = pl.ds(pl.multiple_of((place_ref[0] ^ d) * height, height), height)
        for near, got, start in ((near_a, got_a, 0), (near_b, got_b, width)):
            total = near[at, :].astype(F32) + got[at, :].astype(F32)
            total = total + opposite[at, start : start + width].astype(F32)
            out_ref[:, start : start + width] = total.astype(BF)


def merge_call(place, places, *arrays):
    rows, width = arrays[0].shape
    shape = jax.ShapeDtypeStruct((rows // places, 2 * width), BF)
    vmem = pl.BlockSpec(memory_space=pltpu.VMEM)
    return pl.pallas_call(
        merge_kernel,
        in_specs=[pl.BlockSpec(memory_space=pltpu.SMEM)] + [vmem] * 5,
        out_specs=[vmem] * places,
        out_shape=[shape] * places,
        compiler_params=pltpu.CompilerParams(vmem_limit_bytes=VMEM_BYTES),
        cost_estimate=SMALL_COST,
        name="merge",
    )(place, *arrays)


def final_kernel(
    qw, fw, place_ref, got_ref, p0_ref, p1_ref, p2_ref, p3_ref, wq_ref, wk_ref, wv_ref, wg_ref, wu_ref,
    q_ref, k_ref, v_ref, o_ref, gate_ref, up_ref, down_ref, sum_ref,
):
    places = got_ref.shape[0]

    def side_by_side(start, width):
        return jnp.concatenate(
            [got_ref[p, :, start : start + width] for p in range(places)], 1
        ).astype(F32)

    def rows(weight_ref, grad):
        return jnp.sum(weight_ref[...].astype(F32) * grad, 1, keepdims=True)

    query, key, value = side_by_side(0, qw), side_by_side(qw, HEAD_DIM), side_by_side(qw + HEAD_DIM, HEAD_DIM)
    q_ref[...], k_ref[...], v_ref[...] = query, key, value
    sum_attn = rows(wq_ref, query) + rows(wk_ref, key) + rows(wv_ref, value)
    start = qw + 2 * HEAD_DIM
    o_ref[...] = side_by_side(start, qw)
    pieces = in_order([r[...].astype(F32) for r in (p0_ref, p1_ref, p2_ref, p3_ref)], place_ref[0])
    gate, up, down = (
        jnp.concatenate([p[:, n * fw : (n + 1) * fw] for p in pieces], 1) for n in range(3)
    )
    gate_ref[...], up_ref[...] = gate, up
    sum_ffn = rows(wg_ref, gate) + rows(wu_ref, up)
    down_ref[...] = down
    lane = lanes(sum_ref.shape)
    sum_ref[...] = jnp.where(lane == 0, sum_attn, sum_ffn)


def final_call(qw, fw, place, got, pieces, wq, wk, wv, wg, wu):
    shard = got.shape[1]
    vmem = pl.BlockSpec(memory_space=pltpu.VMEM)
    shapes = [wq.shape, wk.shape, wv.shape, wq.shape, wg.shape, wu.shape, wg.shape]
    shapes.append((shard, LANES))
    return pl.pallas_call(
        functools.partial(final_kernel, qw, fw),
        in_specs=[pl.BlockSpec(memory_space=pltpu.SMEM)] + [vmem] * 10,
        out_specs=[vmem] * 8,
        out_shape=[jax.ShapeDtypeStruct(s, F32) for s in shapes],
        compiler_params=pltpu.CompilerParams(vmem_limit_bytes=VMEM_BYTES),
        cost_estimate=SMALL_COST,
        name="final",
    )(place, got, *pieces, wq, wk, wv, wg, wu)


def body(
    hidden_in,
    lengths,
    positions,
    attn_gain,
    w_query,
    w_key,
    w_value,
    q_gain,
    k_gain,
    w_output,
    ffn_gain,
    w_gate,
    w_up,
    w_down,
    grad_out,
):
    H, B, J, T = (lax.axis_size(a) for a in ("h", "b", "j", "tp"))
    ix, ih, ib, ij, it = (lax.axis_index(a) for a in ("dp", "h", "b", "j", "tp"))
    rows = hidden_in.shape[2]
    d_model = hidden_in.shape[3]
    shard = w_query.shape[0]
    group = HEADS // KV_HEADS
    qw = group * HEAD_DIM
    fw = w_gate.shape[1] // J
    count = T * J * rows
    side = J * rows
    ffn_width = -(-3 * fw // (2 * LANES)) * LANES
    score_scale = HEAD_DIM ** (-0.5)
    quarter = 2 * ix + ih
    part = d_model // 4

    def cut(array, p, width):
        return array[:, p * width : (p + 1) * width]

    def exchange(name, pieces):
        with jax.named_scope(name):
            return lax.all_to_all(pieces, "j", 0, 0)

    def exchange_beside(name, pieces):
        with jax.named_scope(name):
            pieces = in_order(pieces, ij)
            parts = [pieces[0]]
            for d in range(1, J):
                parts.append(lax.ppermute(pieces[d], "j", [(i, i ^ d) for i in range(J)]))
            return parts

    def two_numbers(values):
        high = values.astype(BF)
        low = (values - high.astype(F32)).astype(BF)
        return jnp.pad(jnp.concatenate([high, low], 0), ((0, 6), (0, 0)))

    def one_number(block):
        return block[..., 0:1, :].astype(F32) + block[..., 1:2, :].astype(F32)

    def relative(array):
        pieces = [array[..., p * part : (p + 1) * part] for p in range(4)]
        return jnp.concatenate(in_order(pieces, quarter), -1)

    turn = [(0, 0), (1, 2), (2, 1), (3, 3)]

    def fetch(name, array, *others):
        with jax.named_scope(name):
            mine = lax.dynamic_index_in_dim(array, it, 0, keepdims=False)[0]
            if others:
                mine = after(mine, *others)
            return lax.ppermute(mine, ("h", "tp"), turn)

    def give_back(name, block):
        with jax.named_scope(name):
            mine = lax.ppermute(block, ("h", "tp"), turn)
            both = in_order([mine, swap(mine, "tp")], it)
            return [jnp.stack([b[n] for b in both])[:, None] for n in range(block.shape[0])]

    def gather_half(name, block, *others):
        with jax.named_scope(name):
            sent = jnp.broadcast_to(block[None], (J, *block.shape))
            if others:
                sent = after(sent, *others)
            return lax.all_to_all(sent, "j", 0, 0).reshape(side, d_model)

    def sum_tokens(name, half, *others):
        with jax.named_scope(name):
            got = lax.all_to_all(half.reshape(J, rows, d_model), "j", 0, 0)
            if others:
                got = after(got, *others)
            return jnp.sum(got.astype(F32), 0)

    w_output_t = w_output.T
    w_down_t = w_down.T
    wide = 2 * qw + 2 * HEAD_DIM
    pos = positions[:, 0].reshape(1, H * rows)
    high = pos // 256
    extra = [jnp.concatenate([attn_gain, ffn_gain])[None], high.astype(BF), (pos - high * 256).astype(BF)]
    extra = [jnp.pad(e, ((0, 0), (0, wide - e.shape[1]))) for e in extra]
    extra = jnp.pad(jnp.concatenate(extra, 0), ((0, 5), (0, 0)))
    pack = [
        jnp.concatenate(
            [
                jnp.concatenate(
                    [
                        cut(w_query, p, qw),
                        cut(w_key, p, HEAD_DIM),
                        cut(w_value, p, HEAD_DIM),
                        cut(w_output_t, p, qw),
                    ],
                    1,
                ),
                extra,
            ],
            0,
        )
        for p in range(J)
    ]
    own = exchange("weights_attn", jnp.stack(pack))
    pack = [
        jnp.pad(
            jnp.concatenate([cut(w_gate, p, fw), cut(w_up, p, fw), cut(w_down_t, p, fw)], 1),
            ((0, 0), (0, 2 * ffn_width - 3 * fw)),
        )
        for p in range(J)
    ]
    ffn_own = exchange("weights_ffn", jnp.stack(pack))
    hidden_own = relative(fetch("fetch_hidden", hidden_in))

    def share(name, block):
        with jax.named_scope(name):
            return [block] + [
                lax.ppermute(block, "j", [(i, i ^ d) for i in range(J)]) for d in range(1, J)
            ]

    with jax.named_scope("weights_attn"):
        if B > 1:
            own = lax.all_gather(own, "b", axis=0, tiled=True)
        beside = swap(own, "h")
        opposite = swap(own, "dp")
    half = gather_half("tokens_hidden", hidden_own, ffn_own)
    with jax.named_scope("weights_attn"):
        across = swap(beside, "dp")
    cot_own = relative(fetch("fetch_cot", grad_out, beside))
    with jax.named_scope("weights_attn"):
        parts = [own, beside, opposite, across]
        wa = jnp.stack([p[:, :shard] for p in parts]).reshape(d_model, wide)
        extra = jnp.stack([p[:, shard : shard + 3] for p in parts])
    gains = extra[:, :, 0, : 2 * shard].reshape(4, B * J, 2, shard)
    gains = gains.transpose(2, 0, 1, 3).reshape(2, d_model).astype(F32)
    gain_attn = gains[0]
    gain_ffn = gains[1]
    pos = extra[:2, :, 1:, : H * rows].astype(F32)
    pos = pos[:, :, 0] * 256.0 + pos[:, :, 1]
    pos = lax.dynamic_index_in_dim(pos.reshape(H, B, J, H, rows), ib, 1, keepdims=False)
    pos = jnp.where(ih == 0, pos[:, :, 0], pos[:, :, 1])
    pos = jnp.stack(in_order([pos[0], pos[1]], ih ^ it), 0)
    pos_all = pos.reshape(count)

    place = jnp.arange(T * J, dtype=jnp.int32)
    block_of = (it ^ (place // J)) * (B * J) + place % J
    row_of = jnp.arange(rows, dtype=jnp.int32)
    query_index = ((block_of + ib * J)[:, None] * rows + row_of[None, :]).reshape(count)
    key_index = (
        (block_of[None, :] + jnp.arange(B, dtype=jnp.int32)[:, None] * J)[..., None] * rows + row_of
    ).reshape(B * count)

    inverse = 1.0 / ROPE_BASE ** (jnp.arange(0, HEAD_DIM, 2, dtype=F32) / HEAD_DIM)
    if B == 1:
        inverse = jnp.tile(inverse, 2 * LANES // HEAD_DIM)
    angles = pos_all[:, None] * inverse[None, :]
    cosine = jnp.cos(angles)
    sine = jnp.sin(angles)

    valid_length = lax.dynamic_index_in_dim(lengths[:, 0], ih, 0, keepdims=False)
    at = jnp.stack([valid_length, it])
    ones = jnp.ones((HEAD_DIM,), F32)
    qk_gain = jnp.stack(
        [jnp.concatenate([q_gain, q_gain]).astype(F32), jnp.concatenate([k_gain.astype(F32), ones])]
    )
    half = after(half, wa, gains, cosine, sine, cot_own, at, qk_gain)
    with jax.named_scope("weights_ffn"):
        ffn_own = ffn_own.reshape(J * shard, 2 * ffn_width)
        if B > 1:
            ffn_own = lax.all_gather(ffn_own, "b", axis=0, tiled=True)
        w_a = [ffn_own[:, :ffn_width]]
        w_b = [ffn_own[:, ffn_width:]]
        w_a.append(swap(after(w_a[0], half), "h"))
        w_b.append(swap(after(w_b[0], w_a[1]), "h"))
        w_own = swap(after(ffn_own, half), "dp")
    with jax.named_scope("tokens_hidden"):
        hidden = [half, swap(half, "tp")]
    stream = hidden_own.astype(F32)

    attn_factor = norm_scale(stream)
    if B == 1:
        *normed, raw, qkv = qkv_call(*hidden, gain_attn[None], wa, qk_gain, cosine, sine)
        mixed, probs = attend_call(at, qkv)
    else:
        hidden = jnp.concatenate(hidden, 0).astype(F32)
        normed = (hidden * norm_scale(hidden) * gain_attn).astype(BF)
        cosine = jnp.concatenate([cosine, cosine], -1)[:, None, :]
        sine = jnp.concatenate([sine, sine], -1)[:, None, :]
        raw = mm(normed, wa[:, : qw + 2 * HEAD_DIM])
        normed = [normed[:side], normed[side:]]
        qk_raw = raw[:, : qw + HEAD_DIM].reshape(count, group + 1, HEAD_DIM)
        qk_gain = jnp.stack([q_gain] * group + [k_gain]).astype(F32)
        qk_factor = norm_scale(qk_raw)
        qk_normed = qk_raw * qk_factor * qk_gain
        qk = (qk_normed * cosine + half_turn(qk_normed) * sine).astype(BF)
        queries = qk[:, :group].transpose(1, 0, 2)
        keys = qk[:, group]
        values = raw[:, qw + HEAD_DIM :].astype(BF)
        if B > 1:
            keys = lax.all_gather(keys, "b", axis=0, tiled=True)
            values = lax.all_gather(values, "b", axis=0, tiled=True)
        visible = (key_index[None, :] <= query_index[:, None]) & (key_index[None, :] < valid_length)

        def scores_of(query_head):
            return jnp.where(visible, mm_nt(query_head, keys) * score_scale, MASKED)

        def attend(query_head):
            scores = scores_of(query_head)
            row_max = jnp.max(scores, -1, keepdims=True)
            exp_scores = jnp.exp(scores - row_max)
            row_total = jnp.sum(exp_scores, -1, keepdims=True)
            probs = (exp_scores / row_total).astype(BF)
            return mm(probs, values).astype(BF), row_max + jnp.log(row_total)

        heads = [attend(queries[g]) for g in range(group)]
        mixed = jnp.concatenate([h[0] for h in heads], -1)
    parts = share("tokens_cot", after(cot_own, half))
    mixed = after(mixed, w_a[1], w_own, *parts[1:])
    with jax.named_scope("tokens_cot"):
        cot_half = jnp.concatenate(in_order(parts, ij), 0)
    with jax.named_scope("sum_attn"):
        wo = wa[:, qw + 2 * HEAD_DIM :]
        low = swap(mm_nt(mixed[side:], wo).astype(BF), "tp")
        keep = mm_nt(mixed[:side], wo).astype(BF)
        parts = list(add_cut_call(ij[None], J, keep, low))
        for d in range(1, J):
            parts[d] = lax.ppermute(parts[d], "j", [(i, i ^ d) for i in range(J)])
        w_a.append(swap(w_a[1], "dp"))
        attn_branch = sum(p.astype(F32) for p in parts)

    middle = stream + attn_branch
    gain_ffn = after(gain_ffn, w_b[1], w_a[2])
    ffn_factor = norm_scale(middle)
    xf_own = (middle * ffn_factor * gain_ffn).astype(BF)
    ffn_half = gather_half("tokens_xf", xf_own)
    with jax.named_scope("weights_ffn"):
        w_b.append(swap(w_b[1], "dp"))
    ffn_half = after(ffn_half, w_b[2])
    ffn_in = [ffn_half, swap(ffn_half, "tp")]
    cot = [cot_half, swap(cot_half, "tp")]
    first = ffn_call(fw, ffn_in[0], cot[0], w_a, w_b, w_own)
    second = ffn_call(fw, after(ffn_in[1], first[0]), cot[1], w_a, w_b, w_own)
    hidden_act, grad_pre, grad_in, branch = zip(first, second)
    low = swap(grad_in[1], "tp")
    opposite, across_a, across_b = ffn_grad_call(
        2, ffn_width, True, ffn_in, cot, grad_pre, hidden_act
    )
    low = add(grad_in[0], after(low, across_b))
    with jax.named_scope("grads_ffn"):
        got_b, got_a = swap(across_b, "dp"), swap(across_a, "dp")
    near_a, near_b, beside_a, beside_b = ffn_grad_call(
        0, ffn_width, False, ffn_in, cot, grad_pre, hidden_act
    )
    grad_ffn_in = sum_tokens("sum_dxf", low)
    with jax.named_scope("sum_out"):
        low = add(branch[0], swap(branch[1], "tp"))
    gain_ffn = after(gain_ffn, got_b, near_a, low)

    grad_middle = cot_own.astype(F32) + norm_back(middle, ffn_factor, gain_ffn, grad_ffn_in)
    with jax.named_scope("grads_ffn"):
        beside_b = add(beside_b, got_b)
    half = jnp.concatenate(in_order(share("tokens_dattn", grad_middle.astype(BF)), ij), 0)
    with jax.named_scope("grads_ffn"):
        got_b = swap(beside_b, "h")
        beside_a = add(beside_a, got_a)
        half = after(half, got_b, beside_a)
        got_a = swap(beside_a, "h")
        opposite = swap(after(opposite, half), "dp")
    grad_attn = [half, swap(half, "tp")]
    with jax.named_scope("sum_out"):
        parts = lax.all_to_all(after(low, half).reshape(J, rows, d_model), "j", 0, 0)
    if B == 1:
        grad_raw, totals, *gives, keep = attend_back_call(
            at, qkv, mixed, probs, raw, *grad_attn, wa, qk_gain, cosine, sine
        )
        totals = jnp.concatenate([totals[0, :HEAD_DIM] + totals[0, HEAD_DIM:], totals[1, :HEAD_DIM]])
    else:
        grad_mixed = mm(jnp.concatenate(grad_attn, 0), wo).astype(BF)
        grad_keys = jnp.zeros((B * count, HEAD_DIM), F32)
        grad_values = jnp.zeros((B * count, HEAD_DIM), F32)
        grad_queries = []
        for g in range(group):
            probs = jnp.exp(scores_of(queries[g]) - heads[g][1])
            grad_head = grad_mixed[:, g * HEAD_DIM : (g + 1) * HEAD_DIM]
            grad_probs = mm_nt(grad_head, values)
            row_delta = jnp.sum(grad_probs * probs, -1, keepdims=True)
            grad_scores = (probs * (grad_probs - row_delta)).astype(BF)
            grad_queries.append(mm(grad_scores, keys) * score_scale)
            grad_keys = grad_keys + mm_tn(grad_scores, queries[g]) * score_scale
            grad_values = grad_values + mm_tn(probs.astype(BF), grad_head)
        if B > 1:
            grad_keys = lax.psum_scatter(grad_keys, "b", scatter_dimension=0, tiled=True)
            grad_values = lax.psum_scatter(grad_values, "b", scatter_dimension=0, tiled=True)
        grad_rot = jnp.stack(grad_queries + [grad_keys], 1)
        grad_normed = grad_rot * cosine + half_turn_back(grad_rot * sine)
        grad_qk_raw = norm_back(qk_raw, qk_factor, qk_gain, grad_normed)
        terms = jnp.sum(grad_normed * qk_raw * qk_factor, 0)
        totals = jnp.concatenate([jnp.sum(terms[:group], 0), terms[group]])
        grad_raw = jnp.concatenate(
            [grad_qk_raw.reshape(count, qw + HEAD_DIM), grad_values], 1
        ).astype(BF)
    if B > 1:
        w_qkv = wa[:, : qw + 2 * HEAD_DIM]
        gives = [mm_nt(g, w_qkv).astype(BF) for g in jnp.split(grad_raw[side:], 2)]
        keep = mm_nt(grad_raw[:side], w_qkv).astype(BF)
    grad_raw = after(grad_raw, got_a)
    gives = [swap(after(g, grad_raw), "tp") for g in gives]
    grads_attn = attn_grad_call(normed, grad_attn, grad_raw, mixed)
    gives[0] = after(gives[0], parts, *grads_attn[2:])
    gives[1] = after(gives[1], opposite)
    low = add_call(keep, *gives)
    grad_normed_own = sum_tokens("sum_dxa", low)
    total = jnp.sum(after(parts, low).astype(F32), 0)
    out_own = relative((middle + total).astype(BF))
    with jax.named_scope("grads_ffn"):
        pieces = [near_a, near_b, got_a, got_b, opposite]
        if B == 1:
            pieces = list(merge_call(ij[None], J, after(near_a, low), *pieces[1:]))
        else:
            near = jnp.concatenate([add(near_a, got_a), add(near_b, got_b)], 1)
            near = lax.psum_scatter(add(near, opposite), "b", scatter_dimension=0, tiled=True)
            near = near.reshape(J, shard, 2 * ffn_width)
            pieces = [lax.dynamic_index_in_dim(near, ij ^ d, 0, keepdims=False) for d in range(J)]
        for d in range(1, J):
            pieces[d] = lax.ppermute(pieces[d], "j", [(i, i ^ d) for i in range(J)])
    grad_stream = grad_middle + norm_back(stream, attn_factor, gain_attn, grad_normed_own)
    sent = jnp.stack([out_own, relative(grad_stream.astype(BF))])
    out_hidden, grad_hidden = give_back("return", sent)
    with jax.named_scope("grads_attn"):
        totals = jnp.pad(totals[None], ((0, 0), (0, wide - 2 * HEAD_DIM)))
        near, beside, opposed, across = grads_attn
        got = swap(jnp.concatenate([across, two_numbers(totals)], 0), "dp")
        got_near = swap(opposed, "dp")
        got = after(got, low)
        totals = totals + one_number(got[part:])
        beside = jnp.concatenate([add(beside, got[:part]), two_numbers(totals)], 0)
        got = swap(beside, "h")
        totals = totals + one_number(got[part:])
    with jax.named_scope("grads"):
        got = after(got, grad_normed_own)
        near = add(near.astype(F32) + got_near.astype(F32), got[:part])
        extra = two_numbers(totals[:, :LANES])
        extra = jnp.pad(extra, ((0, shard - extra.shape[0]), (0, 0)))
        extra = jnp.broadcast_to(extra[None], (B * J, shard, LANES))
        near = jnp.concatenate([near.reshape(B * J, shard, near.shape[1]), extra], 2)
        if B > 1:
            near = lax.psum_scatter(near, "b", scatter_dimension=0, tiled=True)
        shards = lax.all_to_all(near, "j", 0, 0)
    totals = jnp.sum(one_number(shards[:, :, -LANES:]), (0, 1))
    *shard_grads, sums = final_call(qw, fw, ij[None], shards, pieces, w_query, w_key, w_value, w_gate, w_up)

    sums = jnp.concatenate([totals, sums[:, 0], sums[:, 1]])
    sums = sums + swap(sums, "tp")
    totals = sums[: 2 * HEAD_DIM].reshape(2, HEAD_DIM)
    sums = sums[2 * HEAD_DIM :].reshape(2, shard) / jnp.stack([attn_gain, ffn_gain]).astype(F32)

    shard_query, shard_key, shard_value, shard_output, shard_gate, shard_up, shard_down = shard_grads
    return (
        out_hidden,
        grad_hidden,
        sums[0],
        shard_query,
        shard_key,
        shard_value,
        totals[0],
        totals[1],
        shard_output.T,
        sums[1],
        shard_gate,
        shard_up,
        shard_down.T,
    )


def solution(mesh):
    places = KV_HEADS // mesh.shape["tp"]

    def run(*args):
        micro = args[0].shape[0]
        shape = (mesh.shape["dp"], micro, mesh.shape["ctx"] // (micro * places), places)
        fine = Mesh(
            mesh.devices.reshape(*shape, mesh.shape["tp"]), ("dp", "h", "b", "j", "tp")
        )
        ctx = ("h", "b", "j")
        rows = ("dp", "h", "b", "j")
        tokens = P(None, "dp", ctx, None)
        return jax.shard_map(
            body,
            mesh=fine,
            in_specs=(
                tokens,
                P(None, "dp"),
                P(None, "dp", ctx),
                P(rows),
                P(rows, "tp"),
                P(rows, "tp"),
                P(rows, "tp"),
                P(),
                P(),
                P("tp", rows),
                P(rows),
                P(rows, "tp"),
                P(rows, "tp"),
                P("tp", rows),
                tokens,
            ),
            out_specs=(
                tokens,
                tokens,
                P(rows),
                P(rows, "tp"),
                P(rows, "tp"),
                P(rows, "tp"),
                P(),
                P(),
                P("tp", rows),
                P(rows),
                P(rows, "tp"),
                P(rows, "tp"),
                P("tp", rows),
            ),
            check_vma=False,
        )(*args)

    return run
```

```python
import functools

import jax
import jax.numpy as jnp
from jax import lax
from jax.experimental import pallas as pl
from jax.experimental.pallas import tpu as pltpu
from jax.sharding import Mesh, PartitionSpec as P

HEADS = 16
KV_HEADS = 8
HEAD_DIM = 64
EPSILON = 1e-05
ROPE_BASE = 1000000.0
MASKED = -1e30
BF = jnp.bfloat16
F32 = jnp.float32
VMEM_BYTES = 60 * 2**20
LANES = 128
SMALL_COST = pl.CostEstimate(flops=1, bytes_accessed=1, transcendentals=0)


def dot(a, b, dims):
    return lax.dot_general(a, b, (dims, ((), ())), preferred_element_type=F32)


def mm(a, b):
    return dot(a, b, ((1,), (0,)))


def mm_nt(a, b):
    return dot(a, b, ((1,), (1,)))


def mm_tn(a, b):
    return dot(a, b, ((0,), (0,)))


def nothing(*refs):
    pass


def after(value, *others):
    anywhere = pl.BlockSpec(memory_space=pl.ANY)
    return pl.pallas_call(
        nothing,
        in_specs=[anywhere] * (1 + len(others)),
        out_specs=anywhere,
        out_shape=jax.ShapeDtypeStruct(value.shape, value.dtype),
        input_output_aliases={0: 0},
        cost_estimate=SMALL_COST,
        name="after",
    )(value, *others)


def swap(v, axis):
    return lax.ppermute(v, axis, [(0, 1), (1, 0)])


def add(a, b):
    return (a.astype(F32) + b.astype(F32)).astype(BF)


def norm_scale(vector):
    return lax.rsqrt(jnp.mean(vector * vector, -1, keepdims=True) + EPSILON)


def norm_back(vector, factor, gain, upstream):
    weighted = upstream * gain
    return factor * weighted - vector * factor * factor * factor * jnp.mean(
        vector * weighted, -1, keepdims=True
    )


def half_turn(vector):
    middle_index = vector.shape[-1] // 2
    return jnp.concatenate([-vector[..., middle_index:], vector[..., :middle_index]], -1)


def half_turn_back(vector):
    middle_index = vector.shape[-1] // 2
    return jnp.concatenate([vector[..., middle_index:], -vector[..., :middle_index]], -1)


def in_order(parts, index):
    bit = 1
    while bit < len(parts):
        flag = (index & bit) != 0
        parts = [jnp.where(flag, parts[i ^ bit], parts[i]) for i in range(len(parts))]
        bit *= 2
    return parts


def row_sums(square, low):
    left = jnp.sum(jnp.where(low, square, 0.0), -1, keepdims=True)
    right = jnp.sum(jnp.where(low, 0.0, square), -1, keepdims=True)
    return jnp.where(low, left, right)


def pair_scale(pair, low):
    return lax.rsqrt(row_sums(pair * pair, low) * (1.0 / HEAD_DIM) + EPSILON)


def lanes(shape):
    return lax.broadcasted_iota(jnp.int32, shape, 1)


def turned(pair, first):
    width = pair.shape[1]
    quarter = HEAD_DIM // 2
    return jnp.where(first, pltpu.roll(pair, width - quarter, 1), pltpu.roll(pair, quarter, 1))


def qkv_kernel(half_tiles, h0_ref, h1_ref, gain_ref, w_ref, qk_gain_ref, cos_ref, sin_ref,
               xa0_ref, xa1_ref, raw_ref, qkv_ref):
    def run(h_ref, xa_ref):
        hidden = h_ref[...].astype(F32)
        factor = lax.rsqrt(jnp.mean(hidden * hidden, -1, keepdims=True) + EPSILON)
        xa = (hidden * factor * gain_ref[...]).astype(BF)
        xa_ref[...] = xa
        raw = mm(xa, w_ref[:, :256])
        raw_ref[...] = raw
        lane = lanes((raw.shape[0], 128))
        low = lane < HEAD_DIM
        first = lane % HEAD_DIM < HEAD_DIM // 2
        cosine, sine = cos_ref[...], sin_ref[...]
        sine = jnp.where(first, -sine, sine)
        for p in range(2):
            pair = raw[:, 128 * p : 128 * (p + 1)]
            normed = pair * pair_scale(pair, low) * qk_gain_ref[p : p + 1, :]
            turned_pair = normed * cosine + turned(normed, first) * sine
            if p == 1:
                turned_pair = jnp.where(low, turned_pair, pair)
            qkv_ref[:, 128 * p : 128 * (p + 1)] = turned_pair.astype(BF)

    @pl.when(pl.program_id(0) < half_tiles)
    def _():
        run(h0_ref, xa0_ref)

    @pl.when(pl.program_id(0) >= half_tiles)
    def _():
        run(h1_ref, xa1_ref)


def qkv_call(h0, h1, gain, w, qk_gain, cosine, sine):
    half, d_model = h0.shape
    tile = min(256, half)
    n = half // tile
    own = pl.BlockSpec((tile, d_model), lambda i: (jnp.minimum(i, n - 1), 0))
    other = pl.BlockSpec((tile, d_model), lambda i: (jnp.maximum(i - n, 0), 0))
    def fixed(a):
        return pl.BlockSpec(a.shape, lambda i: (0, 0))
    def rows(width):
        return pl.BlockSpec((tile, width), lambda i: (i, 0))
    return pl.pallas_call(
        functools.partial(qkv_kernel, n),
        grid=(2 * n,),
        in_specs=[own, other, fixed(gain), fixed(w), fixed(qk_gain), rows(128), rows(128)],
        out_specs=[own, other, rows(256), rows(256)],
        out_shape=[
            jax.ShapeDtypeStruct(h0.shape, BF),
            jax.ShapeDtypeStruct(h0.shape, BF),
            jax.ShapeDtypeStruct((2 * half, 256), F32),
            jax.ShapeDtypeStruct((2 * half, 256), BF),
        ],
        compiler_params=pltpu.CompilerParams(vmem_limit_bytes=VMEM_BYTES),
        cost_estimate=SMALL_COST,
        name="qkv",
    )(h0, h1, gain, w, qk_gain, cosine, sine)


def blocks_of(tiles):
    return [(a, k) for a in range(tiles) for k in range(a + 1)]


def stacked(pair):
    return jnp.concatenate([pair[:, :HEAD_DIM], pair[:, HEAD_DIM:]], 0)


def attend_kernel(tile, tiles, at_ref, qkv_ref, mixed_ref, probs_ref):
    half = tiles // 2
    def place(t):
        return pl.multiple_of((t + half * at_ref[1]) % tiles * tile, tile)
    for a in range(tiles):
        query = stacked(qkv_ref[pl.ds(place(a), tile), :128])
        row = lax.broadcasted_iota(jnp.int32, (2 * tile, 1), 0) % tile + a * tile
        limit = jnp.minimum(row + 1, at_ref[0])
        scores = []
        for k in range(a + 1):
            key = qkv_ref[pl.ds(place(k), tile), 128 : 128 + HEAD_DIM]
            column = lax.broadcasted_iota(jnp.int32, (1, tile), 1) + k * tile
            scores.append(
                jnp.where(column < limit, mm_nt(query, key) * HEAD_DIM ** (-0.5), MASKED)
            )
        peak = functools.reduce(jnp.maximum, [jnp.max(s, -1, keepdims=True) for s in scores])
        exps = [jnp.exp(s - peak) for s in scores]
        total = functools.reduce(jnp.add, [jnp.sum(e, -1, keepdims=True) for e in exps])
        inverse = 1.0 / total
        mixed = 0.0
        for k in range(a + 1):
            probs = (exps[k] * inverse).astype(BF)
            probs_ref[blocks_of(tiles).index((a, k))] = probs
            value = qkv_ref[pl.ds(place(k), tile), 128 + HEAD_DIM :]
            mixed = mixed + mm(probs, value)
        mixed_ref[pl.ds(place(a), tile), :] = jnp.concatenate(
            [mixed[:tile], mixed[tile:]], 1
        ).astype(BF)


def attend_call(at, qkv):
    count = qkv.shape[0]
    tile = min(256, count // 2)
    tiles = count // tile
    pairs = len(blocks_of(tiles))
    return pl.pallas_call(
        functools.partial(attend_kernel, tile, tiles),
        in_specs=[pl.BlockSpec(memory_space=pltpu.SMEM), pl.BlockSpec(memory_space=pltpu.VMEM)],
        out_specs=[pl.BlockSpec(memory_space=pltpu.VMEM)] * 2,
        out_shape=[
            jax.ShapeDtypeStruct((count, 128), BF),
            jax.ShapeDtypeStruct((pairs, 2 * tile, tile), BF),
        ],
        compiler_params=pltpu.CompilerParams(vmem_limit_bytes=VMEM_BYTES),
        cost_estimate=SMALL_COST,
        name="attend",
    )(at, qkv)


def attend_back_kernel(tile, tiles, at_ref, qkv_ref, mixed_ref, probs_ref, raw_ref, g0_ref, g1_ref,
                       wa_ref, qk_gain_ref, cos_ref, sin_ref, out_ref, total_ref, give0_ref,
                       give1_ref, keep_ref, dm_ref, dkv_ref):
    half = tiles // 2
    def place(t):
        return pl.multiple_of((t + half * at_ref[1]) % tiles * tile, tile)
    rows = half * tile
    wide = out_ref.shape[1]
    dm_ref[:rows] = mm(g0_ref[...], wa_ref[:, wide:]).astype(BF)
    dm_ref[rows:] = mm(g1_ref[...], wa_ref[:, wide:]).astype(BF)
    scale = HEAD_DIM ** (-0.5)
    lane = lanes((tile, 128))
    low = lane < HEAD_DIM
    first = lane % HEAD_DIM < HEAD_DIM // 2

    def finish(t, p, grad):
        at = pl.ds(place(t), tile)
        cosine, sine = cos_ref[at], sin_ref[at]
        pair = raw_ref[at, 128 * p : 128 * (p + 1)]
        factor = pair_scale(pair, low)
        signed = grad * jnp.where(first, -sine, sine)
        upstream = grad * cosine + turned(signed, first)
        gain = qk_gain_ref[p : p + 1, :]
        weighted = upstream * gain
        mean = row_sums(pair * weighted, low) * (1.0 / HEAD_DIM)
        result = factor * weighted - pair * (factor * factor * factor * mean)
        terms = jnp.sum(upstream * pair * factor, 0, keepdims=True)
        if p == 1:
            result = jnp.where(low, result, grad)
        out_ref[at, 128 * p : 128 * (p + 1)] = result.astype(BF)
        total_ref[p : p + 1, :] += terms

    total_ref[...] = jnp.zeros_like(total_ref)
    dkv = [0.0] * tiles
    for a in range(tiles):
        at = pl.ds(place(a), tile)
        query = stacked(qkv_ref[at, :128])
        grad = stacked(dm_ref[at])
        mixed = stacked(mixed_ref[at, :])
        delta = jnp.sum(grad.astype(F32) * mixed.astype(F32), -1, keepdims=True)
        grad_query = 0.0
        for k in range(a + 1):
            keys = pl.ds(place(k), tile)
            key = qkv_ref[keys, 128 : 128 + HEAD_DIM]
            value = qkv_ref[keys, 128 + HEAD_DIM :]
            probs = probs_ref[blocks_of(tiles).index((a, k))]
            grad_scores = (probs.astype(F32) * (mm_nt(grad, value) - delta)).astype(BF)
            grad_query = grad_query + mm(grad_scores, key)
            grad_kv = jnp.concatenate(
                [mm_tn(grad_scores, query) * scale, mm_tn(probs, grad)], 1
            )
            if a == k:
                dkv_ref[k] = grad_kv
            else:
                dkv_ref[k] += grad_kv
        grad_query = grad_query * scale
        finish(a, 0, jnp.concatenate([grad_query[:tile], grad_query[tile:]], 1))
    for k in range(tiles):
        finish(k, 1, dkv_ref[k])
    w = wa_ref[:, :wide]
    middle = rows + rows // 2
    give0_ref[...] = mm_nt(out_ref[rows:middle], w).astype(BF)
    give1_ref[...] = mm_nt(out_ref[middle:], w).astype(BF)
    keep_ref[...] = mm_nt(out_ref[:rows], w).astype(BF)


def attend_back_call(at, qkv, mixed, probs, raw, g0, g1, wa, qk_gain, cosine, sine):
    count, d_model = qkv.shape[0], g0.shape[1]
    tile = min(256, count // 2)
    tiles = count // tile
    vmem = pl.BlockSpec(memory_space=pltpu.VMEM)
    return pl.pallas_call(
        functools.partial(attend_back_kernel, tile, tiles),
        in_specs=[pl.BlockSpec(memory_space=pltpu.SMEM)] + [vmem] * 10,
        out_specs=[vmem] * 5,
        out_shape=[
            jax.ShapeDtypeStruct((count, 256), BF),
            jax.ShapeDtypeStruct((8, 128), F32),
            jax.ShapeDtypeStruct((count // 4, d_model), BF),
            jax.ShapeDtypeStruct((count // 4, d_model), BF),
            jax.ShapeDtypeStruct((count // 2, d_model), BF),
        ],
        scratch_shapes=[pltpu.VMEM((count, 128), BF), pltpu.VMEM((tiles, tile, 128), F32)],
        compiler_params=pltpu.CompilerParams(vmem_limit_bytes=VMEM_BYTES),
        cost_estimate=SMALL_COST,
        name="attend_back",
    )(at, qkv, mixed, probs, raw, g0, g1, wa, qk_gain, cosine, sine)


def ffn_kernel(fw, part, x_ref, cot_ref, *refs):
    a_refs, b_refs, (w_ref, act_ref, grad_ref, grad_in_ref, out_ref) = refs[:3], refs[3:6], refs[6:]
    width = a_refs[0].shape[1]
    a_refs = [*a_refs[:2], w_ref.at[:, :width], a_refs[2]]
    b_refs = [*b_refs[:2], w_ref.at[:, width:], b_refs[2]]
    rest = 2 * fw - width
    pre_a, pre_b, grad_act = 0.0, 0.0, 0.0
    for p in range(4):
        cut = slice(p * part, (p + 1) * part)
        pre_a = pre_a + mm(x_ref[:, cut], a_refs[p][...])
        pre_b = pre_b + mm(x_ref[:, cut], b_refs[p][:, :rest])
        grad_act = grad_act + mm(cot_ref[:, cut], b_refs[p][:, rest : rest + fw])
    pre = jnp.concatenate([pre_a, pre_b], 1)
    gate, up = pre[:, :fw], pre[:, fw:]
    sigmoid = 1.0 / (1.0 + jnp.exp(-gate))
    silu = gate * sigmoid
    act = (silu * up).astype(BF)
    act_ref[...] = act
    grad_gate = grad_act * up * sigmoid * (1.0 + gate * (1.0 - sigmoid))
    grad = jnp.concatenate([grad_gate, grad_act * silu], 1).astype(BF)
    grad_ref[...] = grad
    for p in range(4):
        cut = slice(p * part, (p + 1) * part)
        grad_in = mm_nt(grad[:, :width], a_refs[p][...])
        grad_in = grad_in + mm_nt(grad[:, width:], b_refs[p][:, :rest])
        grad_in_ref[:, cut] = grad_in.astype(BF)
        out_ref[:, cut] = mm_nt(act, b_refs[p][:, rest : rest + fw]).astype(BF)


def ffn_call(fw, x, cot, w_a, w_b, w_own):
    count, d_model = x.shape
    part = w_a[0].shape[0]
    tile = min(256, count)
    shapes = [(count, fw), (count, 2 * fw), (count, d_model), (count, d_model)]
    return pl.pallas_call(
        functools.partial(ffn_kernel, fw, part),
        grid=(count // tile,),
        in_specs=[
            pl.BlockSpec((tile, d_model), lambda i: (i, 0)),
            pl.BlockSpec((tile, d_model), lambda i: (i, 0)),
        ]
        + [pl.BlockSpec(p.shape, lambda i: (0, 0)) for p in (*w_a, *w_b, w_own)],
        out_specs=[pl.BlockSpec((tile, s[1]), lambda i: (i, 0)) for s in shapes],
        out_shape=[jax.ShapeDtypeStruct(s, BF) for s in shapes],
        compiler_params=pltpu.CompilerParams(vmem_limit_bytes=VMEM_BYTES),
        cost_estimate=SMALL_COST,
        name="ffn",
    )(x, cot, *w_a, *w_b, w_own)


def ffn_grad_kernel(fw, width, whole, *refs):
    ins, outs = refs[:8], refs[8:]
    x0, x1, cot0, cot1, grad0, grad1, act0, act1 = (r[...] for r in ins)
    grad_in = (mm_tn(x0, grad0) + mm_tn(x1, grad1)).astype(BF)
    grad_out = (mm_tn(cot0, act0) + mm_tn(cot1, act1)).astype(BF)
    rest = 2 * fw - width

    def write(a_ref, b_ref):
        a_ref[...] = grad_in[:, :width]
        b_ref[:, :rest] = grad_in[:, width:]
        b_ref[:, rest : rest + fw] = grad_out
        left = width - rest - fw
        if left:
            b_ref[:, rest + fw :] = jnp.zeros((grad_out.shape[0], left), BF)

    @pl.when(pl.program_id(0) == 0)
    def _():
        if whole:
            write(outs[0].at[:, :width], outs[0].at[:, width:])
        else:
            write(*outs[:2])

    @pl.when(pl.program_id(0) == 1)
    def _():
        write(*outs[-2:])


def ffn_grad_call(p, width, whole, x, cot, grad, act):
    count, d_model = x[0].shape
    fw = act[0].shape[1]
    part = d_model // 4
    columns = pl.BlockSpec((count, part), lambda i: (0, p + i))
    operands = [pl.BlockSpec(a.shape, lambda i: (0, 0)) for a in (*grad, *act)]
    shapes = ([(part, 2 * width)] if whole else [(part, width)] * 2) + [(part, width)] * 2
    return pl.pallas_call(
        functools.partial(ffn_grad_kernel, fw, width, whole),
        grid=(2,),
        in_specs=[columns] * 4 + operands,
        out_specs=[pl.BlockSpec(s, lambda i: (0, 0)) for s in shapes],
        out_shape=[jax.ShapeDtypeStruct(s, BF) for s in shapes],
        compiler_params=pltpu.CompilerParams(vmem_limit_bytes=VMEM_BYTES),
        cost_estimate=SMALL_COST,
        name="ffn_grad",
    )(*x, *cot, *grad, *act)


def add_kernel(keep_ref, got0_ref, got1_ref, out_ref):
    rows = got0_ref.shape[0]
    out_ref[:rows] = (keep_ref[:rows].astype(F32) + got0_ref[...].astype(F32)).astype(BF)
    out_ref[rows:] = (keep_ref[rows:].astype(F32) + got1_ref[...].astype(F32)).astype(BF)


def add_call(keep, got0, got1):
    vmem = pl.BlockSpec(memory_space=pltpu.VMEM)
    return pl.pallas_call(
        add_kernel,
        in_specs=[vmem] * 3,
        out_specs=vmem,
        out_shape=jax.ShapeDtypeStruct(keep.shape, BF),
        compiler_params=pltpu.CompilerParams(vmem_limit_bytes=VMEM_BYTES),
        cost_estimate=SMALL_COST,
        name="add",
    )(keep, got0, got1)


def add_cut_kernel(place_ref, a_ref, b_ref, *outs):
    height = outs[0].shape[0]
    for d, out_ref in enumerate(outs):
        at = pl.ds(pl.multiple_of((place_ref[0] ^ d) * height, height), height)
        out_ref[...] = (a_ref[at, :].astype(F32) + b_ref[at, :].astype(F32)).astype(BF)


def add_cut_call(place, places, a, b):
    vmem = pl.BlockSpec(memory_space=pltpu.VMEM)
    shape = jax.ShapeDtypeStruct((a.shape[0] // places, a.shape[1]), BF)
    return pl.pallas_call(
        add_cut_kernel,
        in_specs=[pl.BlockSpec(memory_space=pltpu.SMEM)] + [vmem] * 2,
        out_specs=[vmem] * places,
        out_shape=[shape] * places,
        compiler_params=pltpu.CompilerParams(vmem_limit_bytes=VMEM_BYTES),
        cost_estimate=SMALL_COST,
        name="add_cut",
    )(place, a, b)


def pack_kernel(qw, wq_ref, wk_ref, wv_ref, wo_ref, g0_ref, g1_ref, pos_ref, out_ref):
    places, height, wide = out_ref.shape
    shard = wq_ref.shape[0]

    def row(*parts):
        parts = [p.astype(F32) for p in parts]
        parts.append(jnp.zeros((1, wide - sum(p.shape[1] for p in parts)), F32))
        return jnp.concatenate(parts, 1)

    pos = pos_ref[...]
    high = lax.shift_right_logical(pos, 8)
    low = pos - high * 256
    index = lax.broadcasted_iota(jnp.int32, (height - shard, wide), 0)
    extra = jnp.where(index == 0, row(g0_ref[...], g1_ref[...]), 0.0)
    for n, part in ((1, high), (2, low)):
        extra = jnp.where(index == n, row(*(part[m : m + 1] for m in range(part.shape[0]))), extra)
    extra = extra.astype(BF)
    for p in range(places):
        wide_at = slice(p * qw, (p + 1) * qw)
        at = slice(p * HEAD_DIM, (p + 1) * HEAD_DIM)
        out_ref[p, :shard, :qw] = wq_ref[:, wide_at]
        out_ref[p, :shard, qw : qw + 2 * HEAD_DIM] = jnp.concatenate(
            [wk_ref[:, at], wv_ref[:, at]], 1
        )
        out_ref[p, :shard, qw + 2 * HEAD_DIM :] = wo_ref[:, wide_at]
        out_ref[p, shard:, :] = extra


def pack_call(qw, places, wide, *arrays):
    vmem = pl.BlockSpec(memory_space=pltpu.VMEM)
    return pl.pallas_call(
        functools.partial(pack_kernel, qw),
        in_specs=[vmem] * 7,
        out_specs=vmem,
        out_shape=jax.ShapeDtypeStruct((places, arrays[0].shape[0] + 8, wide), BF),
        compiler_params=pltpu.CompilerParams(vmem_limit_bytes=VMEM_BYTES),
        cost_estimate=SMALL_COST,
        name="pack",
    )(*arrays)


def attn_grad_kernel(x0_ref, x1_ref, g0_ref, g1_ref, raw_ref, mixed_ref, *outs):
    side = x0_ref.shape[0]
    wide = raw_ref.shape[1]
    grad_qkv = mm_tn(x0_ref[...], raw_ref[:side]) + mm_tn(x1_ref[...], raw_ref[side:])
    grad_o = mm_tn(g0_ref[...], mixed_ref[:side]) + mm_tn(g1_ref[...], mixed_ref[side:])
    for p in range(4):

        @pl.when(pl.program_id(0) == p)
        def _():
            outs[p][:, :wide] = grad_qkv.astype(BF)
            outs[p][:, wide:] = grad_o.astype(BF)


def attn_grad_call(x, g, raw, mixed):
    count, d_model = x[0].shape
    part = d_model // 4
    shape = (part, raw.shape[1] + mixed.shape[1])
    columns = pl.BlockSpec((count, part), lambda i: (0, i))
    return pl.pallas_call(
        attn_grad_kernel,
        grid=(4,),
        in_specs=[columns] * 4 + [pl.BlockSpec(a.shape, lambda i: (0, 0)) for a in (raw, mixed)],
        out_specs=[pl.BlockSpec(shape, lambda i: (0, 0))] * 4,
        out_shape=[jax.ShapeDtypeStruct(shape, BF)] * 4,
        compiler_params=pltpu.CompilerParams(vmem_limit_bytes=VMEM_BYTES),
        cost_estimate=SMALL_COST,
        name="attn_grad",
    )(*x, *g, raw, mixed)


def merge_kernel(place_ref, near_a, near_b, got_a, got_b, opposite, *outs):
    height, width = outs[0].shape[0], near_a.shape[1]
    for d, out_ref in enumerate(outs):
        at = pl.ds(pl.multiple_of((place_ref[0] ^ d) * height, height), height)
        for near, got, start in ((near_a, got_a, 0), (near_b, got_b, width)):
            total = near[at, :].astype(F32) + got[at, :].astype(F32)
            total = total + opposite[at, start : start + width].astype(F32)
            out_ref[:, start : start + width] = total.astype(BF)


def merge_call(place, places, *arrays):
    rows, width = arrays[0].shape
    shape = jax.ShapeDtypeStruct((rows // places, 2 * width), BF)
    vmem = pl.BlockSpec(memory_space=pltpu.VMEM)
    return pl.pallas_call(
        merge_kernel,
        in_specs=[pl.BlockSpec(memory_space=pltpu.SMEM)] + [vmem] * 5,
        out_specs=[vmem] * places,
        out_shape=[shape] * places,
        compiler_params=pltpu.CompilerParams(vmem_limit_bytes=VMEM_BYTES),
        cost_estimate=SMALL_COST,
        name="merge",
    )(place, *arrays)


def final_kernel(
    qw, fw, place_ref, got_ref, p0_ref, p1_ref, p2_ref, p3_ref, wq_ref, wk_ref, wv_ref, wg_ref, wu_ref,
    q_ref, k_ref, v_ref, o_ref, gate_ref, up_ref, down_ref, sum_ref,
):
    places = got_ref.shape[0]

    def side_by_side(start, width):
        return jnp.concatenate(
            [got_ref[p, :, start : start + width] for p in range(places)], 1
        ).astype(F32)

    def rows(weight_ref, grad):
        return jnp.sum(weight_ref[...].astype(F32) * grad, 1, keepdims=True)

    query, key, value = side_by_side(0, qw), side_by_side(qw, HEAD_DIM), side_by_side(qw + HEAD_DIM, HEAD_DIM)
    q_ref[...], k_ref[...], v_ref[...] = query, key, value
    sum_attn = rows(wq_ref, query) + rows(wk_ref, key) + rows(wv_ref, value)
    start = qw + 2 * HEAD_DIM
    o_ref[...] = side_by_side(start, qw)
    pieces = in_order([r[...].astype(F32) for r in (p0_ref, p1_ref, p2_ref, p3_ref)], place_ref[0])
    gate, up, down = (
        jnp.concatenate([p[:, n * fw : (n + 1) * fw] for p in pieces], 1) for n in range(3)
    )
    gate_ref[...], up_ref[...] = gate, up
    sum_ffn = rows(wg_ref, gate) + rows(wu_ref, up)
    down_ref[...] = down
    lane = lanes(sum_ref.shape)
    sum_ref[...] = jnp.where(lane == 0, sum_attn, sum_ffn)


def final_call(qw, fw, place, got, pieces, wq, wk, wv, wg, wu):
    shard = got.shape[1]
    vmem = pl.BlockSpec(memory_space=pltpu.VMEM)
    shapes = [wq.shape, wk.shape, wv.shape, wq.shape, wg.shape, wu.shape, wg.shape]
    shapes.append((shard, LANES))
    return pl.pallas_call(
        functools.partial(final_kernel, qw, fw),
        in_specs=[pl.BlockSpec(memory_space=pltpu.SMEM)] + [vmem] * 10,
        out_specs=[vmem] * 8,
        out_shape=[jax.ShapeDtypeStruct(s, F32) for s in shapes],
        compiler_params=pltpu.CompilerParams(vmem_limit_bytes=VMEM_BYTES),
        cost_estimate=SMALL_COST,
        name="final",
    )(place, got, *pieces, wq, wk, wv, wg, wu)


def body(
    hidden_in,
    lengths,
    positions,
    attn_gain,
    w_query,
    w_key,
    w_value,
    q_gain,
    k_gain,
    w_output,
    ffn_gain,
    w_gate,
    w_up,
    w_down,
    grad_out,
):
    H, B, J, T = (lax.axis_size(a) for a in ("h", "b", "j", "tp"))
    ix, ih, ib, ij, it = (lax.axis_index(a) for a in ("dp", "h", "b", "j", "tp"))
    rows = hidden_in.shape[2]
    d_model = hidden_in.shape[3]
    shard = w_query.shape[0]
    group = HEADS // KV_HEADS
    qw = group * HEAD_DIM
    fw = w_gate.shape[1] // J
    count = T * J * rows
    side = J * rows
    ffn_width = -(-3 * fw // (2 * LANES)) * LANES
    score_scale = HEAD_DIM ** (-0.5)
    quarter = 2 * ix + ih
    part = d_model // 4

    def cut(array, p, width):
        return array[:, p * width : (p + 1) * width]

    def exchange(name, pieces):
        with jax.named_scope(name):
            return lax.all_to_all(pieces, "j", 0, 0)

    def exchange_beside(name, pieces):
        with jax.named_scope(name):
            pieces = in_order(pieces, ij)
            parts = [pieces[0]]
            for d in range(1, J):
                parts.append(lax.ppermute(pieces[d], "j", [(i, i ^ d) for i in range(J)]))
            return parts

    def two_numbers(values):
        high = values.astype(BF)
        low = (values - high.astype(F32)).astype(BF)
        return jnp.pad(jnp.concatenate([high, low], 0), ((0, 6), (0, 0)))

    def one_number(block):
        return block[..., 0:1, :].astype(F32) + block[..., 1:2, :].astype(F32)

    def relative(array):
        pieces = [array[..., p * part : (p + 1) * part] for p in range(4)]
        return jnp.concatenate(in_order(pieces, quarter), -1)

    turn = [(0, 0), (1, 2), (2, 1), (3, 3)]

    def fetch(name, array, *others):
        with jax.named_scope(name):
            mine = lax.dynamic_index_in_dim(array, it, 0, keepdims=False)[0]
            if others:
                mine = after(mine, *others)
            return lax.ppermute(mine, ("h", "tp"), turn)

    def give_back(name, block):
        with jax.named_scope(name):
            mine = lax.ppermute(block, ("h", "tp"), turn)
            both = in_order([mine, swap(mine, "tp")], it)
            return [jnp.stack([b[n] for b in both])[:, None] for n in range(block.shape[0])]

    def gather_half(name, block, *others):
        with jax.named_scope(name):
            sent = jnp.broadcast_to(block[None], (J, *block.shape))
            if others:
                sent = after(sent, *others)
            return lax.all_to_all(sent, "j", 0, 0).reshape(side, d_model)

    def sum_tokens(name, half, *others):
        with jax.named_scope(name):
            got = lax.all_to_all(half.reshape(J, rows, d_model), "j", 0, 0)
            if others:
                got = after(got, *others)
            return jnp.sum(got.astype(F32), 0)

    w_output_t = w_output.T
    w_down_t = w_down.T
    wide = 2 * qw + 2 * HEAD_DIM
    gains = attn_gain[None], ffn_gain[None]
    sent = pack_call(
        qw, J, wide, w_query, w_key, w_value, w_output_t, *gains, positions.reshape(H, rows)
    )
    own = exchange("weights_attn", sent)
    pack = [
        jnp.pad(
            jnp.concatenate([cut(w_gate, p, fw), cut(w_up, p, fw), cut(w_down_t, p, fw)], 1),
            ((0, 0), (0, 2 * ffn_width - 3 * fw)),
        )
        for p in range(J)
    ]
    ffn_own = exchange("weights_ffn", jnp.stack(pack))
    hidden_own = relative(fetch("fetch_hidden", hidden_in))

    def share(name, block):
        with jax.named_scope(name):
            return [block] + [
                lax.ppermute(block, "j", [(i, i ^ d) for i in range(J)]) for d in range(1, J)
            ]

    with jax.named_scope("weights_attn"):
        if B > 1:
            own = lax.all_gather(own, "b", axis=0, tiled=True)
        beside = swap(own, "h")
        opposite = swap(own, "dp")
    half = gather_half("tokens_hidden", hidden_own, ffn_own)
    with jax.named_scope("weights_attn"):
        across = swap(beside, "dp")
    cot_own = relative(fetch("fetch_cot", grad_out, beside))
    with jax.named_scope("weights_attn"):
        parts = [own, beside, opposite, across]
        wa = jnp.stack([p[:, :shard] for p in parts]).reshape(d_model, wide)
        extra = jnp.stack([p[:, shard : shard + 3] for p in parts])
    gains = extra[:, :, 0, : 2 * shard].reshape(4, B * J, 2, shard)
    gains = gains.transpose(2, 0, 1, 3).reshape(2, d_model).astype(F32)
    gain_attn = gains[0]
    gain_ffn = gains[1]
    pos = extra[:2, :, 1:, : H * rows].astype(F32)
    pos = pos[:, :, 0] * 256.0 + pos[:, :, 1]
    pos = lax.dynamic_index_in_dim(pos.reshape(H, B, J, H, rows), ib, 1, keepdims=False)
    pos = jnp.where(ih == 0, pos[:, :, 0], pos[:, :, 1])
    pos = jnp.stack(in_order([pos[0], pos[1]], ih ^ it), 0)
    pos_all = pos.reshape(count)

    place = jnp.arange(T * J, dtype=jnp.int32)
    block_of = (it ^ (place // J)) * (B * J) + place % J
    row_of = jnp.arange(rows, dtype=jnp.int32)
    query_index = ((block_of + ib * J)[:, None] * rows + row_of[None, :]).reshape(count)
    key_index = (
        (block_of[None, :] + jnp.arange(B, dtype=jnp.int32)[:, None] * J)[..., None] * rows + row_of
    ).reshape(B * count)

    inverse = 1.0 / ROPE_BASE ** (jnp.arange(0, HEAD_DIM, 2, dtype=F32) / HEAD_DIM)
    if B == 1:
        inverse = jnp.tile(inverse, 2 * LANES // HEAD_DIM)
    angles = pos_all[:, None] * inverse[None, :]
    cosine = jnp.cos(angles)
    sine = jnp.sin(angles)

    valid_length = lax.dynamic_index_in_dim(lengths[:, 0], ih, 0, keepdims=False)
    at = jnp.stack([valid_length, it])
    ones = jnp.ones((HEAD_DIM,), F32)
    qk_gain = jnp.stack(
        [jnp.concatenate([q_gain, q_gain]).astype(F32), jnp.concatenate([k_gain.astype(F32), ones])]
    )
    half = after(half, wa, gains, cosine, sine, cot_own, at, qk_gain)
    with jax.named_scope("weights_ffn"):
        ffn_own = ffn_own.reshape(J * shard, 2 * ffn_width)
        if B > 1:
            ffn_own = lax.all_gather(ffn_own, "b", axis=0, tiled=True)
        w_a = [ffn_own[:, :ffn_width]]
        w_b = [ffn_own[:, ffn_width:]]
        w_a.append(swap(after(w_a[0], half), "h"))
        w_b.append(swap(after(w_b[0], w_a[1]), "h"))
        w_own = swap(after(ffn_own, half), "dp")
    with jax.named_scope("tokens_hidden"):
        hidden = [half, swap(half, "tp")]
    stream = hidden_own.astype(F32)

    attn_factor = norm_scale(stream)
    if B == 1:
        *normed, raw, qkv = qkv_call(*hidden, gain_attn[None], wa, qk_gain, cosine, sine)
        mixed, probs = attend_call(at, qkv)
    else:
        hidden = jnp.concatenate(hidden, 0).astype(F32)
        normed = (hidden * norm_scale(hidden) * gain_attn).astype(BF)
        cosine = jnp.concatenate([cosine, cosine], -1)[:, None, :]
        sine = jnp.concatenate([sine, sine], -1)[:, None, :]
        raw = mm(normed, wa[:, : qw + 2 * HEAD_DIM])
        normed = [normed[:side], normed[side:]]
        qk_raw = raw[:, : qw + HEAD_DIM].reshape(count, group + 1, HEAD_DIM)
        qk_gain = jnp.stack([q_gain] * group + [k_gain]).astype(F32)
        qk_factor = norm_scale(qk_raw)
        qk_normed = qk_raw * qk_factor * qk_gain
        qk = (qk_normed * cosine + half_turn(qk_normed) * sine).astype(BF)
        queries = qk[:, :group].transpose(1, 0, 2)
        keys = qk[:, group]
        values = raw[:, qw + HEAD_DIM :].astype(BF)
        if B > 1:
            keys = lax.all_gather(keys, "b", axis=0, tiled=True)
            values = lax.all_gather(values, "b", axis=0, tiled=True)
        visible = (key_index[None, :] <= query_index[:, None]) & (key_index[None, :] < valid_length)

        def scores_of(query_head):
            return jnp.where(visible, mm_nt(query_head, keys) * score_scale, MASKED)

        def attend(query_head):
            scores = scores_of(query_head)
            row_max = jnp.max(scores, -1, keepdims=True)
            exp_scores = jnp.exp(scores - row_max)
            row_total = jnp.sum(exp_scores, -1, keepdims=True)
            probs = (exp_scores / row_total).astype(BF)
            return mm(probs, values).astype(BF), row_max + jnp.log(row_total)

        heads = [attend(queries[g]) for g in range(group)]
        mixed = jnp.concatenate([h[0] for h in heads], -1)
    parts = share("tokens_cot", after(cot_own, half))
    mixed = after(mixed, w_a[1], w_own, *parts[1:])
    with jax.named_scope("tokens_cot"):
        cot_half = jnp.concatenate(in_order(parts, ij), 0)
    with jax.named_scope("sum_attn"):
        wo = wa[:, qw + 2 * HEAD_DIM :]
        low = swap(mm_nt(mixed[side:], wo).astype(BF), "tp")
        keep = mm_nt(mixed[:side], wo).astype(BF)
        parts = list(add_cut_call(ij[None], J, keep, low))
        for d in range(1, J):
            parts[d] = lax.ppermute(parts[d], "j", [(i, i ^ d) for i in range(J)])
        w_a.append(swap(w_a[1], "dp"))
        attn_branch = sum(p.astype(F32) for p in parts)

    middle = stream + attn_branch
    gain_ffn = after(gain_ffn, w_b[1], w_a[2])
    ffn_factor = norm_scale(middle)
    xf_own = (middle * ffn_factor * gain_ffn).astype(BF)
    ffn_half = gather_half("tokens_xf", xf_own)
    with jax.named_scope("weights_ffn"):
        w_b.append(swap(w_b[1], "dp"))
    ffn_half = after(ffn_half, w_b[2])
    ffn_in = [ffn_half, swap(ffn_half, "tp")]
    cot = [cot_half, swap(cot_half, "tp")]
    first = ffn_call(fw, ffn_in[0], cot[0], w_a, w_b, w_own)
    second = ffn_call(fw, after(ffn_in[1], first[0]), cot[1], w_a, w_b, w_own)
    hidden_act, grad_pre, grad_in, branch = zip(first, second)
    low = swap(grad_in[1], "tp")
    opposite, across_a, across_b = ffn_grad_call(
        2, ffn_width, True, ffn_in, cot, grad_pre, hidden_act
    )
    low = add(grad_in[0], after(low, across_b))
    with jax.named_scope("grads_ffn"):
        got_b, got_a = swap(across_b, "dp"), swap(across_a, "dp")
    near_a, near_b, beside_a, beside_b = ffn_grad_call(
        0, ffn_width, False, ffn_in, cot, grad_pre, hidden_act
    )
    grad_ffn_in = sum_tokens("sum_dxf", low)
    with jax.named_scope("sum_out"):
        low = add(branch[0], swap(branch[1], "tp"))
    gain_ffn = after(gain_ffn, got_b, near_a, low)

    grad_middle = cot_own.astype(F32) + norm_back(middle, ffn_factor, gain_ffn, grad_ffn_in)
    with jax.named_scope("grads_ffn"):
        beside_b = add(beside_b, got_b)
    half = jnp.concatenate(in_order(share("tokens_dattn", grad_middle.astype(BF)), ij), 0)
    with jax.named_scope("grads_ffn"):
        got_b = swap(beside_b, "h")
        beside_a = add(beside_a, got_a)
        half = after(half, got_b, beside_a)
        got_a = swap(beside_a, "h")
        opposite = swap(after(opposite, half), "dp")
    grad_attn = [half, swap(half, "tp")]
    with jax.named_scope("sum_out"):
        parts = lax.all_to_all(after(low, half).reshape(J, rows, d_model), "j", 0, 0)
    if B == 1:
        grad_raw, totals, *gives, keep = attend_back_call(
            at, qkv, mixed, probs, raw, *grad_attn, wa, qk_gain, cosine, sine
        )
        totals = jnp.concatenate([totals[0, :HEAD_DIM] + totals[0, HEAD_DIM:], totals[1, :HEAD_DIM]])
    else:
        grad_mixed = mm(jnp.concatenate(grad_attn, 0), wo).astype(BF)
        grad_keys = jnp.zeros((B * count, HEAD_DIM), F32)
        grad_values = jnp.zeros((B * count, HEAD_DIM), F32)
        grad_queries = []
        for g in range(group):
            probs = jnp.exp(scores_of(queries[g]) - heads[g][1])
            grad_head = grad_mixed[:, g * HEAD_DIM : (g + 1) * HEAD_DIM]
            grad_probs = mm_nt(grad_head, values)
            row_delta = jnp.sum(grad_probs * probs, -1, keepdims=True)
            grad_scores = (probs * (grad_probs - row_delta)).astype(BF)
            grad_queries.append(mm(grad_scores, keys) * score_scale)
            grad_keys = grad_keys + mm_tn(grad_scores, queries[g]) * score_scale
            grad_values = grad_values + mm_tn(probs.astype(BF), grad_head)
        if B > 1:
            grad_keys = lax.psum_scatter(grad_keys, "b", scatter_dimension=0, tiled=True)
            grad_values = lax.psum_scatter(grad_values, "b", scatter_dimension=0, tiled=True)
        grad_rot = jnp.stack(grad_queries + [grad_keys], 1)
        grad_normed = grad_rot * cosine + half_turn_back(grad_rot * sine)
        grad_qk_raw = norm_back(qk_raw, qk_factor, qk_gain, grad_normed)
        terms = jnp.sum(grad_normed * qk_raw * qk_factor, 0)
        totals = jnp.concatenate([jnp.sum(terms[:group], 0), terms[group]])
        grad_raw = jnp.concatenate(
            [grad_qk_raw.reshape(count, qw + HEAD_DIM), grad_values], 1
        ).astype(BF)
    if B > 1:
        w_qkv = wa[:, : qw + 2 * HEAD_DIM]
        gives = [mm_nt(g, w_qkv).astype(BF) for g in jnp.split(grad_raw[side:], 2)]
        keep = mm_nt(grad_raw[:side], w_qkv).astype(BF)
    grad_raw = after(grad_raw, got_a)
    gives = [swap(after(g, grad_raw), "tp") for g in gives]
    grads_attn = attn_grad_call(normed, grad_attn, grad_raw, mixed)
    gives[0] = after(gives[0], parts, *grads_attn[2:])
    gives[1] = after(gives[1], opposite)
    low = add_call(keep, *gives)
    grad_normed_own = sum_tokens("sum_dxa", low)
    total = jnp.sum(after(parts, low).astype(F32), 0)
    out_own = relative((middle + total).astype(BF))
    with jax.named_scope("grads_ffn"):
        pieces = [near_a, near_b, got_a, got_b, opposite]
        if B == 1:
            pieces = list(merge_call(ij[None], J, after(near_a, low), *pieces[1:]))
        else:
            near = jnp.concatenate([add(near_a, got_a), add(near_b, got_b)], 1)
            near = lax.psum_scatter(add(near, opposite), "b", scatter_dimension=0, tiled=True)
            near = near.reshape(J, shard, 2 * ffn_width)
            pieces = [lax.dynamic_index_in_dim(near, ij ^ d, 0, keepdims=False) for d in range(J)]
        for d in range(1, J):
            pieces[d] = lax.ppermute(pieces[d], "j", [(i, i ^ d) for i in range(J)])
    grad_stream = grad_middle + norm_back(stream, attn_factor, gain_attn, grad_normed_own)
    sent = jnp.stack([out_own, relative(grad_stream.astype(BF))])
    out_hidden, grad_hidden = give_back("return", sent)
    with jax.named_scope("grads_attn"):
        totals = jnp.pad(totals[None], ((0, 0), (0, wide - 2 * HEAD_DIM)))
        near, beside, opposed, across = grads_attn
        got = swap(jnp.concatenate([across, two_numbers(totals)], 0), "dp")
        got_near = swap(opposed, "dp")
        got = after(got, low)
        totals = totals + one_number(got[part:])
        beside = jnp.concatenate([add(beside, got[:part]), two_numbers(totals)], 0)
        got = swap(beside, "h")
        totals = totals + one_number(got[part:])
    with jax.named_scope("grads"):
        got = after(got, grad_normed_own)
        near = add(near.astype(F32) + got_near.astype(F32), got[:part])
        extra = two_numbers(totals[:, :LANES])
        extra = jnp.pad(extra, ((0, shard - extra.shape[0]), (0, 0)))
        extra = jnp.broadcast_to(extra[None], (B * J, shard, LANES))
        near = jnp.concatenate([near.reshape(B * J, shard, near.shape[1]), extra], 2)
        if B > 1:
            near = lax.psum_scatter(near, "b", scatter_dimension=0, tiled=True)
        shards = lax.all_to_all(near, "j", 0, 0)
    totals = jnp.sum(one_number(shards[:, :, -LANES:]), (0, 1))
    *shard_grads, sums = final_call(qw, fw, ij[None], shards, pieces, w_query, w_key, w_value, w_gate, w_up)

    sums = jnp.concatenate([totals, sums[:, 0], sums[:, 1]])
    sums = sums + swap(sums, "tp")
    totals = sums[: 2 * HEAD_DIM].reshape(2, HEAD_DIM)
    sums = sums[2 * HEAD_DIM :].reshape(2, shard) / jnp.stack([attn_gain, ffn_gain]).astype(F32)

    shard_query, shard_key, shard_value, shard_output, shard_gate, shard_up, shard_down = shard_grads
    return (
        out_hidden,
        grad_hidden,
        sums[0],
        shard_query,
        shard_key,
        shard_value,
        totals[0],
        totals[1],
        shard_output.T,
        sums[1],
        shard_gate,
        shard_up,
        shard_down.T,
    )


def solution(mesh):
    places = KV_HEADS // mesh.shape["tp"]

    def run(*args):
        micro = args[0].shape[0]
        shape = (mesh.shape["dp"], micro, mesh.shape["ctx"] // (micro * places), places)
        fine = Mesh(
            mesh.devices.reshape(*shape, mesh.shape["tp"]), ("dp", "h", "b", "j", "tp")
        )
        ctx = ("h", "b", "j")
        rows = ("dp", "h", "b", "j")
        tokens = P(None, "dp", ctx, None)
        return jax.shard_map(
            body,
            mesh=fine,
            in_specs=(
                tokens,
                P(None, "dp"),
                P(None, "dp", ctx),
                P(rows),
                P(rows, "tp"),
                P(rows, "tp"),
                P(rows, "tp"),
                P(),
                P(),
                P("tp", rows),
                P(rows),
                P(rows, "tp"),
                P(rows, "tp"),
                P("tp", rows),
                tokens,
            ),
            out_specs=(
                tokens,
                tokens,
                P(rows),
                P(rows, "tp"),
                P(rows, "tp"),
                P(rows, "tp"),
                P(),
                P(),
                P("tp", rows),
                P(rows),
                P(rows, "tp"),
                P(rows, "tp"),
                P("tp", rows),
            ),
            check_vma=False,
        )(*args)

    return run
```

```python
import functools

import jax
import jax.numpy as jnp
from jax import lax
from jax.experimental import pallas as pl
from jax.experimental.pallas import tpu as pltpu
from jax.sharding import Mesh, PartitionSpec as P

HEADS = 16
KV_HEADS = 8
HEAD_DIM = 64
EPSILON = 1e-05
ROPE_BASE = 1000000.0
MASKED = -1e30
BF = jnp.bfloat16
F32 = jnp.float32
VMEM_BYTES = 60 * 2**20
LANES = 128
SMALL_COST = pl.CostEstimate(flops=1, bytes_accessed=1, transcendentals=0)


def dot(a, b, dims):
    return lax.dot_general(a, b, (dims, ((), ())), preferred_element_type=F32)


def mm(a, b):
    return dot(a, b, ((1,), (0,)))


def mm_nt(a, b):
    return dot(a, b, ((1,), (1,)))


def mm_tn(a, b):
    return dot(a, b, ((0,), (0,)))


def nothing(*refs):
    pass


def after(value, *others):
    anywhere = pl.BlockSpec(memory_space=pl.ANY)
    return pl.pallas_call(
        nothing,
        in_specs=[anywhere] * (1 + len(others)),
        out_specs=anywhere,
        out_shape=jax.ShapeDtypeStruct(value.shape, value.dtype),
        input_output_aliases={0: 0},
        cost_estimate=SMALL_COST,
        name="after",
    )(value, *others)


def swap(v, axis):
    return lax.ppermute(v, axis, [(0, 1), (1, 0)])


def add(a, b):
    return (a.astype(F32) + b.astype(F32)).astype(BF)


def norm_scale(vector):
    return lax.rsqrt(jnp.mean(vector * vector, -1, keepdims=True) + EPSILON)


def norm_back(vector, factor, gain, upstream):
    weighted = upstream * gain
    return factor * weighted - vector * factor * factor * factor * jnp.mean(
        vector * weighted, -1, keepdims=True
    )


def half_turn(vector):
    middle_index = vector.shape[-1] // 2
    return jnp.concatenate([-vector[..., middle_index:], vector[..., :middle_index]], -1)


def half_turn_back(vector):
    middle_index = vector.shape[-1] // 2
    return jnp.concatenate([vector[..., middle_index:], -vector[..., :middle_index]], -1)


def in_order(parts, index):
    bit = 1
    while bit < len(parts):
        flag = (index & bit) != 0
        parts = [jnp.where(flag, parts[i ^ bit], parts[i]) for i in range(len(parts))]
        bit *= 2
    return parts


def row_sums(square, low):
    left = jnp.sum(jnp.where(low, square, 0.0), -1, keepdims=True)
    right = jnp.sum(jnp.where(low, 0.0, square), -1, keepdims=True)
    return jnp.where(low, left, right)


def pair_scale(pair, low):
    return lax.rsqrt(row_sums(pair * pair, low) * (1.0 / HEAD_DIM) + EPSILON)


def lanes(shape):
    return lax.broadcasted_iota(jnp.int32, shape, 1)


def turned(pair, first):
    width = pair.shape[1]
    quarter = HEAD_DIM // 2
    return jnp.where(first, pltpu.roll(pair, width - quarter, 1), pltpu.roll(pair, quarter, 1))


def qkv_kernel(half_tiles, h0_ref, h1_ref, gain_ref, w_ref, qk_gain_ref, cos_ref, sin_ref,
               xa0_ref, xa1_ref, raw_ref, qkv_ref):
    def run(h_ref, xa_ref):
        hidden = h_ref[...].astype(F32)
        factor = lax.rsqrt(jnp.mean(hidden * hidden, -1, keepdims=True) + EPSILON)
        xa = (hidden * factor * gain_ref[...]).astype(BF)
        xa_ref[...] = xa
        raw = mm(xa, w_ref[:, :256])
        raw_ref[...] = raw
        lane = lanes((raw.shape[0], 128))
        low = lane < HEAD_DIM
        first = lane % HEAD_DIM < HEAD_DIM // 2
        cosine, sine = cos_ref[...], sin_ref[...]
        sine = jnp.where(first, -sine, sine)
        for p in range(2):
            pair = raw[:, 128 * p : 128 * (p + 1)]
            normed = pair * pair_scale(pair, low) * qk_gain_ref[p : p + 1, :]
            turned_pair = normed * cosine + turned(normed, first) * sine
            if p == 1:
                turned_pair = jnp.where(low, turned_pair, pair)
            qkv_ref[:, 128 * p : 128 * (p + 1)] = turned_pair.astype(BF)

    @pl.when(pl.program_id(0) < half_tiles)
    def _():
        run(h0_ref, xa0_ref)

    @pl.when(pl.program_id(0) >= half_tiles)
    def _():
        run(h1_ref, xa1_ref)


def qkv_call(h0, h1, gain, w, qk_gain, cosine, sine):
    half, d_model = h0.shape
    tile = min(256, half)
    n = half // tile
    own = pl.BlockSpec((tile, d_model), lambda i: (jnp.minimum(i, n - 1), 0))
    other = pl.BlockSpec((tile, d_model), lambda i: (jnp.maximum(i - n, 0), 0))
    def fixed(a):
        return pl.BlockSpec(a.shape, lambda i: (0, 0))
    def rows(width):
        return pl.BlockSpec((tile, width), lambda i: (i, 0))
    return pl.pallas_call(
        functools.partial(qkv_kernel, n),
        grid=(2 * n,),
        in_specs=[own, other, fixed(gain), fixed(w), fixed(qk_gain), rows(128), rows(128)],
        out_specs=[own, other, rows(256), rows(256)],
        out_shape=[
            jax.ShapeDtypeStruct(h0.shape, BF),
            jax.ShapeDtypeStruct(h0.shape, BF),
            jax.ShapeDtypeStruct((2 * half, 256), F32),
            jax.ShapeDtypeStruct((2 * half, 256), BF),
        ],
        compiler_params=pltpu.CompilerParams(vmem_limit_bytes=VMEM_BYTES),
        cost_estimate=SMALL_COST,
        name="qkv",
    )(h0, h1, gain, w, qk_gain, cosine, sine)


def blocks_of(tiles):
    return [(a, k) for a in range(tiles) for k in range(a + 1)]


def stacked(pair):
    return jnp.concatenate([pair[:, :HEAD_DIM], pair[:, HEAD_DIM:]], 0)


def attend_kernel(tile, tiles, at_ref, qkv_ref, mixed_ref, probs_ref):
    half = tiles // 2
    def place(t):
        return pl.multiple_of((t + half * at_ref[1]) % tiles * tile, tile)
    for a in range(tiles):
        query = stacked(qkv_ref[pl.ds(place(a), tile), :128])
        row = lax.broadcasted_iota(jnp.int32, (2 * tile, 1), 0) % tile + a * tile
        limit = jnp.minimum(row + 1, at_ref[0])
        scores = []
        for k in range(a + 1):
            key = qkv_ref[pl.ds(place(k), tile), 128 : 128 + HEAD_DIM]
            column = lax.broadcasted_iota(jnp.int32, (1, tile), 1) + k * tile
            scores.append(
                jnp.where(column < limit, mm_nt(query, key) * HEAD_DIM ** (-0.5), MASKED)
            )
        peak = functools.reduce(jnp.maximum, [jnp.max(s, -1, keepdims=True) for s in scores])
        exps = [jnp.exp(s - peak) for s in scores]
        total = functools.reduce(jnp.add, [jnp.sum(e, -1, keepdims=True) for e in exps])
        inverse = 1.0 / total
        mixed = 0.0
        for k in range(a + 1):
            probs = (exps[k] * inverse).astype(BF)
            probs_ref[blocks_of(tiles).index((a, k))] = probs
            value = qkv_ref[pl.ds(place(k), tile), 128 + HEAD_DIM :]
            mixed = mixed + mm(probs, value)
        mixed_ref[pl.ds(place(a), tile), :] = jnp.concatenate(
            [mixed[:tile], mixed[tile:]], 1
        ).astype(BF)


def attend_call(at, qkv):
    count = qkv.shape[0]
    tile = min(256, count // 2)
    tiles = count // tile
    pairs = len(blocks_of(tiles))
    return pl.pallas_call(
        functools.partial(attend_kernel, tile, tiles),
        in_specs=[pl.BlockSpec(memory_space=pltpu.SMEM), pl.BlockSpec(memory_space=pltpu.VMEM)],
        out_specs=[pl.BlockSpec(memory_space=pltpu.VMEM)] * 2,
        out_shape=[
            jax.ShapeDtypeStruct((count, 128), BF),
            jax.ShapeDtypeStruct((pairs, 2 * tile, tile), BF),
        ],
        compiler_params=pltpu.CompilerParams(vmem_limit_bytes=VMEM_BYTES),
        cost_estimate=SMALL_COST,
        name="attend",
    )(at, qkv)


def attend_back_kernel(tile, tiles, at_ref, qkv_ref, mixed_ref, probs_ref, raw_ref, g0_ref, g1_ref,
                       wa_ref, qk_gain_ref, cos_ref, sin_ref, out_ref, total_ref, give0_ref,
                       give1_ref, keep_ref, dm_ref, dkv_ref):
    half = tiles // 2
    def place(t):
        return pl.multiple_of((t + half * at_ref[1]) % tiles * tile, tile)
    rows = half * tile
    wide = out_ref.shape[1]
    dm_ref[:rows] = mm(g0_ref[...], wa_ref[:, wide:]).astype(BF)
    dm_ref[rows:] = mm(g1_ref[...], wa_ref[:, wide:]).astype(BF)
    scale = HEAD_DIM ** (-0.5)
    lane = lanes((tile, 128))
    low = lane < HEAD_DIM
    first = lane % HEAD_DIM < HEAD_DIM // 2

    def finish(t, p, grad):
        at = pl.ds(place(t), tile)
        cosine, sine = cos_ref[at], sin_ref[at]
        pair = raw_ref[at, 128 * p : 128 * (p + 1)]
        factor = pair_scale(pair, low)
        signed = grad * jnp.where(first, -sine, sine)
        upstream = grad * cosine + turned(signed, first)
        gain = qk_gain_ref[p : p + 1, :]
        weighted = upstream * gain
        mean = row_sums(pair * weighted, low) * (1.0 / HEAD_DIM)
        result = factor * weighted - pair * (factor * factor * factor * mean)
        terms = jnp.sum(upstream * pair * factor, 0, keepdims=True)
        if p == 1:
            result = jnp.where(low, result, grad)
        out_ref[at, 128 * p : 128 * (p + 1)] = result.astype(BF)
        total_ref[p : p + 1, :] += terms

    total_ref[...] = jnp.zeros_like(total_ref)
    dkv = [0.0] * tiles
    for a in range(tiles):
        at = pl.ds(place(a), tile)
        query = stacked(qkv_ref[at, :128])
        grad = stacked(dm_ref[at])
        mixed = stacked(mixed_ref[at, :])
        delta = jnp.sum(grad.astype(F32) * mixed.astype(F32), -1, keepdims=True)
        grad_query = 0.0
        for k in range(a + 1):
            keys = pl.ds(place(k), tile)
            key = qkv_ref[keys, 128 : 128 + HEAD_DIM]
            value = qkv_ref[keys, 128 + HEAD_DIM :]
            probs = probs_ref[blocks_of(tiles).index((a, k))]
            grad_scores = (probs.astype(F32) * (mm_nt(grad, value) - delta)).astype(BF)
            grad_query = grad_query + mm(grad_scores, key)
            grad_kv = jnp.concatenate(
                [mm_tn(grad_scores, query) * scale, mm_tn(probs, grad)], 1
            )
            if a == k:
                dkv_ref[k] = grad_kv
            else:
                dkv_ref[k] += grad_kv
        grad_query = grad_query * scale
        finish(a, 0, jnp.concatenate([grad_query[:tile], grad_query[tile:]], 1))
    for k in range(tiles):
        finish(k, 1, dkv_ref[k])
    w = wa_ref[:, :wide]
    middle = rows + rows // 2
    give0_ref[...] = mm_nt(out_ref[rows:middle], w).astype(BF)
    give1_ref[...] = mm_nt(out_ref[middle:], w).astype(BF)
    keep_ref[...] = mm_nt(out_ref[:rows], w).astype(BF)


def attend_back_call(at, qkv, mixed, probs, raw, g0, g1, wa, qk_gain, cosine, sine):
    count, d_model = qkv.shape[0], g0.shape[1]
    tile = min(256, count // 2)
    tiles = count // tile
    vmem = pl.BlockSpec(memory_space=pltpu.VMEM)
    return pl.pallas_call(
        functools.partial(attend_back_kernel, tile, tiles),
        in_specs=[pl.BlockSpec(memory_space=pltpu.SMEM)] + [vmem] * 10,
        out_specs=[vmem] * 5,
        out_shape=[
            jax.ShapeDtypeStruct((count, 256), BF),
            jax.ShapeDtypeStruct((8, 128), F32),
            jax.ShapeDtypeStruct((count // 4, d_model), BF),
            jax.ShapeDtypeStruct((count // 4, d_model), BF),
            jax.ShapeDtypeStruct((count // 2, d_model), BF),
        ],
        scratch_shapes=[pltpu.VMEM((count, 128), BF), pltpu.VMEM((tiles, tile, 128), F32)],
        compiler_params=pltpu.CompilerParams(vmem_limit_bytes=VMEM_BYTES),
        cost_estimate=SMALL_COST,
        name="attend_back",
    )(at, qkv, mixed, probs, raw, g0, g1, wa, qk_gain, cosine, sine)


def ffn_kernel(fw, part, x_ref, cot_ref, *refs):
    a_refs, b_refs, (w_ref, act_ref, grad_ref, grad_in_ref, out_ref) = refs[:3], refs[3:6], refs[6:]
    width = a_refs[0].shape[1]
    a_refs = [*a_refs[:2], w_ref.at[:, :width], a_refs[2]]
    b_refs = [*b_refs[:2], w_ref.at[:, width:], b_refs[2]]
    rest = 2 * fw - width
    pre_a, pre_b, grad_act = 0.0, 0.0, 0.0
    for p in range(4):
        cut = slice(p * part, (p + 1) * part)
        pre_a = pre_a + mm(x_ref[:, cut], a_refs[p][...])
        pre_b = pre_b + mm(x_ref[:, cut], b_refs[p][:, :rest])
        grad_act = grad_act + mm(cot_ref[:, cut], b_refs[p][:, rest : rest + fw])
    pre = jnp.concatenate([pre_a, pre_b], 1)
    gate, up = pre[:, :fw], pre[:, fw:]
    sigmoid = 1.0 / (1.0 + jnp.exp(-gate))
    silu = gate * sigmoid
    act = (silu * up).astype(BF)
    act_ref[...] = act
    grad_gate = grad_act * up * sigmoid * (1.0 + gate * (1.0 - sigmoid))
    grad = jnp.concatenate([grad_gate, grad_act * silu], 1).astype(BF)
    grad_ref[...] = grad
    for p in range(4):
        cut = slice(p * part, (p + 1) * part)
        grad_in = mm_nt(grad[:, :width], a_refs[p][...])
        grad_in = grad_in + mm_nt(grad[:, width:], b_refs[p][:, :rest])
        grad_in_ref[:, cut] = grad_in.astype(BF)
        out_ref[:, cut] = mm_nt(act, b_refs[p][:, rest : rest + fw]).astype(BF)


def ffn_call(fw, x, cot, w_a, w_b, w_own):
    count, d_model = x.shape
    part = w_a[0].shape[0]
    tile = min(256, count)
    shapes = [(count, fw), (count, 2 * fw), (count, d_model), (count, d_model)]
    return pl.pallas_call(
        functools.partial(ffn_kernel, fw, part),
        grid=(count // tile,),
        in_specs=[
            pl.BlockSpec((tile, d_model), lambda i: (i, 0)),
            pl.BlockSpec((tile, d_model), lambda i: (i, 0)),
        ]
        + [pl.BlockSpec(p.shape, lambda i: (0, 0)) for p in (*w_a, *w_b, w_own)],
        out_specs=[pl.BlockSpec((tile, s[1]), lambda i: (i, 0)) for s in shapes],
        out_shape=[jax.ShapeDtypeStruct(s, BF) for s in shapes],
        compiler_params=pltpu.CompilerParams(vmem_limit_bytes=VMEM_BYTES),
        cost_estimate=SMALL_COST,
        name="ffn",
    )(x, cot, *w_a, *w_b, w_own)


def ffn_grad_kernel(fw, width, whole, *refs):
    ins, outs = refs[:8], refs[8:]
    x0, x1, cot0, cot1, grad0, grad1, act0, act1 = (r[...] for r in ins)
    grad_in = (mm_tn(x0, grad0) + mm_tn(x1, grad1)).astype(BF)
    grad_out = (mm_tn(cot0, act0) + mm_tn(cot1, act1)).astype(BF)
    rest = 2 * fw - width

    def write(a_ref, b_ref):
        a_ref[...] = grad_in[:, :width]
        b_ref[:, :rest] = grad_in[:, width:]
        b_ref[:, rest : rest + fw] = grad_out
        left = width - rest - fw
        if left:
            b_ref[:, rest + fw :] = jnp.zeros((grad_out.shape[0], left), BF)

    @pl.when(pl.program_id(0) == 0)
    def _():
        if whole:
            write(outs[0].at[:, :width], outs[0].at[:, width:])
        else:
            write(*outs[:2])

    @pl.when(pl.program_id(0) == 1)
    def _():
        write(*outs[-2:])


def ffn_grad_call(p, width, whole, x, cot, grad, act):
    count, d_model = x[0].shape
    fw = act[0].shape[1]
    part = d_model // 4
    columns = pl.BlockSpec((count, part), lambda i: (0, p + i))
    operands = [pl.BlockSpec(a.shape, lambda i: (0, 0)) for a in (*grad, *act)]
    shapes = ([(part, 2 * width)] if whole else [(part, width)] * 2) + [(part, width)] * 2
    return pl.pallas_call(
        functools.partial(ffn_grad_kernel, fw, width, whole),
        grid=(2,),
        in_specs=[columns] * 4 + operands,
        out_specs=[pl.BlockSpec(s, lambda i: (0, 0)) for s in shapes],
        out_shape=[jax.ShapeDtypeStruct(s, BF) for s in shapes],
        compiler_params=pltpu.CompilerParams(vmem_limit_bytes=VMEM_BYTES),
        cost_estimate=SMALL_COST,
        name="ffn_grad",
    )(*x, *cot, *grad, *act)


def add_kernel(keep_ref, got0_ref, got1_ref, out_ref):
    rows = got0_ref.shape[0]
    out_ref[:rows] = (keep_ref[:rows].astype(F32) + got0_ref[...].astype(F32)).astype(BF)
    out_ref[rows:] = (keep_ref[rows:].astype(F32) + got1_ref[...].astype(F32)).astype(BF)


def add_call(keep, got0, got1):
    vmem = pl.BlockSpec(memory_space=pltpu.VMEM)
    return pl.pallas_call(
        add_kernel,
        in_specs=[vmem] * 3,
        out_specs=vmem,
        out_shape=jax.ShapeDtypeStruct(keep.shape, BF),
        compiler_params=pltpu.CompilerParams(vmem_limit_bytes=VMEM_BYTES),
        cost_estimate=SMALL_COST,
        name="add",
    )(keep, got0, got1)


def add_cut_kernel(place_ref, a_ref, b_ref, *outs):
    height = outs[0].shape[0]
    for d, out_ref in enumerate(outs):
        at = pl.ds(pl.multiple_of((place_ref[0] ^ d) * height, height), height)
        out_ref[...] = (a_ref[at, :].astype(F32) + b_ref[at, :].astype(F32)).astype(BF)


def add_cut_call(place, places, a, b):
    vmem = pl.BlockSpec(memory_space=pltpu.VMEM)
    shape = jax.ShapeDtypeStruct((a.shape[0] // places, a.shape[1]), BF)
    return pl.pallas_call(
        add_cut_kernel,
        in_specs=[pl.BlockSpec(memory_space=pltpu.SMEM)] + [vmem] * 2,
        out_specs=[vmem] * places,
        out_shape=[shape] * places,
        compiler_params=pltpu.CompilerParams(vmem_limit_bytes=VMEM_BYTES),
        cost_estimate=SMALL_COST,
        name="add_cut",
    )(place, a, b)


def pack_kernel(qw, wq_ref, wk_ref, wv_ref, wo_ref, g0_ref, g1_ref, pos_ref, out_ref):
    places, height, wide = out_ref.shape
    shard = wq_ref.shape[0]

    def row(*parts):
        parts = [p.astype(F32) for p in parts]
        parts.append(jnp.zeros((1, wide - sum(p.shape[1] for p in parts)), F32))
        return jnp.concatenate(parts, 1)

    pos = pos_ref[...]
    high = lax.shift_right_logical(pos, 8)
    low = pos - high * 256
    index = lax.broadcasted_iota(jnp.int32, (height - shard, wide), 0)
    extra = jnp.where(index == 0, row(g0_ref[...], g1_ref[...]), 0.0)
    for n, part in ((1, high), (2, low)):
        extra = jnp.where(index == n, row(*(part[m : m + 1] for m in range(part.shape[0]))), extra)
    extra = extra.astype(BF)
    for p in range(places):
        wide_at = slice(p * qw, (p + 1) * qw)
        at = slice(p * HEAD_DIM, (p + 1) * HEAD_DIM)
        out_ref[p, :shard, :qw] = wq_ref[:, wide_at]
        out_ref[p, :shard, qw : qw + 2 * HEAD_DIM] = jnp.concatenate(
            [wk_ref[:, at], wv_ref[:, at]], 1
        )
        out_ref[p, :shard, qw + 2 * HEAD_DIM :] = wo_ref[:, wide_at]
        out_ref[p, shard:, :] = extra


def pack_call(qw, places, wide, *arrays):
    vmem = pl.BlockSpec(memory_space=pltpu.VMEM)
    return pl.pallas_call(
        functools.partial(pack_kernel, qw),
        in_specs=[vmem] * 7,
        out_specs=vmem,
        out_shape=jax.ShapeDtypeStruct((places, arrays[0].shape[0] + 8, wide), BF),
        compiler_params=pltpu.CompilerParams(vmem_limit_bytes=VMEM_BYTES),
        cost_estimate=SMALL_COST,
        name="pack",
    )(*arrays)


def attn_grad_kernel(x0_ref, x1_ref, g0_ref, g1_ref, raw_ref, mixed_ref, *outs):
    side = x0_ref.shape[0]
    wide = raw_ref.shape[1]
    grad_qkv = mm_tn(x0_ref[...], raw_ref[:side]) + mm_tn(x1_ref[...], raw_ref[side:])
    grad_o = mm_tn(g0_ref[...], mixed_ref[:side]) + mm_tn(g1_ref[...], mixed_ref[side:])
    for p in range(4):

        @pl.when(pl.program_id(0) == p)
        def _():
            outs[p][:, :wide] = grad_qkv.astype(BF)
            outs[p][:, wide:] = grad_o.astype(BF)


def attn_grad_call(x, g, raw, mixed):
    count, d_model = x[0].shape
    part = d_model // 4
    shape = (part, raw.shape[1] + mixed.shape[1])
    columns = pl.BlockSpec((count, part), lambda i: (0, i))
    return pl.pallas_call(
        attn_grad_kernel,
        grid=(4,),
        in_specs=[columns] * 4 + [pl.BlockSpec(a.shape, lambda i: (0, 0)) for a in (raw, mixed)],
        out_specs=[pl.BlockSpec(shape, lambda i: (0, 0))] * 4,
        out_shape=[jax.ShapeDtypeStruct(shape, BF)] * 4,
        compiler_params=pltpu.CompilerParams(vmem_limit_bytes=VMEM_BYTES),
        cost_estimate=SMALL_COST,
        name="attn_grad",
    )(*x, *g, raw, mixed)


def merge_kernel(place_ref, near_a, near_b, got_a, got_b, opposite, *outs):
    height, width = outs[0].shape[0], near_a.shape[1]
    for d, out_ref in enumerate(outs):
        at = pl.ds(pl.multiple_of((place_ref[0] ^ d) * height, height), height)
        for near, got, start in ((near_a, got_a, 0), (near_b, got_b, width)):
            total = near[at, :].astype(F32) + got[at, :].astype(F32)
            total = total + opposite[at, start : start + width].astype(F32)
            out_ref[:, start : start + width] = total.astype(BF)


def merge_call(place, places, *arrays):
    rows, width = arrays[0].shape
    shape = jax.ShapeDtypeStruct((rows // places, 2 * width), BF)
    vmem = pl.BlockSpec(memory_space=pltpu.VMEM)
    return pl.pallas_call(
        merge_kernel,
        in_specs=[pl.BlockSpec(memory_space=pltpu.SMEM)] + [vmem] * 5,
        out_specs=[vmem] * places,
        out_shape=[shape] * places,
        compiler_params=pltpu.CompilerParams(vmem_limit_bytes=VMEM_BYTES),
        cost_estimate=SMALL_COST,
        name="merge",
    )(place, *arrays)


def final_kernel(
    qw, fw, place_ref, got_ref, p0_ref, p1_ref, p2_ref, p3_ref, wq_ref, wk_ref, wv_ref, wg_ref, wu_ref,
    q_ref, k_ref, v_ref, o_ref, gate_ref, up_ref, down_ref, sum_ref,
):
    places = got_ref.shape[0]

    def side_by_side(start, width):
        return jnp.concatenate(
            [got_ref[p, :, start : start + width] for p in range(places)], 1
        ).astype(F32)

    def rows(weight_ref, grad):
        return jnp.sum(weight_ref[...].astype(F32) * grad, 1, keepdims=True)

    query, key, value = side_by_side(0, qw), side_by_side(qw, HEAD_DIM), side_by_side(qw + HEAD_DIM, HEAD_DIM)
    q_ref[...], k_ref[...], v_ref[...] = query, key, value
    sum_attn = rows(wq_ref, query) + rows(wk_ref, key) + rows(wv_ref, value)
    start = qw + 2 * HEAD_DIM
    o_ref[...] = side_by_side(start, qw)
    pieces = in_order([r[...].astype(F32) for r in (p0_ref, p1_ref, p2_ref, p3_ref)], place_ref[0])
    gate, up, down = (
        jnp.concatenate([p[:, n * fw : (n + 1) * fw] for p in pieces], 1) for n in range(3)
    )
    gate_ref[...], up_ref[...] = gate, up
    sum_ffn = rows(wg_ref, gate) + rows(wu_ref, up)
    down_ref[...] = down
    lane = lanes(sum_ref.shape)
    sum_ref[...] = jnp.where(lane == 0, sum_attn, sum_ffn)


def final_call(qw, fw, place, got, pieces, wq, wk, wv, wg, wu):
    shard = got.shape[1]
    vmem = pl.BlockSpec(memory_space=pltpu.VMEM)
    shapes = [wq.shape, wk.shape, wv.shape, wq.shape, wg.shape, wu.shape, wg.shape]
    shapes.append((shard, LANES))
    return pl.pallas_call(
        functools.partial(final_kernel, qw, fw),
        in_specs=[pl.BlockSpec(memory_space=pltpu.SMEM)] + [vmem] * 10,
        out_specs=[vmem] * 8,
        out_shape=[jax.ShapeDtypeStruct(s, F32) for s in shapes],
        compiler_params=pltpu.CompilerParams(vmem_limit_bytes=VMEM_BYTES),
        cost_estimate=SMALL_COST,
        name="final",
    )(place, got, *pieces, wq, wk, wv, wg, wu)


def body(
    hidden_in,
    lengths,
    positions,
    attn_gain,
    w_query,
    w_key,
    w_value,
    q_gain,
    k_gain,
    w_output,
    ffn_gain,
    w_gate,
    w_up,
    w_down,
    grad_out,
):
    H, B, J, T = (lax.axis_size(a) for a in ("h", "b", "j", "tp"))
    ix, ih, ib, ij, it = (lax.axis_index(a) for a in ("dp", "h", "b", "j", "tp"))
    rows = hidden_in.shape[2]
    d_model = hidden_in.shape[3]
    shard = w_query.shape[0]
    group = HEADS // KV_HEADS
    qw = group * HEAD_DIM
    fw = w_gate.shape[1] // J
    count = T * J * rows
    side = J * rows
    ffn_width = -(-3 * fw // (2 * LANES)) * LANES
    score_scale = HEAD_DIM ** (-0.5)
    quarter = 2 * ix + ih
    part = d_model // 4

    def cut(array, p, width):
        return array[:, p * width : (p + 1) * width]

    def exchange(name, pieces):
        with jax.named_scope(name):
            return lax.all_to_all(pieces, "j", 0, 0)

    def exchange_beside(name, pieces):
        with jax.named_scope(name):
            pieces = in_order(pieces, ij)
            parts = [pieces[0]]
            for d in range(1, J):
                parts.append(lax.ppermute(pieces[d], "j", [(i, i ^ d) for i in range(J)]))
            return parts

    def two_numbers(values):
        high = values.astype(BF)
        low = (values - high.astype(F32)).astype(BF)
        return jnp.pad(jnp.concatenate([high, low], 0), ((0, 6), (0, 0)))

    def one_number(block):
        return block[..., 0:1, :].astype(F32) + block[..., 1:2, :].astype(F32)

    def relative(array):
        pieces = [array[..., p * part : (p + 1) * part] for p in range(4)]
        return jnp.concatenate(in_order(pieces, quarter), -1)

    turn = [(0, 0), (1, 2), (2, 1), (3, 3)]

    def fetch(name, array, *others):
        with jax.named_scope(name):
            mine = lax.dynamic_index_in_dim(array, it, 0, keepdims=False)[0]
            if others:
                mine = after(mine, *others)
            return lax.ppermute(mine, ("h", "tp"), turn)

    def give_back(name, block):
        with jax.named_scope(name):
            mine = lax.ppermute(block, ("h", "tp"), turn)
            both = in_order([mine, swap(mine, "tp")], it)
            return [jnp.stack([b[n] for b in both])[:, None] for n in range(block.shape[0])]

    def gather_half(name, block, *others):
        with jax.named_scope(name):
            sent = jnp.broadcast_to(block[None], (J, *block.shape))
            if others:
                sent = after(sent, *others)
            return lax.all_to_all(sent, "j", 0, 0).reshape(side, d_model)

    def sum_tokens(name, half, *others):
        with jax.named_scope(name):
            got = lax.all_to_all(half.reshape(J, rows, d_model), "j", 0, 0)
            if others:
                got = after(got, *others)
            return jnp.sum(got.astype(F32), 0)

    w_output_t = w_output.T
    w_down_t = w_down.T
    wide = 2 * qw + 2 * HEAD_DIM
    gains = attn_gain[None], ffn_gain[None]
    sent = pack_call(
        qw, J, wide, w_query, w_key, w_value, w_output_t, *gains, positions.reshape(H, rows)
    )
    own = exchange("weights_attn", sent)
    pack = [
        jnp.pad(
            jnp.concatenate([cut(w_gate, p, fw), cut(w_up, p, fw), cut(w_down_t, p, fw)], 1),
            ((0, 0), (0, 2 * ffn_width - 3 * fw)),
        )
        for p in range(J)
    ]
    ffn_own = exchange("weights_ffn", jnp.stack(pack))
    hidden_own = relative(fetch("fetch_hidden", hidden_in))

    def share(name, block):
        with jax.named_scope(name):
            return [block] + [
                lax.ppermute(block, "j", [(i, i ^ d) for i in range(J)]) for d in range(1, J)
            ]

    with jax.named_scope("weights_attn"):
        if B > 1:
            own = lax.all_gather(own, "b", axis=0, tiled=True)
        beside = swap(own, "h")
        opposite = swap(own, "dp")
    half = gather_half("tokens_hidden", hidden_own, ffn_own)
    with jax.named_scope("weights_attn"):
        across = swap(beside, "dp")
    cot_own = relative(fetch("fetch_cot", grad_out))
    with jax.named_scope("weights_attn"):
        parts = [own, beside, opposite, across]
        wa = jnp.stack([p[:, :shard] for p in parts]).reshape(d_model, wide)
        extra = jnp.stack([p[:, shard : shard + 3] for p in parts])
    gains = extra[:, :, 0, : 2 * shard].reshape(4, B * J, 2, shard)
    gains = gains.transpose(2, 0, 1, 3).reshape(2, d_model).astype(F32)
    gain_attn = gains[0]
    gain_ffn = gains[1]
    pos = extra[:2, :, 1:, : H * rows].astype(F32)
    pos = pos[:, :, 0] * 256.0 + pos[:, :, 1]
    pos = lax.dynamic_index_in_dim(pos.reshape(H, B, J, H, rows), ib, 1, keepdims=False)
    pos = jnp.where(ih == 0, pos[:, :, 0], pos[:, :, 1])
    pos = jnp.stack(in_order([pos[0], pos[1]], ih ^ it), 0)
    pos_all = pos.reshape(count)

    place = jnp.arange(T * J, dtype=jnp.int32)
    block_of = (it ^ (place // J)) * (B * J) + place % J
    row_of = jnp.arange(rows, dtype=jnp.int32)
    query_index = ((block_of + ib * J)[:, None] * rows + row_of[None, :]).reshape(count)
    key_index = (
        (block_of[None, :] + jnp.arange(B, dtype=jnp.int32)[:, None] * J)[..., None] * rows + row_of
    ).reshape(B * count)

    inverse = 1.0 / ROPE_BASE ** (jnp.arange(0, HEAD_DIM, 2, dtype=F32) / HEAD_DIM)
    if B == 1:
        inverse = jnp.tile(inverse, 2 * LANES // HEAD_DIM)
    angles = pos_all[:, None] * inverse[None, :]
    cosine = jnp.cos(angles)
    sine = jnp.sin(angles)

    valid_length = lax.dynamic_index_in_dim(lengths[:, 0], ih, 0, keepdims=False)
    at = jnp.stack([valid_length, it])
    ones = jnp.ones((HEAD_DIM,), F32)
    qk_gain = jnp.stack(
        [jnp.concatenate([q_gain, q_gain]).astype(F32), jnp.concatenate([k_gain.astype(F32), ones])]
    )
    half = after(half, wa, gains, cosine, sine, cot_own, at, qk_gain)
    with jax.named_scope("weights_ffn"):
        ffn_own = ffn_own.reshape(J * shard, 2 * ffn_width)
        if B > 1:
            ffn_own = lax.all_gather(ffn_own, "b", axis=0, tiled=True)
        w_a = [ffn_own[:, :ffn_width]]
        w_b = [ffn_own[:, ffn_width:]]
        w_a.append(swap(after(w_a[0], half), "h"))
        w_b.append(swap(after(w_b[0], w_a[1]), "h"))
        w_own = swap(after(ffn_own, half), "dp")
    with jax.named_scope("tokens_hidden"):
        hidden = [half, swap(half, "tp")]
    stream = hidden_own.astype(F32)

    attn_factor = norm_scale(stream)
    if B == 1:
        *normed, raw, qkv = qkv_call(*hidden, gain_attn[None], wa, qk_gain, cosine, sine)
        mixed, probs = attend_call(at, qkv)
    else:
        hidden = jnp.concatenate(hidden, 0).astype(F32)
        normed = (hidden * norm_scale(hidden) * gain_attn).astype(BF)
        cosine = jnp.concatenate([cosine, cosine], -1)[:, None, :]
        sine = jnp.concatenate([sine, sine], -1)[:, None, :]
        raw = mm(normed, wa[:, : qw + 2 * HEAD_DIM])
        normed = [normed[:side], normed[side:]]
        qk_raw = raw[:, : qw + HEAD_DIM].reshape(count, group + 1, HEAD_DIM)
        qk_gain = jnp.stack([q_gain] * group + [k_gain]).astype(F32)
        qk_factor = norm_scale(qk_raw)
        qk_normed = qk_raw * qk_factor * qk_gain
        qk = (qk_normed * cosine + half_turn(qk_normed) * sine).astype(BF)
        queries = qk[:, :group].transpose(1, 0, 2)
        keys = qk[:, group]
        values = raw[:, qw + HEAD_DIM :].astype(BF)
        if B > 1:
            keys = lax.all_gather(keys, "b", axis=0, tiled=True)
            values = lax.all_gather(values, "b", axis=0, tiled=True)
        visible = (key_index[None, :] <= query_index[:, None]) & (key_index[None, :] < valid_length)

        def scores_of(query_head):
            return jnp.where(visible, mm_nt(query_head, keys) * score_scale, MASKED)

        def attend(query_head):
            scores = scores_of(query_head)
            row_max = jnp.max(scores, -1, keepdims=True)
            exp_scores = jnp.exp(scores - row_max)
            row_total = jnp.sum(exp_scores, -1, keepdims=True)
            probs = (exp_scores / row_total).astype(BF)
            return mm(probs, values).astype(BF), row_max + jnp.log(row_total)

        heads = [attend(queries[g]) for g in range(group)]
        mixed = jnp.concatenate([h[0] for h in heads], -1)
    parts = share("tokens_cot", after(cot_own, half))
    mixed = after(mixed, w_a[1], w_own, *parts[1:])
    with jax.named_scope("tokens_cot"):
        cot_half = jnp.concatenate(in_order(parts, ij), 0)
    with jax.named_scope("sum_attn"):
        wo = wa[:, qw + 2 * HEAD_DIM :]
        low = swap(mm_nt(mixed[side:], wo).astype(BF), "tp")
        keep = mm_nt(mixed[:side], wo).astype(BF)
        parts = list(add_cut_call(ij[None], J, keep, low))
        for d in range(1, J):
            parts[d] = lax.ppermute(parts[d], "j", [(i, i ^ d) for i in range(J)])
        w_a.append(swap(w_a[1], "dp"))
        attn_branch = sum(p.astype(F32) for p in parts)

    middle = stream + attn_branch
    gain_ffn = after(gain_ffn, w_b[1], w_a[2])
    ffn_factor = norm_scale(middle)
    xf_own = (middle * ffn_factor * gain_ffn).astype(BF)
    ffn_half = gather_half("tokens_xf", xf_own)
    with jax.named_scope("weights_ffn"):
        w_b.append(swap(w_b[1], "dp"))
    ffn_half = after(ffn_half, w_b[2])
    ffn_in = [ffn_half, swap(ffn_half, "tp")]
    cot = [cot_half, swap(cot_half, "tp")]
    first = ffn_call(fw, ffn_in[0], cot[0], w_a, w_b, w_own)
    second = ffn_call(fw, after(ffn_in[1], first[0]), cot[1], w_a, w_b, w_own)
    hidden_act, grad_pre, grad_in, branch = zip(first, second)
    low = swap(grad_in[1], "tp")
    opposite, across_a, across_b = ffn_grad_call(
        2, ffn_width, True, ffn_in, cot, grad_pre, hidden_act
    )
    low = add(grad_in[0], after(low, across_b))
    with jax.named_scope("grads_ffn"):
        got_b, got_a = swap(across_b, "dp"), swap(across_a, "dp")
    near_a, near_b, beside_a, beside_b = ffn_grad_call(
        0, ffn_width, False, ffn_in, cot, grad_pre, hidden_act
    )
    grad_ffn_in = sum_tokens("sum_dxf", low)
    with jax.named_scope("sum_out"):
        low = add(branch[0], swap(branch[1], "tp"))
    gain_ffn = after(gain_ffn, got_b, near_a, low)

    grad_middle = cot_own.astype(F32) + norm_back(middle, ffn_factor, gain_ffn, grad_ffn_in)
    with jax.named_scope("grads_ffn"):
        beside_b = add(beside_b, got_b)
    half = jnp.concatenate(in_order(share("tokens_dattn", grad_middle.astype(BF)), ij), 0)
    with jax.named_scope("grads_ffn"):
        got_b = swap(beside_b, "h")
        beside_a = add(beside_a, got_a)
        half = after(half, got_b, beside_a)
        got_a = swap(beside_a, "h")
        opposite = swap(after(opposite, half), "dp")
    grad_attn = [half, swap(half, "tp")]
    with jax.named_scope("sum_out"):
        parts = lax.all_to_all(after(low, half).reshape(J, rows, d_model), "j", 0, 0)
    if B == 1:
        grad_raw, totals, *gives, keep = attend_back_call(
            at, qkv, mixed, probs, raw, *grad_attn, wa, qk_gain, cosine, sine
        )
        totals = jnp.concatenate([totals[0, :HEAD_DIM] + totals[0, HEAD_DIM:], totals[1, :HEAD_DIM]])
    else:
        grad_mixed = mm(jnp.concatenate(grad_attn, 0), wo).astype(BF)
        grad_keys = jnp.zeros((B * count, HEAD_DIM), F32)
        grad_values = jnp.zeros((B * count, HEAD_DIM), F32)
        grad_queries = []
        for g in range(group):
            probs = jnp.exp(scores_of(queries[g]) - heads[g][1])
            grad_head = grad_mixed[:, g * HEAD_DIM : (g + 1) * HEAD_DIM]
            grad_probs = mm_nt(grad_head, values)
            row_delta = jnp.sum(grad_probs * probs, -1, keepdims=True)
            grad_scores = (probs * (grad_probs - row_delta)).astype(BF)
            grad_queries.append(mm(grad_scores, keys) * score_scale)
            grad_keys = grad_keys + mm_tn(grad_scores, queries[g]) * score_scale
            grad_values = grad_values + mm_tn(probs.astype(BF), grad_head)
        if B > 1:
            grad_keys = lax.psum_scatter(grad_keys, "b", scatter_dimension=0, tiled=True)
            grad_values = lax.psum_scatter(grad_values, "b", scatter_dimension=0, tiled=True)
        grad_rot = jnp.stack(grad_queries + [grad_keys], 1)
        grad_normed = grad_rot * cosine + half_turn_back(grad_rot * sine)
        grad_qk_raw = norm_back(qk_raw, qk_factor, qk_gain, grad_normed)
        terms = jnp.sum(grad_normed * qk_raw * qk_factor, 0)
        totals = jnp.concatenate([jnp.sum(terms[:group], 0), terms[group]])
        grad_raw = jnp.concatenate(
            [grad_qk_raw.reshape(count, qw + HEAD_DIM), grad_values], 1
        ).astype(BF)
    if B > 1:
        w_qkv = wa[:, : qw + 2 * HEAD_DIM]
        gives = [mm_nt(g, w_qkv).astype(BF) for g in jnp.split(grad_raw[side:], 2)]
        keep = mm_nt(grad_raw[:side], w_qkv).astype(BF)
    grad_raw = after(grad_raw, got_a)
    gives = [swap(after(g, grad_raw), "tp") for g in gives]
    grads_attn = attn_grad_call(normed, grad_attn, grad_raw, mixed)
    gives[0] = after(gives[0], parts, *grads_attn[2:])
    gives[1] = after(gives[1], opposite)
    low = add_call(keep, *gives)
    grad_normed_own = sum_tokens("sum_dxa", low)
    total = jnp.sum(after(parts, low).astype(F32), 0)
    out_own = relative((middle + total).astype(BF))
    with jax.named_scope("grads_ffn"):
        pieces = [near_a, near_b, got_a, got_b, opposite]
        if B == 1:
            pieces = list(merge_call(ij[None], J, after(near_a, low), *pieces[1:]))
        else:
            near = jnp.concatenate([add(near_a, got_a), add(near_b, got_b)], 1)
            near = lax.psum_scatter(add(near, opposite), "b", scatter_dimension=0, tiled=True)
            near = near.reshape(J, shard, 2 * ffn_width)
            pieces = [lax.dynamic_index_in_dim(near, ij ^ d, 0, keepdims=False) for d in range(J)]
        for d in range(1, J):
            pieces[d] = lax.ppermute(pieces[d], "j", [(i, i ^ d) for i in range(J)])
    grad_stream = grad_middle + norm_back(stream, attn_factor, gain_attn, grad_normed_own)
    sent = jnp.stack([out_own, relative(grad_stream.astype(BF))])
    out_hidden, grad_hidden = give_back("return", sent)
    with jax.named_scope("grads_attn"):
        totals = jnp.pad(totals[None], ((0, 0), (0, wide - 2 * HEAD_DIM)))
        near, beside, opposed, across = grads_attn
        got = swap(jnp.concatenate([across, two_numbers(totals)], 0), "dp")
        got_near = swap(opposed, "dp")
        got = after(got, low)
        totals = totals + one_number(got[part:])
        beside = jnp.concatenate([add(beside, got[:part]), two_numbers(totals)], 0)
        got = swap(beside, "h")
        totals = totals + one_number(got[part:])
    with jax.named_scope("grads"):
        got = after(got, grad_normed_own)
        near = add(near.astype(F32) + got_near.astype(F32), got[:part])
        extra = two_numbers(totals[:, :LANES])
        extra = jnp.pad(extra, ((0, shard - extra.shape[0]), (0, 0)))
        extra = jnp.broadcast_to(extra[None], (B * J, shard, LANES))
        near = jnp.concatenate([near.reshape(B * J, shard, near.shape[1]), extra], 2)
        if B > 1:
            near = lax.psum_scatter(near, "b", scatter_dimension=0, tiled=True)
        shards = lax.all_to_all(near, "j", 0, 0)
    totals = jnp.sum(one_number(shards[:, :, -LANES:]), (0, 1))
    *shard_grads, sums = final_call(qw, fw, ij[None], shards, pieces, w_query, w_key, w_value, w_gate, w_up)

    sums = jnp.concatenate([totals, sums[:, 0], sums[:, 1]])
    sums = sums + swap(sums, "tp")
    totals = sums[: 2 * HEAD_DIM].reshape(2, HEAD_DIM)
    sums = sums[2 * HEAD_DIM :].reshape(2, shard) / jnp.stack([attn_gain, ffn_gain]).astype(F32)

    shard_query, shard_key, shard_value, shard_output, shard_gate, shard_up, shard_down = shard_grads
    return (
        out_hidden,
        grad_hidden,
        sums[0],
        shard_query,
        shard_key,
        shard_value,
        totals[0],
        totals[1],
        shard_output.T,
        sums[1],
        shard_gate,
        shard_up,
        shard_down.T,
    )


def solution(mesh):
    places = KV_HEADS // mesh.shape["tp"]

    def run(*args):
        micro = args[0].shape[0]
        shape = (mesh.shape["dp"], micro, mesh.shape["ctx"] // (micro * places), places)
        fine = Mesh(
            mesh.devices.reshape(*shape, mesh.shape["tp"]), ("dp", "h", "b", "j", "tp")
        )
        ctx = ("h", "b", "j")
        rows = ("dp", "h", "b", "j")
        tokens = P(None, "dp", ctx, None)
        return jax.shard_map(
            body,
            mesh=fine,
            in_specs=(
                tokens,
                P(None, "dp"),
                P(None, "dp", ctx),
                P(rows),
                P(rows, "tp"),
                P(rows, "tp"),
                P(rows, "tp"),
                P(),
                P(),
                P("tp", rows),
                P(rows),
                P(rows, "tp"),
                P(rows, "tp"),
                P("tp", rows),
                tokens,
            ),
            out_specs=(
                tokens,
                tokens,
                P(rows),
                P(rows, "tp"),
                P(rows, "tp"),
                P(rows, "tp"),
                P(),
                P(),
                P("tp", rows),
                P(rows),
                P(rows, "tp"),
                P(rows, "tp"),
                P("tp", rows),
            ),
            check_vma=False,
        )(*args)

    return run
```
